32 devices in a mesh: dp: 16 (over z, x, core), pb: 2 (over y).
Axes of the slice: x: 2, y: 2, z: 4, core: 2. Of those that a mesh axis runs over, the one named last changes fastest.
Arguments:
- obs_first: float32 [24, 4096], P(None, ('dp', 'pb')), may hold values from -6 to 6
- obs_next: float32 [5, 24, 4096], P(None, None, ('dp', 'pb')), may hold values from -6 to 6
- actions: float32 [5, 6, 4096], P(None, None, ('dp', 'pb')), may hold values from -1 to 1
- rewards: float32 [5, 4096], P(None, ('dp', 'pb')), may hold values from 0 to 1
- enc_w1: float32 [24, 256], replicated, may hold values from -1.25 to 1.25
- enc_b1: float32 [256], replicated, may hold values from -1.5 to 1.5
- enc_w2: float32 [256, 50], replicated, may hold values from -0.375 to 0.375
- enc_b2: float32 [50], replicated, may hold values from -1.5 to 1.5
- dyn_w1: float32 [56, 512], replicated, may hold values from -0.75 to 0.75
- dyn_b1: float32 [512], replicated, may hold values from -1.5 to 1.5
- dyn_w2: float32 [512, 512], replicated, may hold values from -0.25 to 0.25
- dyn_b2: float32 [512], replicated, may hold values from -1.5 to 1.5
- dyn_w3: float32 [512, 50], replicated, may hold values from -0.25 to 0.25
- dyn_b3: float32 [50], replicated, may hold values from -1.5 to 1.5
- rew_w1: float32 [56, 512], replicated, may hold values from -0.75 to 0.75
- rew_b1: float32 [512], replicated, may hold values from -1.5 to 1.5
- rew_w2: float32 [512, 512], replicated, may hold values from -0.25 to 0.25
- rew_b2: float32 [512], replicated, may hold values from -1.5 to 1.5
- rew_w3: float32 [512], replicated, may hold values from -0.25 to 0.25
- rew_b3: float32 [1], replicated, may hold values from -2.5 to 2.5
- pol_w1: float32 [50, 512], replicated, may hold values from -0.875 to 0.875
- pol_b1: float32 [512], replicated, may hold values from -1.5 to 1.5
- pol_w2: float32 [512, 512], replicated, may hold values from -0.25 to 0.25
- pol_b2: float32 [512], replicated, may hold values from -1.5 to 1.5
- pol_w3: float32 [512, 6], replicated, may hold values from -0.25 to 0.25
- pol_b3: float32 [6], replicated, may hold values from -1.5 to 1.5
- q_w1: float32 [2, 56, 512], P('pb'), may hold values from -0.75 to 0.75
- q_b1: float32 [2, 512], P('pb'), may hold values from -1.5 to 1.5
- q_gain: float32 [2, 512], P('pb'), may hold values from 0.5 to 1.5
- q_shift: float32 [2, 512], P('pb'), may hold values from -1.5 to 1.5
- q_w2: float32 [2, 512, 512], P('pb'), may hold values from -0.25 to 0.25
- q_b2: float32 [2, 512], P('pb'), may hold values from -1.5 to 1.5
- q_w3: float32 [2, 512], P('pb'), may hold values from -0.25 to 0.25
- q_b3: float32 [2], P('pb'), may hold values from -2.5 to 2.5
Outputs:
- grad_enc_w1: float32 [24, 256], replicated
- grad_enc_b1: float32 [256], replicated
- grad_enc_w2: float32 [256, 50], replicated
- grad_enc_b2: float32 [50], replicated
- grad_dyn_w1: float32 [56, 512], replicated
- grad_dyn_b1: float32 [512], replicated
- grad_dyn_w2: float32 [512, 512], replicated
- grad_dyn_b2: float32 [512], replicated
- grad_dyn_w3: float32 [512, 50], replicated
- grad_dyn_b3: float32 [50], replicated
- grad_rew_w1: float32 [56, 512], replicated
- grad_rew_b1: float32 [512], replicated
- grad_rew_w2: float32 [512, 512], replicated
- grad_rew_b2: float32 [512], replicated
- grad_rew_w3: float32 [512], replicated
- grad_rew_b3: float32 [1], replicated
- grad_pol_w1: float32 [50, 512], replicated
- grad_pol_b1: float32 [512], replicated
- grad_pol_w2: float32 [512, 512], replicated
- grad_pol_b2: float32 [512], replicated
- grad_pol_w3: float32 [512, 6], replicated
- grad_pol_b3: float32 [6], replicated
- grad_q_w1: float32 [2, 56, 512], P('pb')
- grad_q_b1: float32 [2, 512], P('pb')
- grad_q_gain: float32 [2, 512], P('pb')
- grad_q_shift: float32 [2, 512], P('pb')
- grad_q_w2: float32 [2, 512, 512], P('pb')
- grad_q_b2: float32 [2, 512], P('pb')
- grad_q_w3: float32 [2, 512], P('pb')
- grad_q_b3: float32 [2], P('pb')
- obs_grad: float32 [24, 4096], P(None, ('dp', 'pb'))
- priorities: float32 [4096], replicated
The draws below stay inside these ranges and needn't reach their ends.
All inputs are finite; a program needn't handle non-finite values.
Results may differ from the reference program's by a relative error of at most 0.0003.
Values sent between devices are 32-bit elements; how exact they have to be, the bound alone decides.
No kernel may reach another device: no remote copies, remote signals or barrier semaphores. Data moves between devices by JAX's collectives and lax.ppermute only.
A program may use at most 128 MiB of HBM per device.

```python
import jax
import jax.numpy as jnp
from jax import lax

OBS = 24
ACT = 6
ENC_H = 256
LAT = 50
MLP = 512
HORIZON = 5
TWIN = 2
SEQS = 4096
N_DP = 16


def steps_of(key, shape, shards, low, largest):
    def one(axis_at, parts):
        steps = jax.random.uniform(jax.random.fold_in(jax.random.fold_in(key, 6), axis_at), (parts,), jnp.float32, low / len(shards), largest / len(shards))
        return jnp.repeat(jnp.exp(steps), shape[axis_at] // parts).reshape((-1,) + (1,) * (len(shape) - axis_at - 1))

    gain = one(*shards[0])
    for cut in shards[1:]:
        gain = gain * one(*cut)
    return gain


def bell_draw(rng, extent, scale, bound, pieces=(), kind=jnp.bfloat16):
    values = jax.random.normal(rng, extent, jnp.float32) * scale
    if len(pieces) > 0:
        values = steps_of(rng, extent, pieces, -0.22, 0.18) * values
    return jnp.clip(values, min=-bound, max=bound).astype(kind)


def setup_inputs(seed: int = 0) -> dict:
    streams_of = jax.random.split(jax.random.key(seed), 35)
    obs_first = bell_draw(streams_of[0], (OBS, SEQS), 1.0, 6.0, ((1, 32),), jnp.float32)
    obs_next = bell_draw(streams_of[1], (HORIZON, OBS, SEQS), 1.0, 6.0, ((2, 32),), jnp.float32)
    actions = jnp.clip(jax.random.uniform(streams_of[2], (HORIZON, ACT, SEQS), jnp.float32, -1.0, 1.0) * steps_of(streams_of[2], (HORIZON, ACT, SEQS), ((2, 32),), -0.4, 0.0), -1.0, 1.0)
    rewards = jnp.clip(1.0 * jax.random.uniform(streams_of[3], (HORIZON, SEQS), jnp.float32) ** steps_of(streams_of[3], (HORIZON, SEQS), ((1, 32),), -0.2, 0.2), 0.0, 1.0)
    enc_w1 = bell_draw(streams_of[4], (OBS, ENC_H), OBS ** -0.5, 1.25, (), jnp.float32)
    enc_b1 = bell_draw(streams_of[5], (ENC_H,), 0.3, 1.5, (), jnp.float32)
    enc_w2 = bell_draw(streams_of[6], (ENC_H, LAT), ENC_H ** -0.5, 0.375, (), jnp.float32)
    enc_b2 = bell_draw(streams_of[7], (LAT,), 0.3, 1.5, (), jnp.float32)
    dyn_w1 = bell_draw(streams_of[8], (LAT + ACT, MLP), (LAT + ACT) ** -0.5, 0.75, (), jnp.float32)
    dyn_b1 = bell_draw(streams_of[9], (MLP,), 0.3, 1.5, (), jnp.float32)
    dyn_w2 = bell_draw(streams_of[10], (MLP, MLP), MLP ** -0.5, 0.25, (), jnp.float32)
    dyn_b2 = bell_draw(streams_of[11], (MLP,), 0.3, 1.5, (), jnp.float32)
    dyn_w3 = bell_draw(streams_of[12], (MLP, LAT), MLP ** -0.5, 0.25, (), jnp.float32)
    dyn_b3 = bell_draw(streams_of[13], (LAT,), 0.3, 1.5, (), jnp.float32)
    rew_w1 = bell_draw(streams_of[14], (LAT + ACT, MLP), (LAT + ACT) ** -0.5, 0.75, (), jnp.float32)
    rew_b1 = bell_draw(streams_of[15], (MLP,), 0.3, 1.5, (), jnp.float32)
    rew_w2 = bell_draw(streams_of[16], (MLP, MLP), MLP ** -0.5, 0.25, (), jnp.float32)
    rew_b2 = bell_draw(streams_of[17], (MLP,), 0.3, 1.5, (), jnp.float32)
    rew_w3 = bell_draw(streams_of[18], (MLP,), MLP ** -0.5, 0.25, (), jnp.float32)
    rew_b3 = bell_draw(streams_of[19], (1,), 0.5, 2.5, (), jnp.float32)
    pol_w1 = bell_draw(streams_of[20], (LAT, MLP), LAT ** -0.5, 0.875, (), jnp.float32)
    pol_b1 = bell_draw(streams_of[21], (MLP,), 0.3, 1.5, (), jnp.float32)
    pol_w2 = bell_draw(streams_of[22], (MLP, MLP), MLP ** -0.5, 0.25, (), jnp.float32)
    pol_b2 = bell_draw(streams_of[23], (MLP,), 0.3, 1.5, (), jnp.float32)
    pol_w3 = bell_draw(streams_of[24], (MLP, ACT), MLP ** -0.5, 0.25, (), jnp.float32)
    pol_b3 = bell_draw(streams_of[25], (ACT,), 0.3, 1.5, (), jnp.float32)
    q_w1 = bell_draw(streams_of[26], (TWIN, LAT + ACT, MLP), (LAT + ACT) ** -0.5, 0.75, ((0, 2),), jnp.float32)
    q_b1 = bell_draw(streams_of[27], (TWIN, MLP), 0.3, 1.5, ((0, 2),), jnp.float32)
    q_gain = jnp.clip(1.0 + 0.1 * jax.random.normal(streams_of[28], (TWIN, MLP), jnp.float32), 0.5, 1.5)
    q_shift = bell_draw(streams_of[29], (TWIN, MLP), 0.3, 1.5, ((0, 2),), jnp.float32)
    q_w2 = bell_draw(streams_of[30], (TWIN, MLP, MLP), MLP ** -0.5, 0.25, ((0, 2),), jnp.float32)
    q_b2 = bell_draw(streams_of[31], (TWIN, MLP), 0.3, 1.5, ((0, 2),), jnp.float32)
    q_w3 = bell_draw(streams_of[32], (TWIN, MLP), MLP ** -0.5, 0.25, ((0, 2),), jnp.float32)
    q_b3 = bell_draw(streams_of[33], (TWIN,), 0.5, 2.5, ((0, 2),), jnp.float32)
    return dict(obs_first=obs_first, obs_next=obs_next, actions=actions, rewards=rewards, enc_w1=enc_w1, enc_b1=enc_b1, enc_w2=enc_w2, enc_b2=enc_b2, dyn_w1=dyn_w1, dyn_b1=dyn_b1, dyn_w2=dyn_w2, dyn_b2=dyn_b2, dyn_w3=dyn_w3, dyn_b3=dyn_b3, rew_w1=rew_w1, rew_b1=rew_b1, rew_w2=rew_w2, rew_b2=rew_b2, rew_w3=rew_w3, rew_b3=rew_b3, pol_w1=pol_w1, pol_b1=pol_b1, pol_w2=pol_w2, pol_b2=pol_b2, pol_w3=pol_w3, pol_b3=pol_b3, q_w1=q_w1, q_b1=q_b1, q_gain=q_gain, q_shift=q_shift, q_w2=q_w2, q_b2=q_b2, q_w3=q_w3, q_b3=q_b3)


@jax.custom_vjp
def low(v):
    return lax.optimization_barrier(v.astype(jnp.bfloat16)).astype(jnp.float32)

@jax.custom_vjp
def low_back(v):
    return v

def low_keep(v):
    return (low(v), None)

def low_pass(kept, grad):
    return (grad,)

def back_keep(v):
    return (v, None)

def back_low(kept, grad):
    return (low(grad),)
low.defvjp(low_keep, low_pass)
low_back.defvjp(back_keep, back_low)
highest = lax.Precision.HIGHEST
decay_rate = 0.5
discount = 0.99
consist_coef = 2.0
reward_coef = 0.5
value_coef = 0.1
policy_coef = 0.1
norm_epsilon = 1e-05

def linear(weight, bias, inputs):
    return jnp.einsum('io,...ir->...or', weight, inputs, precision=highest) + bias[:, None]

def encode(weights, observed):
    hidden = jax.nn.elu(linear(weights[0], weights[1], observed))
    return linear(weights[2], weights[3], hidden)

def hidden_pair(weights, inputs):
    hidden = jax.nn.elu(linear(weights[0], weights[1], inputs))
    return jax.nn.elu(linear(weights[2], weights[3], hidden))

def policy(pol_weights, latent):
    return jnp.tanh(linear(pol_weights[4], pol_weights[5], hidden_pair(pol_weights[0:4], latent)))

def reward_head(weights, latent, action):
    hidden = hidden_pair(weights[10:14], jnp.concatenate([latent, action], axis=-2))
    return jnp.einsum('i,...ir->...r', weights[14], hidden, precision=highest) + weights[15][0]

def qvalue_stack(weights, latent, action):
    inputs = jnp.concatenate([latent, action], axis=-2)
    first = jnp.einsum('qio,tir->qtor', weights[0], inputs, precision=highest) + weights[1][:, None, :, None]
    center = first - lax.optimization_barrier(jnp.mean(first, axis=2, keepdims=True))
    normed = center * lax.rsqrt(lax.optimization_barrier(jnp.mean(center * center, axis=2, keepdims=True)) + norm_epsilon)
    hidden = jnp.tanh(weights[2][:, None, :, None] * normed + weights[3][:, None, :, None])
    second = jax.nn.elu(jnp.einsum('qio,qtir->qtor', weights[4], hidden, precision=highest) + weights[5][:, None, :, None])
    return jnp.einsum('qi,qtir->qtr', weights[6], second, precision=highest) + weights[7][:, None, None]

def local_terms(weights, first, action_block, reward_block, latent_next, scale):
    latent = encode(weights[0:4], first)
    states = []
    predicted = []
    for step in range(action_block.shape[0]):
        states.append(latent)
        joined = jnp.concatenate([latent, action_block[step]], axis=0)
        latent = linear(weights[8], weights[9], hidden_pair(weights[4:8], joined))
        predicted.append(latent)
    states = jnp.stack(states)
    predicted = jnp.stack(predicted)
    consist = lax.optimization_barrier(jnp.mean((predicted - latent_next) ** 2, axis=1))
    reward_err = (reward_head(weights, states, action_block) - reward_block) ** 2
    decay = decay_rate ** jnp.arange(states.shape[0], dtype=jnp.float32)
    loss = jnp.sum(decay[:, None] * (consist_coef * consist + reward_coef * reward_err)) * scale
    return (loss, states)

def value_terms(weights, states, action_block, target, scale):
    error = qvalue_stack(weights, states, action_block) - target
    decay = decay_rate ** jnp.arange(states.shape[0], dtype=jnp.float32)
    loss = jnp.sum(decay[None, :, None] * value_coef * error * error) * scale
    spread = lax.optimization_barrier(jnp.sum(jnp.sqrt(error * error + 1.0), axis=(0, 1)))
    return (loss, spread)

def picked_terms(held_weights, held_states, chosen, scale):
    picked = qvalue_stack(held_weights, held_states, chosen)
    decay = decay_rate ** jnp.arange(held_states.shape[0], dtype=jnp.float32)
    return -policy_coef * 0.5 * jnp.sum(decay[None, :, None] * picked) * scale

def reference(obs_first, obs_next, actions, rewards, enc_w1, enc_b1, enc_w2, enc_b2, dyn_w1, dyn_b1, dyn_w2, dyn_b2, dyn_w3, dyn_b3, rew_w1, rew_b1, rew_w2, rew_b2, rew_w3, rew_b3, pol_w1, pol_b1, pol_w2, pol_b2, pol_w3, pol_b3, q_w1, q_b1, q_gain, q_shift, q_w2, q_b2, q_w3, q_b3):
    params = (enc_w1, enc_b1, enc_w2, enc_b2, dyn_w1, dyn_b1, dyn_w2, dyn_b2, dyn_w3, dyn_b3, rew_w1, rew_b1, rew_w2, rew_b2, rew_w3, rew_b3, pol_w1, pol_b1, pol_w2, pol_b2, pol_w3, pol_b3, q_w1, q_b1, q_gain, q_shift, q_w2, q_b2, q_w3, q_b3)
    blocks = N_DP
    width = SEQS // blocks
    scale = 1.0 / SEQS

    def split(array):
        return jnp.moveaxis(array.reshape(array.shape[:-1] + (blocks, width)), -2, 0)
    inputs = (split(obs_first), split(obs_next), split(actions), split(rewards))
    zeros = tuple((jnp.zeros_like(weight) for weight in params))

    def one_block(carry, block):
        first_block, next_block, action_block, reward_block = block
        latent_next = encode(params[0:4], next_block)
        action_next = policy(params[16:22], latent_next)
        target = reward_block + discount * lax.optimization_barrier(jnp.min(qvalue_stack(params[22:30], latent_next, action_next), axis=0))

        def forward(weights, observed):
            loss, states = local_terms(weights[0:22], observed, action_block, reward_block, latent_next, scale)
            value, spread = value_terms(weights[22:30], states, action_block, target, scale)
            return (loss + value, (states, spread))
        total, back, (states, spread) = jax.vjp(forward, params, first_block, has_aux=True)
        grads, obs_part = back(jnp.ones_like(total))

        def policy_forward(pol_weights):
            return picked_terms(params[22:30], states, policy(pol_weights, states), scale)
        pol_total, pol_back = jax.vjp(policy_forward, params[16:22])
        pol_grads = pol_back(jnp.ones_like(pol_total))[0]
        grads = tuple(grads[0:16]) + tuple((older + newer for older, newer in zip(grads[16:22], pol_grads))) + tuple(grads[22:30])
        carry = tuple((older + newer for older, newer in zip(carry, grads)))
        return (carry, (obs_part * SEQS, spread / (TWIN * HORIZON)))
    grads, (obs_parts, spreads) = lax.scan(one_block, zeros, inputs)
    obs_grad = jnp.moveaxis(obs_parts, 0, 1).reshape(OBS, SEQS)
    priorities = spreads.reshape(SEQS)
    return (grads[0], grads[1], grads[2], grads[3], grads[4], grads[5], grads[6], grads[7], grads[8], grads[9], grads[10], grads[11], grads[12], grads[13], grads[14], grads[15], grads[16], grads[17], grads[18], grads[19], grads[20], grads[21], grads[22], grads[23], grads[24], grads[25], grads[26], grads[27], grads[28], grads[29], obs_grad, priorities)
```

```python
import functools

import jax
import jax.numpy as jnp
from jax import lax
from jax.experimental import pallas as pl
from jax.experimental.pallas import tpu as pltpu
from jax.sharding import PartitionSpec as P

f32 = jnp.float32
bf16 = jnp.bfloat16

TWIN = 2
LANES = 128
decay_rate = 0.5
discount = 0.99
consist_coef = 2.0
reward_coef = 0.5
value_coef = 0.1
policy_coef = 0.1
norm_epsilon = 1e-05

TURNED = ("enc_w2", "dyn_w3", "pol_w3")
NN = ((1,), (0,))
NT = ((1,), (1,))
TN = ((0,), (0,))

NAMES = (
    "obs_first",
    "obs_next",
    "actions",
    "rewards",
    "enc_w1",
    "enc_b1",
    "enc_w2",
    "enc_b2",
    "dyn_w1",
    "dyn_b1",
    "dyn_w2",
    "dyn_b2",
    "dyn_w3",
    "dyn_b3",
    "rew_w1",
    "rew_b1",
    "rew_w2",
    "rew_b2",
    "rew_w3",
    "rew_b3",
    "pol_w1",
    "pol_b1",
    "pol_w2",
    "pol_b2",
    "pol_w3",
    "pol_b3",
    "q_w1",
    "q_b1",
    "q_gain",
    "q_shift",
    "q_w2",
    "q_b2",
    "q_w3",
    "q_b3",
)


def up(number, multiple):
    return -(-number // multiple) * multiple


def mm(left, right, dims):
    return lax.dot_general(left, right, (dims, ((), ())), preferred_element_type=f32)


def split(value):
    high = value.astype(bf16)
    return high, (value - high.astype(f32)).astype(bf16)


def dot3(left, right, dims):
    return (
        mm(left[0], right[0], dims) + mm(left[0], right[1], dims) + mm(left[1], right[0], dims)
    )


def dot3_narrow(left, right, dims):
    width = right[0].shape[1]
    both = mm(left[0], jnp.concatenate(right, axis=1), dims)
    return both[:, :width] + both[:, width:] + mm(left[1], right[0], dims)


def stack_weight(parts):
    return jnp.concatenate([parts[0], parts[0], parts[1]], axis=0)


def stack_input(parts):
    return jnp.concatenate([parts[0], parts[1], parts[0]], axis=0)


def elu(value):
    return jnp.where(value > 0, value, jnp.exp(jnp.minimum(value, 0.0)) - 1.0)


def elu_slope(result):
    return jnp.where(result > 0, 1.0, result + 1.0)


def fold(value):
    total = value[:, :LANES]
    for at in range(LANES, value.shape[1], LANES):
        total = total + value[:, at : at + LANES]
    return total


def spread_lanes(column, width):
    return jnp.concatenate([column] * (width // LANES), axis=1)


def columns_of(rows):
    count = len(rows)
    deep = up(3 * count, 16)
    value = jnp.concatenate(rows, axis=0)
    first = value.astype(bf16)
    rest = value - first.astype(f32)
    second = rest.astype(bf16)
    third = (rest - second.astype(f32)).astype(bf16)
    parts = [first.astype(f32), second.astype(f32), third.astype(f32)]
    if deep > 3 * count:
        parts.append(jnp.zeros((deep - 3 * count, value.shape[1]), f32))
    stacked = jnp.concatenate(parts, axis=0).astype(bf16)
    at = lax.broadcasted_iota(jnp.int32, (deep, count * LANES), 0)
    lane = lax.broadcasted_iota(jnp.int32, (deep, count * LANES), 1)
    block = lane // LANES
    pick = ((at == block) | (at == block + count) | (at == block + 2 * count)) & (at < 3 * count)
    return mm(stacked, pick.astype(f32).astype(bf16), TN)


def rows_of(blocks):
    count = len(blocks)
    high, low = split(jnp.concatenate(blocks, axis=1))
    at = lax.broadcasted_iota(jnp.int32, (16, count * LANES), 0)
    lane = lax.broadcasted_iota(jnp.int32, (16, count * LANES), 1)
    pick = (lane // LANES == at).astype(f32).astype(bf16)
    return mm(pick, high, NT) + mm(pick, low, NT)


def decay_row(horizon, width, factor):
    return jnp.concatenate(
        [jnp.full((1, width), factor * decay_rate**step, f32) for step in range(horizon)], axis=1
    )


def first_lane(total, width):
    lane = lax.broadcasted_iota(jnp.int32, (1, width), 1)
    return jnp.where(lane == 0, total, 0.0)


def row(ref):
    return ref[...].reshape(1, ref.shape[-1])


class Sizes:
    def __init__(self, obs_next, actions, enc_w1, dyn_w1):
        self.horizon, self.obs, self.seqs = obs_next.shape
        self.act = actions.shape[1]
        self.hidden = enc_w1.shape[1]
        joined, self.mlp = dyn_w1.shape
        self.lat = joined - self.act
        self.one = joined
        self.deep = up(joined + 1, 16)
        self.obs_deep = up(self.obs + 1, 16)
        self.lat_deep = up(self.lat, 16)
        self.act_deep = up(self.act, 16)
        self.cols = self.horizon * self.seqs
        self.net_rows = self.mlp + self.deep
        self.at_w3 = self.net_rows
        self.at_enc = self.at_w3 + up(self.lat, 8)
        self.at_prio = self.at_enc + up(max(self.lat, self.obs_deep + 1), 16)

    def dyn_rows(self, total):
        self.prio_rows = up(-(-total // self.mlp), 8)
        return up(self.at_prio + self.prio_rows, 64)


def places():
    dp = lax.axis_index("dp")
    pb = lax.axis_index("pb")
    core = lax.rem(dp, 2)
    side = lax.rem(lax.div(dp, 2), 2)
    return dp, pb, core, side


def square(relative):
    dp, pb, core, side = places()
    return lax.rem(side + relative // 2, 2) * 2 + lax.rem(pb + relative % 2, 2)


def ready_kernel(out):
    out[...] = jnp.zeros_like(out)


def pack_kernel(w1, b1, gain, shift, w2, b2, w3, b3, out, lines, rows, sems):
    mlp = w2.shape[1]
    joined = w1.shape[1]
    half = out.shape[0]
    core = places()[2]

    @pl.when(core == 0)
    def _():
        copy = pltpu.make_async_copy(w2.at[0, pl.ds(0, half)], out, sems.at[0])
        copy.start()
        copy.wait()

    @pl.when(core == 1)
    def _():
        rest = mlp - half
        big = [
            pltpu.make_async_copy(w2.at[0, pl.ds(half, rest)], out.at[pl.ds(0, rest)], sems.at[0]),
            pltpu.make_async_copy(w1.at[0], out.at[pl.ds(rest, joined)], sems.at[1]),
        ]
        small = [
            pltpu.make_async_copy(ref, lines.at[at], sems.at[2 + at])
            for at, ref in enumerate((b1, gain, shift, b2, w3))
        ]
        for copy in big + small:
            copy.start()
        rows[...] = jnp.zeros_like(rows)
        for at, copy in enumerate(small):
            copy.wait()
            rows[at : at + 1] = lines[at]
        rows[5:6] = jnp.full((1, mlp), b3[0], f32)
        copy = pltpu.make_async_copy(rows, out.at[pl.ds(rest + joined, 8)], sems.at[7])
        copy.start()
        for each in big + [copy]:
            each.wait()


def rollout_kernel(
    size,
    scale,
    obs_first,
    obs_next,
    actions,
    rewards,
    enc_w1,
    enc_b1,
    enc_w2,
    enc_b2,
    dyn_w1,
    dyn_b1,
    dyn_w2,
    dyn_b2,
    dyn_w3,
    dyn_b3,
    rew_w1,
    rew_b1,
    rew_w2,
    rew_b2,
    rew_w3,
    rew_b3,
    pol_w1,
    pol_b1,
    pol_w2,
    pol_b2,
    pol_w3,
    pol_b3,
    joint,
    reward_grads,
    state_grad,
    consist,
    dyn_h1,
    dyn_h2,
    pol_h1,
    pol_h2,
    enc_h,
    obs_aug,
    w_aug,
    w_out,
    w_act,
    e_aug,
    e_out,
):
    lat, act, one, deep = size.lat, size.act, size.one, size.deep
    mlp, seqs, cols, horizon = size.mlp, size.seqs, size.cols, size.horizon
    joined = lat + act

    def first_weight(ref, bias, kept):
        w_aug[...] = jnp.zeros_like(w_aug)
        w_aug[:kept] = ref[...]
        w_aug[one : one + 1] = row(bias)
        return split(w_aug[...])

    obs_aug[...] = jnp.zeros_like(obs_aug)
    for step in range(horizon):
        obs_aug[: size.obs, step * seqs : (step + 1) * seqs] = obs_next[step]
    obs_aug[: size.obs, cols:] = obs_first[...]
    obs_aug[size.obs : size.obs + 1] = jnp.ones((1, cols + seqs), f32)
    e_aug[...] = jnp.zeros_like(e_aug)
    e_aug[: size.obs] = enc_w1[...]
    e_aug[size.obs : size.obs + 1] = row(enc_b1)
    e_out[...] = jnp.zeros_like(e_out)
    e_out[:lat] = enc_w2[...]
    w_out[...] = jnp.zeros_like(w_out)
    w_out[:lat] = dyn_w3[...]
    w_act[...] = jnp.zeros_like(w_act)
    w_act[:act] = pol_w3[...]
    small = jnp.concatenate(
        [
            jnp.concatenate([row(enc_b2), jnp.zeros((1, LANES - lat), f32)], axis=1),
            jnp.concatenate([row(dyn_b3), jnp.zeros((1, LANES - lat), f32)], axis=1),
            jnp.concatenate([row(pol_b3), jnp.zeros((1, LANES - act), f32)], axis=1),
        ],
        axis=0,
    )
    small = columns_of([small[0:1], small[1:2], small[2:3]])
    enc_b2_col = small[: size.lat_deep, :LANES]
    dyn_b3_col = small[: size.lat_deep, LANES : 2 * LANES]
    pol_b3_col = small[: size.act_deep, 2 * LANES :]
    wide = columns_of([row(dyn_b2), row(rew_b2), row(rew_w3), row(pol_b2)])
    dyn_b2_col = wide[:, :LANES]

    enc_first = mm(stack_weight(split(e_aug[...])), stack_input(split(obs_aug[...])), TN)
    enc_hidden = elu(enc_first)
    enc_h[...] = enc_hidden[:, cols:]
    latent = dot3(split(e_out[...]), split(enc_hidden), NN) + spread_lanes(
        enc_b2_col, cols + seqs
    )
    joint[:, :] = jnp.zeros_like(joint)
    joint[: size.lat_deep, 2 * cols :] = latent[:, :cols]
    for step in range(horizon):
        joint[lat : lat + act, step * seqs : (step + 1) * seqs] = actions[step]
    joint[one : one + 1] = jnp.ones((1, 3 * cols), f32)

    first = stack_weight(first_weight(dyn_w1, dyn_b1, joined))
    second = split(dyn_w2[...].T)
    third = split(w_out[...])
    latent = latent[:, cols:]
    for step in range(horizon):
        here = slice(step * seqs, (step + 1) * seqs)
        joint[:lat, here] = latent[:lat]
        hidden = elu(mm(first, stack_input(split(joint[:, here])), TN))
        dyn_h1[:, here] = hidden
        hidden = elu(dot3_narrow(second, split(hidden), NN) + dyn_b2_col)
        dyn_h2[:, here] = hidden
        latent = dot3_narrow(third, split(hidden), NN) + dyn_b3_col
        after = 2 * cols + step * seqs
        goal = joint[: size.lat_deep, after : after + seqs]
        factor = scale * decay_rate**step * consist_coef * 2.0 / lat
        consist[:, here] = factor * (latent - goal)

    states = split(joint[:, :cols])
    first = first_weight(rew_w1, rew_b1, joined)
    second = split(rew_w2[...])
    b2_col = spread_lanes(wide[:, LANES : 2 * LANES], cols)
    w3_col = spread_lanes(wide[:, 2 * LANES : 3 * LANES], cols)
    h1 = elu(mm(stack_weight(first), stack_input(states), TN))
    h1_parts = split(h1)
    h2 = elu(dot3(second, h1_parts, TN) + b2_col)
    predicted = jnp.sum(w3_col * h2, axis=0, keepdims=True) + rew_b3[0]
    wanted = jnp.concatenate([rewards[step : step + 1] for step in range(horizon)], axis=1)
    out_grad = decay_row(horizon, seqs, scale * reward_coef * 2.0) * (predicted - wanted)
    h2_grad = w3_col * out_grad * elu_slope(h2)
    h2_parts = split(h2_grad)
    reward_grads[:mlp] = dot3(h1_parts, h2_parts, NT)
    h1_grad = dot3(second, h2_parts, NN) * elu_slope(h1)
    h1_grad = split(h1_grad)
    reward_grads[mlp:] = dot3(states, h1_grad, NT)
    state_grad[...] = dot3(first, h1_grad, NN)
    sums = rows_of([fold(h2_grad), fold(h2 * out_grad)])
    reward_grads[mlp + one + 1 : mlp + one + 3] = sums[:2]
    reward_grads[mlp + one + 3 : mlp + one + 4] = first_lane(jnp.sum(out_grad), mlp)

    first = stack_weight(first_weight(pol_w1, pol_b1, lat))
    b2_col = spread_lanes(wide[:, 3 * LANES :], cols)
    second = split(pol_w2[...])
    third = split(w_act[...])
    for block in (0, 2):
        here = slice(block * cols, (block + 1) * cols)
        h1 = elu(mm(first, stack_input(split(joint[:, here])), TN))
        h2 = elu(dot3(second, split(h1), TN) + b2_col)
        action = jnp.tanh(dot3(third, split(h2), NN) + spread_lanes(pol_b3_col, cols))[:act]
        if block == 0:
            pol_h1[...] = h1
            pol_h2[...] = h2
            joint[:lat, cols : 2 * cols] = joint[:lat, :cols]
            joint[lat:joined, cols : 2 * cols] = action
        else:
            joint[lat:joined, here] = action


def value_kernel(
    size,
    scale,
    joint,
    rewards,
    reward_grads,
    q_w1,
    q_b1,
    q_gain,
    q_shift,
    q_w2,
    q_b2,
    q_w3,
    q_b3,
    packed_y,
    packed_c,
    keep0,
    keep1,
    keep2,
    keep3,
    send0,
    send1,
    send2,
    send3,
    state_grad,
    chosen_grad,
    prio,
    packed,
    aug,
    w1_rows,
    w1_lanes,
    w2_rows,
    w2_lanes,
    vectors,
    last,
    inputs,
    next_value,
    spread,
    grads,
    work,
    normed,
    second,
    hidden,
    backs,
    sums,
):
    lat, act, one, deep = size.lat, size.act, size.one, size.deep
    mlp, seqs, cols, horizon = size.mlp, size.seqs, size.cols, size.horizon
    joined = lat + act
    dp, pb, core, side = places()
    half = packed_y.shape[0]
    packed[pl.ds(pl.multiple_of(core * half, 8), half)] = packed_y[...]
    packed[pl.ds(pl.multiple_of((1 - core) * half, 8), half)] = packed_c[...]

    at = mlp + joined
    for slot in range(TWIN):
        if slot == 0:
            w1, b1, w2 = q_w1[0], q_b1[...], q_w2[0]
            rows = [q_gain[...], q_shift[...], q_b2[...], q_w3[...]]
            b3 = jnp.full((1, LANES), q_b3[0], f32)
        else:
            w1, b1, w2 = packed[mlp:at], packed[at : at + 1], packed[:mlp]
            rows = [packed[at + i : at + i + 1] for i in (1, 2, 3, 4)]
            b3 = packed[at + 5 : at + 6, :LANES]
        aug[...] = jnp.zeros_like(aug)
        aug[:joined] = w1
        aug[one : one + 1] = b1
        high, low = split(aug[...])
        for place, part in enumerate((high, high, low)):
            w1_rows[slot, place * deep : (place + 1) * deep] = part
            w1_lanes[slot, :, place * mlp : (place + 1) * mlp] = part
        high, low = split(w2)
        for place, part in enumerate((high, high, low)):
            w2_rows[slot, place * mlp : (place + 1) * mlp] = part
            w2_lanes[slot, :, place * mlp : (place + 1) * mlp] = part
        vectors[slot] = columns_of(rows)
        last[slot] = b3
    inputs[...] = stack_input(split(joint[...]))

    height = 16

    def blocks(width):
        for left in range(0, width, cols):
            for top in range(0, mlp, height):
                yield slice(top, top + height), slice(left, left + cols)

    def column(slot, which, rows):
        return spread_lanes(vectors[slot, rows, which * LANES : (which + 1) * LANES], cols)

    def keep_parts(ref, rows, here, value):
        high, low = split(value)
        for place, part in enumerate((high, low, high)):
            ref[rows.start + place * mlp : rows.stop + place * mlp, here] = part

    def added(totals, here, value):
        eight = value.reshape(height // 8, 8, cols).sum(axis=0)
        at = here.start // cols
        totals[at] = eight if totals[at] is None else totals[at] + eight

    def total_of(totals):
        return jnp.concatenate([jnp.sum(t, axis=0, keepdims=True) for t in totals], axis=1)

    def forward(slot, start, width, kept):
        work[:, :width] = mm(w1_rows[slot], inputs[:, start : start + width], TN)
        totals = [None] * (width // cols)
        for rows, here in blocks(width):
            added(totals, here, work[rows, here])
        mean = total_of(totals) / mlp
        totals = [None] * (width // cols)
        for rows, here in blocks(width):
            center = work[rows, here] - mean[:, here]
            added(totals, here, center * center)
        inverse = lax.rsqrt(total_of(totals) / mlp + norm_epsilon)
        for rows, here in blocks(width):
            value = (work[rows, here] - mean[:, here]) * inverse[:, here]
            if kept:
                normed[rows, here] = value
            value = jnp.tanh(column(slot, 0, rows) * value + column(slot, 1, rows))
            keep_parts(hidden, rows, here, value)
        work[:, :width] = mm(w2_rows[slot], hidden[:, :width], TN)
        totals = [None] * (width // cols)
        for rows, here in blocks(width):
            value = elu(work[rows, here] + column(slot, 2, rows))
            if kept:
                second[rows, here] = value
            if here.start == 0:
                added(totals, here, column(slot, 3, rows) * value)
        return total_of(totals[:1]) + spread_lanes(last[slot], cols), inverse

    @pl.loop(0, TWIN)
    def _(slot):
        next_value[slot] = forward(slot, 2 * cols, cols, False)[0]

    wanted = jnp.concatenate([rewards[step : step + 1] for step in range(horizon)], axis=1)
    next_value[0] = wanted + discount * jnp.minimum(next_value[0], next_value[1])
    spread[...] = jnp.zeros_like(spread)
    state_grad[...] = jnp.zeros_like(state_grad)
    chosen_grad[...] = jnp.zeros_like(chosen_grad)

    @pl.loop(0, TWIN)
    def _(slot):
        value, inverse = forward(slot, 0, 2 * cols, True)
        error = value - next_value[0]
        spread[...] += jnp.sqrt(error * error + 1.0)
        out_grad = jnp.concatenate(
            [
                decay_row(horizon, seqs, scale * value_coef * 2.0) * error,
                decay_row(horizon, seqs, -policy_coef * 0.5 * scale),
            ],
            axis=1,
        )
        for rows, here in blocks(2 * cols):
            result = second[rows, here]
            back = column(slot, 3, rows) * out_grad[:, here] * elu_slope(result)
            keep_parts(backs, rows, here, back)
            if here.start == 0:
                sums[rows, :LANES] = fold(back)
                sums[rows, 3 * LANES :] = fold(result * out_grad[:, here])
        work[...] = mm(w2_lanes[slot], backs[...], NN)
        grads[slot, :mlp] = dot3(
            (hidden[:mlp, :cols], hidden[mlp : 2 * mlp, :cols]),
            (backs[:mlp, :cols], backs[mlp : 2 * mlp, :cols]),
            NT,
        )
        plain, along = [None] * 2, [None] * 2
        for rows, here in blocks(2 * cols):
            high = hidden[rows, here].astype(f32)
            low = hidden[mlp + rows.start : mlp + rows.stop, here].astype(f32)
            result = high + low
            pre = work[rows, here] * (1.0 - result * result)
            unit = normed[rows, here]
            if here.start == 0:
                sums[rows, LANES : 2 * LANES] = fold(pre * unit)
                sums[rows, 2 * LANES : 3 * LANES] = fold(pre)
            back = column(slot, 0, rows) * pre
            work[rows, here] = back
            added(plain, here, back)
            added(along, here, back * unit)
        plain, along = total_of(plain) / mlp, total_of(along) / mlp
        for rows, here in blocks(2 * cols):
            back = work[rows, here] - plain[:, here] - normed[rows, here] * along[:, here]
            keep_parts(backs, rows, here, back * inverse[:, here])
        states = (inputs[:deep, :cols], inputs[deep : 2 * deep, :cols])
        first_parts = (backs[:mlp, :cols], backs[mlp : 2 * mlp, :cols])
        grads[slot, mlp:] = dot3(states, first_parts, NT)
        into = mm(w1_lanes[slot], backs[...], NN)
        state_grad[...] += into[:, :cols]
        chosen_grad[...] += into[:, cols:]
        lines = rows_of([sums[:, at * LANES : (at + 1) * LANES] for at in range(4)])
        grads[slot, mlp + one + 1 : mlp + one + 5] = lines[:4]
        grads[slot, mlp + one + 5 : mlp + one + 6] = first_lane(jnp.sum(out_grad[:, :cols]), mlp)

    total = spread[:, :seqs]
    for step in range(1, horizon):
        total = total + spread[:, step * seqs : (step + 1) * seqs]
    prio[...] = total / (TWIN * horizon)

    eighth, quarter = size.net_rows // 8, size.net_rows // 4
    for h in range(2):
        place = core if h == 0 else 1 - core
        for k in range(4):
            out = ((keep0, keep1, keep2, keep3), (send0, send1, send2, send3))[h][k]
            start = (place * 4 + square(k)) * eighth
            out[:eighth] = reward_grads[pl.ds(pl.multiple_of(start, 8), eighth)]
            start = (place * 2 + lax.div(square(k), 2)) * quarter
            out[eighth:] = grads[k % 2, pl.ds(pl.multiple_of(start, 8), quarter)]


def policy_kernel(
    size, pol_w2, pol_w3, joint, pol_h1, pol_h2, chosen_grad, pol, w_act, act_grad
):
    lat, act, one = size.lat, size.act, size.one
    mlp, cols = size.mlp, size.cols
    joined = lat + act
    states = split(joint[:, :cols])
    w_act[...] = jnp.zeros_like(w_act)
    w_act[:act] = pol_w3[...]
    act_grad[...] = jnp.zeros_like(act_grad)
    chosen = joint[lat:joined, cols : 2 * cols]
    act_grad[:act] = chosen_grad[lat:joined] * (1.0 - chosen * chosen)
    out_parts = split(act_grad[...])
    weight = split(w_act[...])
    h2 = pol_h2[...]
    h2_grad = mm(stack_weight(weight), stack_input(out_parts), TN) * elu_slope(h2)
    h2_parts = split(h2_grad)
    h1 = pol_h1[...]
    pol[:mlp] = dot3(split(h1), h2_parts, NT)
    h1_grad = dot3(split(pol_w2[...]), h2_parts, NN) * elu_slope(h1)
    pol[mlp:] = dot3(states, split(h1_grad), NT)
    pol[mlp + lat : mlp + joined] = dot3(out_parts, split(h2), NT)[:act]
    pol[mlp + one + 1 : mlp + one + 2] = rows_of([fold(h2_grad)])[:1]
    sums = rows_of([fold(act_grad[...])])
    pol[mlp + one + 2 : mlp + one + 3] = jnp.zeros((1, mlp), f32)
    pol[mlp + one + 2 : mlp + one + 3, : size.act_deep] = sums[:1]


def shared_kernel(
    size,
    scale,
    total,
    obs_first,
    enc_w1,
    enc_w2,
    dyn_w1,
    dyn_w2,
    dyn_w3,
    joint,
    reward_state,
    consist,
    dyn_h1,
    dyn_h2,
    enc_h,
    value_state,
    prio,
    pol,
    keep0,
    keep1,
    keep2,
    keep3,
    send0,
    send1,
    send2,
    send3,
    obs_grad,
    obs_aug,
    w_out,
    e_out,
    lat_grad,
    second_high,
    second_low,
    first_high,
    first_low,
    dyn,
):
    lat, act, one, deep = size.lat, size.act, size.one, size.deep
    mlp, seqs, cols, horizon = size.mlp, size.seqs, size.cols, size.horizon
    joined = lat + act
    lat_deep, hidden = size.lat_deep, size.hidden
    dp, pb, core, side = places()
    states = split(joint[:, :cols])

    w_out[...] = jnp.zeros_like(w_out)
    w_out[:lat] = dyn_w3[...]
    third = stack_weight(split(w_out[...]))
    second = split(dyn_w2[...])
    first = split(dyn_w1[...])
    lat_rows = lax.broadcasted_iota(jnp.int32, (lat_deep, seqs), 0)
    carry = None
    for step in reversed(range(horizon)):
        here = slice(step * seqs, (step + 1) * seqs)
        grad = consist[:, here]
        if carry is not None:
            after = slice((step + 1) * seqs, (step + 2) * seqs)
            grad = grad + carry + reward_state[:lat_deep, after] + value_state[:lat_deep, after]
            grad = jnp.where(lat_rows < lat, grad, 0.0)
        lat_grad[:, here] = grad
        high, low = split(grad)
        h2_grad = mm(third, jnp.concatenate([high, low, high], axis=0), TN)
        h2_grad = h2_grad * elu_slope(dyn_h2[:, here])
        parts = split(h2_grad)
        second_high[:, here], second_low[:, here] = parts
        h1_grad = dot3_narrow(second, parts, NN) * elu_slope(dyn_h1[:, here])
        parts = split(h1_grad)
        first_high[:, here], first_low[:, here] = parts
        back = dot3_narrow(first, parts, NN)
        carry = jnp.concatenate([back, jnp.zeros((lat_deep - joined, seqs), f32)], axis=0)
    grad = carry + reward_state[:lat_deep, :seqs] + value_state[:lat_deep, :seqs]
    grad = jnp.where(lat_rows < lat, grad, 0.0)
    second_parts = (second_high[...], second_low[...])
    first_parts = (first_high[...], first_low[...])
    dyn[:mlp] = dot3(split(dyn_h1[...]), second_parts, NT)
    dyn[mlp : size.net_rows] = dot3(states, first_parts, NT)
    out_grad = lat_grad[...]
    b2_sum = fold(second_high[...].astype(f32) + second_low[...].astype(f32))
    dyn[size.at_w3 : size.at_enc] = dot3(split(out_grad), split(dyn_h2[...]), NT)[
        : size.at_enc - size.at_w3
    ]
    dyn[mlp + one + 1 : mlp + one + 2] = rows_of([b2_sum])[:1]
    dyn[mlp + one + 2 : mlp + one + 3] = jnp.zeros((1, mlp), f32)
    dyn[mlp + one + 2 : mlp + one + 3, :lat_deep] = rows_of([fold(out_grad)])[:1]

    dyn[size.at_enc :] = jnp.zeros((dyn.shape[0] - size.at_enc, mlp), f32)
    obs_aug[...] = jnp.zeros_like(obs_aug)
    obs_aug[: size.obs] = obs_first[...]
    obs_aug[size.obs : size.obs + 1] = jnp.ones((1, seqs), f32)
    e_out[...] = jnp.zeros_like(e_out)
    e_out[:lat] = enc_w2[...]
    parts = split(grad)
    h = enc_h[...]
    h_grad = dot3(split(e_out[...]), parts, TN) * elu_slope(h)
    h_parts = split(h_grad)
    dyn[size.at_enc : size.at_enc + lat_deep, :hidden] = dot3(parts, split(h), NT)
    dyn[size.at_enc : size.at_enc + size.obs_deep, hidden : 2 * hidden] = dot3(
        split(obs_aug[...]), h_parts, NT
    )
    at = size.at_enc + size.obs_deep
    dyn[at : at + 1, hidden : hidden + lat_deep] = rows_of([grad])[:1]
    obs_grad[...] = total * dot3(split(enc_w1[...]), h_parts, NN)

    index = (dp * 2 + pb) * seqs
    rows = size.prio_rows
    at = lax.broadcasted_iota(jnp.int32, (rows, mlp), 0) * mlp
    at = at + lax.broadcasted_iota(jnp.int32, (rows, mlp), 1)
    mine = (at >= index) & (at < index + seqs)
    value = jnp.concatenate([prio[...]] * (mlp // seqs), axis=1)
    dyn[size.at_prio : size.at_prio + rows] = jnp.where(mine, value, 0.0)

    small, large = size.net_rows // 8, dyn.shape[0] // 8
    for h in range(2):
        place = core if h == 0 else 1 - core
        for k in range(4):
            out = ((keep0, keep1, keep2, keep3), (send0, send1, send2, send3))[h][k]
            start = (place * 4 + square(k)) * small
            out[:small] = pol[pl.ds(pl.multiple_of(start, 8), small)]
            start = (place * 4 + square(k)) * large
            out[small:] = dyn[pl.ds(pl.multiple_of(start, 8), large)]


def halve_kernel(*refs):
    for k in range(4):
        refs[8 + k][...] = refs[k][...] + refs[4 + k][...]


def sum_kernel(*refs):
    total = refs[0][...]
    for ref in refs[1:-1]:
        total = total + ref[...]
    refs[-1][...] = total


def lane_block(relative):
    width = 128
    mine = lax.rem(lax.div(lax.axis_index("dp"), 4), 4)
    return pl.ds(pl.multiple_of((mine ^ relative) * width, width), width)


def quarter_kernel(own, from_x, from_y, from_xy, *refs):
    whole = refs[-1]
    whole[...] = (own[...] + from_x[...]) + (from_y[...] + from_xy[...])
    for relative in range(4):
        refs[relative][...] = whole[:, lane_block(relative)]


def gather_kernel(first, second, third, fourth, *outs):
    for relative, ref in enumerate((first, second, third, fourth)):
        for out in outs:
            out[:, lane_block(relative)] = ref[: out.shape[0]]


def collect(out, pieces, first, rows, core, side, pb):
    for h in range(2):
        for k in range(4):
            place = lax.rem(core + h, 2) * 4 + lax.rem(side + k // 2, 2) * 2 + lax.rem(pb + k, 2)
            out[pl.ds(pl.multiple_of(place * rows, 8), rows)] = pieces[h][k][first : first + rows]


def finish_value_kernel(
    size,
    own,
    from_x,
    from_y,
    from_xy,
    c_own,
    c_x,
    c_y,
    c_xy,
    rew_w1,
    rew_b1,
    rew_w2,
    rew_b2,
    rew_w3,
    rew_b3,
    q_w1,
    q_b1,
    q_gain,
    q_shift,
    q_w2,
    q_b2,
    q_w3,
    q_b3,
    rew,
    twin,
):
    dp, pb, core, side = places()
    mlp, one = size.mlp, size.one
    eighth, quarter = size.net_rows // 8, size.net_rows // 4
    pieces = ((own, from_y, from_x, from_xy), (c_own, c_y, c_x, c_xy))
    collect(rew, pieces, 0, eighth, core, side, pb)
    for h in range(2):
        for k in range(2):
            place = lax.rem(core + h, 2) * 2 + lax.rem(side + k, 2)
            twin[pl.ds(pl.multiple_of(place * quarter, 8), quarter)] = pieces[h][2 * k][eighth:]
    rew_w2[...] = rew[:mlp]
    rew_w1[...] = rew[mlp : mlp + one]
    for ref, at in ((rew_b1, 0), (rew_b2, 1), (rew_w3, 2), (rew_b3, 3)):
        n = ref.shape[0]
        ref[...] = rew[mlp + one + at : mlp + one + at + 1, :n].reshape(n)
    q_w2[0] = twin[:mlp]
    q_w1[0] = twin[mlp : mlp + one]
    for at, ref in enumerate((q_b1, q_b2, q_gain, q_shift, q_w3)):
        ref[...] = twin[mlp + one + at : mlp + one + at + 1]
    q_b3[...] = twin[mlp + one + 5 : mlp + one + 6, :1].reshape(1)


def finish_shared_kernel(
    size,
    own,
    from_x,
    from_y,
    from_xy,
    c_own,
    c_x,
    c_y,
    c_xy,
    enc_w1,
    enc_b1,
    enc_w2,
    enc_b2,
    dyn_w1,
    dyn_b1,
    dyn_w2,
    dyn_b2,
    dyn_w3,
    dyn_b3,
    pol_w1,
    pol_b1,
    pol_w2,
    pol_b2,
    pol_w3,
    pol_b3,
    prio,
    pol,
    dyn,
):
    dp, pb, core, side = places()
    mlp, one, lat, act, hidden = size.mlp, size.one, size.lat, size.act, size.hidden
    pieces = ((own, from_y, from_x, from_xy), (c_own, c_y, c_x, c_xy))
    small, large = size.net_rows // 8, dyn.shape[0] // 8
    collect(pol, pieces, 0, small, core, side, pb)
    collect(dyn, pieces, small, large, core, side, pb)

    def line(out, source, at, first=0):
        n = out.shape[0]
        out[...] = source[at : at + 1, first : first + n].reshape(n)

    pol_w2[...] = pol[:mlp]
    pol_w1[...] = pol[mlp : mlp + lat]
    pol_w3[...] = pol[mlp + lat : mlp + lat + act]
    line(pol_b1, pol, mlp + one)
    line(pol_b2, pol, mlp + one + 1)
    line(pol_b3, pol, mlp + one + 2)
    dyn_w2[...] = dyn[:mlp]
    dyn_w1[...] = dyn[mlp : mlp + one]
    dyn_w3[...] = dyn[size.at_w3 : size.at_w3 + lat]
    line(dyn_b1, dyn, mlp + one)
    line(dyn_b2, dyn, mlp + one + 1)
    line(dyn_b3, dyn, mlp + one + 2)
    enc_w2[...] = dyn[size.at_enc : size.at_enc + lat, :hidden]
    enc_w1[...] = dyn[size.at_enc : size.at_enc + size.obs, hidden : 2 * hidden]
    line(enc_b1, dyn, size.at_enc + size.obs, hidden)
    line(enc_b2, dyn, size.at_enc + size.obs_deep, hidden)
    prio[...] = dyn[size.at_prio : size.at_prio + prio.shape[0]]


VMEM = pl.BlockSpec(memory_space=pltpu.VMEM)
SMEM = pl.BlockSpec(memory_space=pltpu.SMEM)


ANY = pl.BlockSpec(memory_space=pl.ANY)
HBM = pl.BlockSpec(memory_space=pltpu.HBM)


def call(
    kernel, name, outs, args, scratch=(), scalars=(), left=(), after=(), flops=0, out_any=False
):
    def made(shape):
        return jax.ShapeDtypeStruct(shape, f32)

    def ordered(*refs):
        return kernel(*refs[: len(args)], *refs[len(args) + len(after) :])

    single = not isinstance(outs, list)
    shapes = [made(shape) for shape in ([outs] if single else outs)]
    moved = 4 * sum(a.size for a in args) + 4 * sum(s.size for s in shapes)
    specs = [SMEM if at in scalars else HBM if at in left else VMEM for at in range(len(args))]
    out_spec = HBM if out_any else VMEM
    return pl.pallas_call(
        ordered,
        out_shape=shapes[0] if single else shapes,
        in_specs=specs + [ANY] * len(after),
        out_specs=out_spec if single else [out_spec] * len(shapes),
        scratch_shapes=list(scratch),
        compiler_params=pltpu.CompilerParams(vmem_limit_bytes=52 * 2**20),
        cost_estimate=pl.CostEstimate(flops=1, bytes_accessed=1, transcendentals=0),
        name=name,
    )(*args, *after)


def flipped(axis, bit):
    count = lax.axis_size(axis)
    return [(at, at ^ (1 << bit)) for at in range(count)]


def on_device(*args):
    a = dict(zip(NAMES, args))
    size = Sizes(a["obs_next"], a["actions"], a["enc_w1"], a["dyn_w1"])
    n_dp, n_pb = lax.axis_size("dp"), lax.axis_size("pb")
    total = size.seqs * n_dp * n_pb
    scale = 1.0 / total
    mlp, cols, seqs, deep = size.mlp, size.cols, size.seqs, size.deep
    dyn_rows = size.dyn_rows(total)
    net_rows = size.net_rows
    joined = size.lat + size.act

    def swap_core(block):
        return lax.ppermute(block, "dp", flipped("dp", 0))

    def swap_x(block):
        return lax.ppermute(block, "dp", flipped("dp", 1))

    def swap_y(block):
        return lax.ppermute(block, "pb", flipped("pb", 0))

    def swap_xy(block):
        route = []
        for dp in range(n_dp):
            for pb in range(n_pb):
                route.append((dp * n_pb + pb, (dp ^ 2) * n_pb + (pb ^ 1)))
        return lax.ppermute(block, ("dp", "pb"), route)

    def shape(rows, width, kind=f32):
        return pltpu.VMEM((rows, width), kind)

    q = [a[n] for n in NAMES[26:]]
    ready = call(ready_kernel, "ready", (8, LANES), [])
    packed = call(
        pack_kernel,
        "pack",
        (net_rows // 2, mlp),
        q,
        scratch=[
            pltpu.VMEM((5, 1, mlp), f32),
            shape(8, mlp),
            pltpu.SemaphoreType.DMA((8,)),
        ],
        scalars=(7,),
        left=(0, 1, 2, 3, 4, 5, 6),
        after=[ready],
        out_any=True,
    )
    packed_y = swap_y(packed)

    joint, reward_grads, reward_state, consist, dyn_h1, dyn_h2, pol_h1, pol_h2, enc_h = call(
        functools.partial(rollout_kernel, size, scale),
        "rollout",
        [
            (deep, 3 * cols),
            (net_rows, mlp),
            (deep, cols),
            (size.lat_deep, cols),
            (mlp, cols),
            (mlp, cols),
            (mlp, cols),
            (mlp, cols),
            (size.hidden, seqs),
        ],
        [a[n].T if n in TURNED else a[n] for n in NAMES[:26]],
        scratch=[
            shape(size.obs_deep, cols + seqs),
            shape(deep, mlp),
            shape(size.lat_deep, mlp),
            shape(size.act_deep, mlp),
            shape(size.obs_deep, size.hidden),
            shape(size.lat_deep, size.hidden),
        ],
        scalars=(19,),
        flops=12 * 6 * mlp * mlp * cols,
    )

    packed_y, joint = lax.optimization_barrier((packed_y, joint))
    packed_c = swap_core(packed_y)

    eighth = net_rows // 8
    rows = 3 * eighth
    *parts, value_state, chosen_grad, prio = call(
        functools.partial(value_kernel, size, scale),
        "value",
        [(rows, mlp)] * 8 + [(deep, cols), (deep, cols), (1, seqs)],
        [joint, a["rewards"], reward_grads] + q + [packed_y, packed_c],
        scratch=[
            shape(net_rows, mlp),
            shape(deep, mlp),
            pltpu.VMEM((TWIN, 3 * deep, mlp), bf16),
            pltpu.VMEM((TWIN, deep, 3 * mlp), bf16),
            pltpu.VMEM((TWIN, 3 * mlp, mlp), bf16),
            pltpu.VMEM((TWIN, mlp, 3 * mlp), bf16),
            pltpu.VMEM((TWIN, mlp, 4 * LANES), f32),
            pltpu.VMEM((TWIN, 1, LANES), f32),
            shape(3 * deep, 3 * cols, bf16),
            pltpu.VMEM((TWIN, 1, cols), f32),
            shape(1, cols),
            pltpu.VMEM((TWIN, net_rows, mlp), f32),
            shape(mlp, 2 * cols),
            shape(mlp, 2 * cols),
            shape(mlp, 2 * cols),
            shape(3 * mlp, 2 * cols, bf16),
            shape(3 * mlp, 2 * cols, bf16),
            shape(mlp, 4 * LANES),
        ],
        scalars=(10,),
        flops=24 * 6 * mlp * mlp * cols,
    )

    def to_square(block):
        return [swap_x(block[0]), swap_y(block[1]), swap_xy(block[2])]

    def along_z(blocks):
        return [
            lax.ppermute(block, "dp", [(at, at ^ (relative << 2)) for at in range(n_dp)])
            for relative, block in zip((1, 2, 3), blocks)
        ]

    def swapped(parts):
        return parts[:4] + [swap_core(part) for part in parts[4:]]

    def halve(name, parts, after=()):
        own, to_y, to_x, to_xy = call(
            halve_kernel, name, [parts[0].shape] * 4, parts, after=after
        )
        return [own] + to_square((to_x, to_y, to_xy))

    def quarter(name, parts, after=()):
        rows = parts[0].shape[0]
        parts = call(
            quarter_kernel,
            name,
            [(rows, LANES)] * 4,
            parts,
            scratch=[shape(rows, mlp)],
            after=after,
        )
        return [parts[0]] + along_z(parts[1:])

    def across_z(name, parts, after=()):
        whole = call(sum_kernel, name, parts[0].shape, parts, after=after)
        for bit in range(4, n_dp.bit_length() - 1):
            come = lax.ppermute(whole, "dp", flipped("dp", bit))
            whole = call(sum_kernel, name, whole.shape, [whole, come])
        return [whole] + along_z([whole] * 3)

    def rejoin(name, parts, head, after=()):
        rows = parts[0].shape[0]
        outs = [(rows, mlp)] + ([(head, mlp)] if head < rows else [])
        outs = call(gather_kernel, name, outs, parts, after=after)
        return [outs[0]] + to_square([outs[0], outs[-1], outs[-1]])

    def both_cores(parts):
        return parts + [swap_core(part) for part in parts]

    parts = swapped(parts)
    pol = call(
        functools.partial(policy_kernel, size),
        "policy",
        (net_rows, mlp),
        [a["pol_w2"], a["pol_w3"].T, joint, pol_h1, pol_h2, chosen_grad],
        scratch=[shape(size.act_deep, mlp), shape(size.act_deep, cols)],
        flops=3 * 6 * mlp * mlp * cols,
    )
    value_rows, shared_rows = rows, eighth + dyn_rows // 8
    value = halve("value_halve", parts, after=[pol])

    *parts, obs_grad = call(
        functools.partial(shared_kernel, size, scale, total),
        "shared",
        [(shared_rows, mlp)] * 8 + [(size.obs, seqs)],
        [
            a["obs_first"],
            a["enc_w1"],
            a["enc_w2"].T,
            a["dyn_w1"],
            a["dyn_w2"],
            a["dyn_w3"].T,
            joint,
            reward_state,
            consist,
            dyn_h1,
            dyn_h2,
            enc_h,
            value_state,
            prio,
            pol,
        ],
        scratch=[
            shape(size.obs_deep, seqs),
            shape(size.lat_deep, mlp),
            shape(size.lat_deep, size.hidden),
            shape(size.lat_deep, cols),
            shape(mlp, cols, bf16),
            shape(mlp, cols, bf16),
            shape(mlp, cols, bf16),
            shape(mlp, cols, bf16),
            shape(dyn_rows, mlp),
        ],
        after=[value[0]],
        flops=10 * 6 * mlp * mlp * cols,
    )
    parts[4:], value[1:] = lax.optimization_barrier((parts[4:], value[1:]))
    parts = swapped(parts)
    value = quarter("value_quarter", value, after=[obs_grad])
    shared = halve("shared_halve", parts, after=[value[0]])
    value = across_z("value_across", value, after=[shared[0]])
    shared = quarter("shared_quarter", shared, after=[value[0]])
    value = rejoin("value_rejoin", value, eighth, after=[shared[0]])
    shared = across_z("shared_across", shared, after=[value[0]])
    shared = rejoin("shared_rejoin", shared, shared_rows)
    value = both_cores(value)
    value_grads = call(
        functools.partial(finish_value_kernel, size),
        "finish_value",
        [a[n].shape for n in NAMES[14:20]] + [a[n].shape for n in NAMES[26:]],
        value,
        scratch=[shape(net_rows, mlp), shape(net_rows, mlp)],
        after=[shared[0]],
    )
    shared = both_cores(shared)
    names = NAMES[4:14] + NAMES[20:26]
    shared_grads = call(
        functools.partial(finish_shared_kernel, size),
        "finish_shared",
        [a[n].shape[::-1] if n in TURNED else a[n].shape for n in names] + [(size.prio_rows, mlp)],
        shared,
        scratch=[shape(net_rows, mlp), shape(dyn_rows, mlp)],
        after=[value_grads[0]],
    )
    shared_grads = list(shared_grads)
    for at, n in enumerate(names):
        if n in TURNED:
            shared_grads[at] = shared_grads[at].T
    priorities = shared_grads[-1].reshape(-1)[:total]
    return (
        tuple(shared_grads[:10])
        + tuple(value_grads[:6])
        + tuple(shared_grads[10:16])
        + tuple(value_grads[6:])
        + (obs_grad, priorities)
    )


def solution(mesh):
    whole = P()
    seqs = ("dp", "pb")
    twin = (P("pb", None, None),) + (P("pb", None),) * 3 + (P("pb", None, None),)
    twin = twin + (P("pb", None), P("pb", None), P("pb"))
    placed = (P(None, seqs), P(None, None, seqs), P(None, None, seqs), P(None, seqs))
    return jax.shard_map(
        on_device,
        mesh=mesh,
        in_specs=placed + (whole,) * 22 + twin,
        out_specs=(whole,) * 22 + twin + (P(None, seqs), whole),
        check_vma=False,
    )
```

```python
import functools

import jax
import jax.numpy as jnp
from jax import lax
from jax.experimental import pallas as pl
from jax.experimental.pallas import tpu as pltpu
from jax.sharding import PartitionSpec as P

f32 = jnp.float32
bf16 = jnp.bfloat16

TWIN = 2
LANES = 128
decay_rate = 0.5
discount = 0.99
consist_coef = 2.0
reward_coef = 0.5
value_coef = 0.1
policy_coef = 0.1
norm_epsilon = 1e-05

TURNED = ("enc_w2", "dyn_w3", "pol_w3")
NN = ((1,), (0,))
NT = ((1,), (1,))
TN = ((0,), (0,))

NAMES = (
    "obs_first",
    "obs_next",
    "actions",
    "rewards",
    "enc_w1",
    "enc_b1",
    "enc_w2",
    "enc_b2",
    "dyn_w1",
    "dyn_b1",
    "dyn_w2",
    "dyn_b2",
    "dyn_w3",
    "dyn_b3",
    "rew_w1",
    "rew_b1",
    "rew_w2",
    "rew_b2",
    "rew_w3",
    "rew_b3",
    "pol_w1",
    "pol_b1",
    "pol_w2",
    "pol_b2",
    "pol_w3",
    "pol_b3",
    "q_w1",
    "q_b1",
    "q_gain",
    "q_shift",
    "q_w2",
    "q_b2",
    "q_w3",
    "q_b3",
)


def up(number, multiple):
    return -(-number // multiple) * multiple


def mm(left, right, dims):
    return lax.dot_general(left, right, (dims, ((), ())), preferred_element_type=f32)


def split(value):
    high = value.astype(bf16)
    return high, (value - high.astype(f32)).astype(bf16)


def dot3(left, right, dims):
    return (
        mm(left[0], right[0], dims) + mm(left[0], right[1], dims) + mm(left[1], right[0], dims)
    )


def dot3_narrow(left, right, dims):
    width = right[0].shape[1]
    both = mm(left[0], jnp.concatenate(right, axis=1), dims)
    return both[:, :width] + both[:, width:] + mm(left[1], right[0], dims)


def dot3_short(left, right, dims):
    rows = left[0].shape[0]
    both = mm(jnp.concatenate(left, axis=0), right[0], dims)
    return both[:rows] + both[rows:] + mm(left[0], right[1], dims)


def stack_weight(parts):
    return jnp.concatenate([parts[0], parts[0], parts[1]], axis=0)


def stack_input(parts):
    return jnp.concatenate([parts[0], parts[1], parts[0]], axis=0)


def elu(value):
    return jnp.where(value > 0, value, jnp.exp(jnp.minimum(value, 0.0)) - 1.0)


def elu_slope(result):
    return jnp.where(result > 0, 1.0, result + 1.0)


def fold(value):
    total = value[:, :LANES]
    for at in range(LANES, value.shape[1], LANES):
        total = total + value[:, at : at + LANES]
    return total


def spread_lanes(column, width):
    return jnp.concatenate([column] * (width // LANES), axis=1)


def columns_of(rows):
    count = len(rows)
    deep = up(3 * count, 16)
    value = jnp.concatenate(rows, axis=0)
    first = value.astype(bf16)
    rest = value - first.astype(f32)
    second = rest.astype(bf16)
    third = (rest - second.astype(f32)).astype(bf16)
    parts = [first.astype(f32), second.astype(f32), third.astype(f32)]
    if deep > 3 * count:
        parts.append(jnp.zeros((deep - 3 * count, value.shape[1]), f32))
    stacked = jnp.concatenate(parts, axis=0).astype(bf16)
    at = lax.broadcasted_iota(jnp.int32, (deep, count * LANES), 0)
    lane = lax.broadcasted_iota(jnp.int32, (deep, count * LANES), 1)
    block = lane // LANES
    pick = ((at == block) | (at == block + count) | (at == block + 2 * count)) & (at < 3 * count)
    return mm(stacked, pick.astype(f32).astype(bf16), TN)


def rows_of(blocks):
    count = len(blocks)
    high, low = split(jnp.concatenate(blocks, axis=1))
    at = lax.broadcasted_iota(jnp.int32, (16, count * LANES), 0)
    lane = lax.broadcasted_iota(jnp.int32, (16, count * LANES), 1)
    pick = (lane // LANES == at).astype(f32).astype(bf16)
    return mm(pick, high, NT) + mm(pick, low, NT)


def decay_row(horizon, width, factor):
    return jnp.concatenate(
        [jnp.full((1, width), factor * decay_rate**step, f32) for step in range(horizon)], axis=1
    )


def first_lane(total, width):
    lane = lax.broadcasted_iota(jnp.int32, (1, width), 1)
    return jnp.where(lane == 0, total, 0.0)


def row(ref):
    return ref[...].reshape(1, ref.shape[-1])


class Sizes:
    def __init__(self, obs_next, actions, enc_w1, dyn_w1):
        self.horizon, self.obs, self.seqs = obs_next.shape
        self.act = actions.shape[1]
        self.hidden = enc_w1.shape[1]
        joined, self.mlp = dyn_w1.shape
        self.lat = joined - self.act
        self.one = joined
        self.deep = up(joined + 1, 16)
        self.obs_deep = up(self.obs + 1, 16)
        self.lat_deep = up(self.lat, 16)
        self.act_deep = up(self.act, 16)
        self.cols = self.horizon * self.seqs
        self.net_rows = self.mlp + self.deep
        self.at_w3 = self.net_rows
        self.at_enc = self.at_w3 + up(self.lat, 8)
        self.at_prio = self.at_enc + up(max(self.lat, self.obs_deep + 1), 16)

    def dyn_rows(self, total):
        self.prio_rows = up(-(-total // self.mlp), 8)
        return up(self.at_prio + self.prio_rows, 64)


def places():
    dp = lax.axis_index("dp")
    pb = lax.axis_index("pb")
    core = lax.rem(dp, 2)
    side = lax.rem(lax.div(dp, 2), 2)
    return dp, pb, core, side


def square(relative):
    dp, pb, core, side = places()
    return lax.rem(side + relative // 2, 2) * 2 + lax.rem(pb + relative % 2, 2)


def pack_kernel(w1, b1, gain, shift, w2, b2, w3, b3, out):
    mlp = w2.shape[1]
    joined = w1.shape[1]
    half = out.shape[0]
    core = places()[2]

    @pl.when(core == 0)
    def _():
        out[...] = w2[0, :half]

    @pl.when(core == 1)
    def _():
        at = mlp - half
        out[:at] = w2[0, half:]
        out[at : at + joined] = w1[0]
        at = at + joined
        out[at:] = jnp.zeros((half - at, mlp), f32)
        for ref in (b1, gain, shift, b2, w3):
            out[at : at + 1] = ref[...]
            at = at + 1
        out[at : at + 1] = jnp.full((1, mlp), b3[0], f32)


def rollout_kernel(
    size,
    scale,
    obs_first,
    obs_next,
    actions,
    rewards,
    enc_w1,
    enc_b1,
    enc_w2,
    enc_b2,
    dyn_w1,
    dyn_b1,
    dyn_w2,
    dyn_b2,
    dyn_w3,
    dyn_b3,
    rew_w1,
    rew_b1,
    rew_w2,
    rew_b2,
    rew_w3,
    rew_b3,
    joint,
    keep0,
    keep1,
    keep2,
    keep3,
    send0,
    send1,
    send2,
    send3,
    state_grad,
    consist,
    dyn_h1,
    dyn_h2,
    enc_h,
    obs_aug,
    w_aug,
    w_out,
    e_aug,
    e_out,
    reward_grads,
    dyn_square,
    rew_square,
    sems,
):
    lat, act, one, deep = size.lat, size.act, size.one, size.deep
    mlp, seqs, cols, horizon = size.mlp, size.seqs, size.cols, size.horizon
    joined = lat + act
    dp, pb, core, side = places()
    fetch = [
        pltpu.make_async_copy(dyn_w2, dyn_square, sems.at[0]),
        pltpu.make_async_copy(rew_w2, rew_square, sems.at[1]),
    ]
    for copy in fetch:
        copy.start()

    def first_weight(ref, bias, kept):
        w_aug[...] = jnp.zeros_like(w_aug)
        w_aug[:kept] = ref[...]
        w_aug[one : one + 1] = row(bias)
        return split(w_aug[...])

    obs_aug[...] = jnp.zeros_like(obs_aug)
    for step in range(horizon):
        obs_aug[: size.obs, step * seqs : (step + 1) * seqs] = obs_next[step]
    obs_aug[: size.obs, cols:] = obs_first[...]
    obs_aug[size.obs : size.obs + 1] = jnp.ones((1, cols + seqs), f32)
    e_aug[...] = jnp.zeros_like(e_aug)
    e_aug[: size.obs] = enc_w1[...]
    e_aug[size.obs : size.obs + 1] = row(enc_b1)
    e_out[...] = jnp.zeros_like(e_out)
    e_out[:lat] = enc_w2[...]
    w_out[...] = jnp.zeros_like(w_out)
    w_out[:lat] = dyn_w3[...]
    small = jnp.concatenate(
        [
            jnp.concatenate([row(enc_b2), jnp.zeros((1, LANES - lat), f32)], axis=1),
            jnp.concatenate([row(dyn_b3), jnp.zeros((1, LANES - lat), f32)], axis=1),
        ],
        axis=0,
    )
    small = columns_of([small[0:1], small[1:2]])
    enc_b2_col = small[: size.lat_deep, :LANES]
    dyn_b3_col = small[: size.lat_deep, LANES:]
    wide = columns_of([row(dyn_b2), row(rew_b2), row(rew_w3)])
    dyn_b2_col = wide[:, :LANES]

    enc_first = mm(stack_weight(split(e_aug[...])), stack_input(split(obs_aug[...])), TN)
    enc_hidden = elu(enc_first)
    enc_h[...] = enc_hidden[:, cols:]
    latent = dot3(split(e_out[...]), split(enc_hidden), NN) + spread_lanes(
        enc_b2_col, cols + seqs
    )
    joint[:, :] = jnp.zeros_like(joint)
    joint[: size.lat_deep, 2 * cols :] = latent[:, :cols]
    for step in range(horizon):
        joint[lat : lat + act, step * seqs : (step + 1) * seqs] = actions[step]
    joint[one : one + 1] = jnp.ones((1, 3 * cols), f32)

    first = stack_weight(first_weight(dyn_w1, dyn_b1, joined))
    fetch[0].wait()
    second = split(dyn_square[...].T)
    third = split(w_out[...])
    latent = latent[:, cols:]
    for step in range(horizon):
        here = slice(step * seqs, (step + 1) * seqs)
        joint[:lat, here] = latent[:lat]
        hidden = elu(mm(first, stack_input(split(joint[:, here])), TN))
        dyn_h1[:, here] = hidden
        hidden = elu(dot3_narrow(second, split(hidden), NN) + dyn_b2_col)
        dyn_h2[:, here] = hidden
        latent = dot3_narrow(third, split(hidden), NN) + dyn_b3_col
        after = 2 * cols + step * seqs
        goal = joint[: size.lat_deep, after : after + seqs]
        factor = scale * decay_rate**step * consist_coef * 2.0 / lat
        consist[:, here] = factor * (latent - goal)

    states = split(joint[:, :cols])
    first = first_weight(rew_w1, rew_b1, joined)
    fetch[1].wait()
    second = split(rew_square[...])
    b2_col = spread_lanes(wide[:, LANES : 2 * LANES], cols)
    w3_col = spread_lanes(wide[:, 2 * LANES : 3 * LANES], cols)
    h1 = elu(mm(stack_weight(first), stack_input(states), TN))
    h1_parts = split(h1)
    h2 = elu(dot3(second, h1_parts, TN) + b2_col)
    predicted = jnp.sum(w3_col * h2, axis=0, keepdims=True) + rew_b3[0]
    wanted = jnp.concatenate([rewards[step : step + 1] for step in range(horizon)], axis=1)
    out_grad = decay_row(horizon, seqs, scale * reward_coef * 2.0) * (predicted - wanted)
    h2_grad = w3_col * out_grad * elu_slope(h2)
    h2_parts = split(h2_grad)
    reward_grads[:mlp] = dot3(h1_parts, h2_parts, NT)
    h1_grad = dot3(second, h2_parts, NN) * elu_slope(h1)
    h1_grad = split(h1_grad)
    reward_grads[mlp:] = dot3(states, h1_grad, NT)
    state_grad[...] = dot3_short(first, h1_grad, NN)
    sums = rows_of([fold(h2_grad), fold(h2 * out_grad)])
    reward_grads[mlp + one + 1 : mlp + one + 3] = sums[:2]
    reward_grads[mlp + one + 3 : mlp + one + 4] = first_lane(jnp.sum(out_grad), mlp)

    eighth = size.net_rows // 8
    for h in range(2):
        place = core if h == 0 else 1 - core
        for k in range(4):
            out = ((keep0, keep1, keep2, keep3), (send0, send1, send2, send3))[h][k]
            start = (place * 4 + square(k)) * eighth
            out[...] = reward_grads[pl.ds(pl.multiple_of(start, 8), eighth)]


def act_kernel(
    size,
    begun,
    pol_w1,
    pol_b1,
    pol_w2,
    pol_b2,
    pol_w3,
    pol_b3,
    joint,
    pol_h1,
    pol_h2,
    w_aug,
    w_act,
):
    lat, act, one = size.lat, size.act, size.one
    cols = size.cols
    joined = lat + act
    joint[...] = begun[...]
    w_act[...] = jnp.zeros_like(w_act)
    w_act[:act] = pol_w3[...]
    small = jnp.concatenate([row(pol_b3), jnp.zeros((1, LANES - act), f32)], axis=1)
    pol_b3_col = columns_of([small])[: size.act_deep]
    b2_col = spread_lanes(columns_of([row(pol_b2)]), cols)
    w_aug[...] = jnp.zeros_like(w_aug)
    w_aug[:lat] = pol_w1[...]
    w_aug[one : one + 1] = row(pol_b1)
    first = stack_weight(split(w_aug[...]))
    second = split(pol_w2[...])
    third = split(w_act[...])
    for block in (0, 2):
        here = slice(block * cols, (block + 1) * cols)
        h1 = elu(mm(first, stack_input(split(joint[:, here])), TN))
        h2 = elu(dot3(second, split(h1), TN) + b2_col)
        action = jnp.tanh(dot3(third, split(h2), NN) + spread_lanes(pol_b3_col, cols))[:act]
        if block == 0:
            pol_h1[...] = h1
            pol_h2[...] = h2
            joint[:lat, cols : 2 * cols] = joint[:lat, :cols]
            joint[lat:joined, cols : 2 * cols] = action
        else:
            joint[lat:joined, here] = action


def value_kernel(
    size,
    scale,
    joint,
    rewards,
    q_w1,
    q_b1,
    q_gain,
    q_shift,
    q_w2,
    q_b2,
    q_w3,
    q_b3,
    packed_y,
    packed_c,
    keep0,
    keep1,
    keep2,
    keep3,
    send0,
    send1,
    send2,
    send3,
    state_grad,
    chosen_grad,
    prio,
    packed,
    aug,
    w1_rows,
    w1_parts,
    w2_rows,
    w2_lanes,
    vectors,
    last,
    inputs,
    next_value,
    spread,
    grads,
    work,
    normed,
    second,
    hidden,
    backs,
    sums,
):
    lat, act, one, deep = size.lat, size.act, size.one, size.deep
    mlp, seqs, cols, horizon = size.mlp, size.seqs, size.cols, size.horizon
    joined = lat + act
    dp, pb, core, side = places()
    half = packed_y.shape[0]
    packed[pl.ds(pl.multiple_of(core * half, 8), half)] = packed_y[...]
    packed[pl.ds(pl.multiple_of((1 - core) * half, 8), half)] = packed_c[...]

    at = mlp + joined
    for slot in range(TWIN):
        if slot == 0:
            w1, b1, w2 = q_w1[0], q_b1[...], q_w2[0]
            rows = [q_gain[...], q_shift[...], q_b2[...], q_w3[...]]
            b3 = jnp.full((1, LANES), q_b3[0], f32)
        else:
            w1, b1, w2 = packed[mlp:at], packed[at : at + 1], packed[:mlp]
            rows = [packed[at + i : at + i + 1] for i in (1, 2, 3, 4)]
            b3 = packed[at + 5 : at + 6, :LANES]
        aug[...] = jnp.zeros_like(aug)
        aug[:joined] = w1
        aug[one : one + 1] = b1
        high, low = split(aug[...])
        for place, part in enumerate((high, high, low)):
            w1_rows[slot, place * deep : (place + 1) * deep] = part
            if place > 0:
                w1_parts[slot, (place - 1) * deep : place * deep] = part
        high, low = split(w2)
        for place, part in enumerate((high, high, low)):
            w2_rows[slot, place * mlp : (place + 1) * mlp] = part
            w2_lanes[slot, :, place * mlp : (place + 1) * mlp] = part
        vectors[slot] = columns_of(rows)
        last[slot] = b3
    inputs[...] = stack_input(split(joint[...]))

    height = 32

    def blocks(width):
        for left in range(0, width, cols):
            for top in range(0, mlp, height):
                yield slice(top, top + height), slice(left, left + cols)

    def column(slot, which, rows):
        return spread_lanes(vectors[slot, rows, which * LANES : (which + 1) * LANES], cols)

    def keep_parts(ref, rows, here, value):
        high, low = split(value)
        for place, part in enumerate((high, low, high)):
            ref[rows.start + place * mlp : rows.stop + place * mlp, here] = part

    def added(totals, here, value):
        eight = value.reshape(height // 8, 8, cols).sum(axis=0)
        at = here.start // cols
        totals[at] = eight if totals[at] is None else totals[at] + eight

    def total_of(totals):
        return jnp.concatenate([jnp.sum(t, axis=0, keepdims=True) for t in totals], axis=1)

    def forward(slot, start, width, kept):
        work[:, :width] = mm(w1_rows[slot], inputs[:, start : start + width], TN)
        totals = [None] * (width // cols)
        for rows, here in blocks(width):
            added(totals, here, work[rows, here])
        mean = total_of(totals) / mlp
        totals = [None] * (width // cols)
        for rows, here in blocks(width):
            center = work[rows, here] - mean[:, here]
            added(totals, here, center * center)
        inverse = lax.rsqrt(total_of(totals) / mlp + norm_epsilon)
        for rows, here in blocks(width):
            value = (work[rows, here] - mean[:, here]) * inverse[:, here]
            if kept:
                normed[rows, here] = value
            value = jnp.tanh(column(slot, 0, rows) * value + column(slot, 1, rows))
            keep_parts(hidden, rows, here, value)
        work[:, :width] = mm(w2_rows[slot], hidden[:, :width], TN)
        totals = [None] * (width // cols)
        for rows, here in blocks(width):
            value = elu(work[rows, here] + column(slot, 2, rows))
            if kept:
                second[rows, here] = value
            if here.start == 0:
                added(totals, here, column(slot, 3, rows) * value)
        return total_of(totals[:1]) + spread_lanes(last[slot], cols), inverse

    @pl.loop(0, TWIN)
    def _(slot):
        next_value[slot] = forward(slot, 2 * cols, cols, False)[0]

    wanted = jnp.concatenate([rewards[step : step + 1] for step in range(horizon)], axis=1)
    next_value[0] = wanted + discount * jnp.minimum(next_value[0], next_value[1])
    spread[...] = jnp.zeros_like(spread)
    state_grad[...] = jnp.zeros_like(state_grad)
    chosen_grad[...] = jnp.zeros_like(chosen_grad)

    @pl.loop(0, TWIN)
    def _(slot):
        value, inverse = forward(slot, 0, 2 * cols, True)
        error = value - next_value[0]
        spread[...] += jnp.sqrt(error * error + 1.0)
        out_grad = jnp.concatenate(
            [
                decay_row(horizon, seqs, scale * value_coef * 2.0) * error,
                decay_row(horizon, seqs, -policy_coef * 0.5 * scale),
            ],
            axis=1,
        )
        for rows, here in blocks(2 * cols):
            result = second[rows, here]
            back = column(slot, 3, rows) * out_grad[:, here] * elu_slope(result)
            keep_parts(backs, rows, here, back)
            if here.start == 0:
                sums[rows, :LANES] = fold(back)
                sums[rows, 3 * LANES :] = fold(result * out_grad[:, here])
        work[...] = mm(w2_lanes[slot], backs[...], NN)
        grads[slot, :mlp] = dot3(
            (hidden[:mlp, :cols], hidden[mlp : 2 * mlp, :cols]),
            (backs[:mlp, :cols], backs[mlp : 2 * mlp, :cols]),
            NT,
        )
        plain, along = [None] * 2, [None] * 2
        for rows, here in blocks(2 * cols):
            high = hidden[rows, here].astype(f32)
            low = hidden[mlp + rows.start : mlp + rows.stop, here].astype(f32)
            result = high + low
            pre = work[rows, here] * (1.0 - result * result)
            unit = normed[rows, here]
            if here.start == 0:
                sums[rows, LANES : 2 * LANES] = fold(pre * unit)
                sums[rows, 2 * LANES : 3 * LANES] = fold(pre)
            back = column(slot, 0, rows) * pre
            work[rows, here] = back
            added(plain, here, back)
            added(along, here, back * unit)
        plain, along = total_of(plain) / mlp, total_of(along) / mlp
        for rows, here in blocks(2 * cols):
            back = work[rows, here] - plain[:, here] - normed[rows, here] * along[:, here]
            keep_parts(backs, rows, here, back * inverse[:, here])
        states = (inputs[:deep, :cols], inputs[deep : 2 * deep, :cols])
        first_parts = (backs[:mlp, :cols], backs[mlp : 2 * mlp, :cols])
        grads[slot, mlp:] = dot3(states, first_parts, NT)
        both = mm(w1_parts[slot], backs[:mlp], NN)
        into = both[:deep] + both[deep:] + mm(w1_parts[slot, :deep], backs[mlp : 2 * mlp], NN)
        state_grad[...] += into[:, :cols]
        chosen_grad[...] += into[:, cols:]
        lines = rows_of([sums[:, at * LANES : (at + 1) * LANES] for at in range(4)])
        grads[slot, mlp + one + 1 : mlp + one + 5] = lines[:4]
        grads[slot, mlp + one + 5 : mlp + one + 6] = first_lane(jnp.sum(out_grad[:, :cols]), mlp)

    total = spread[:, :seqs]
    for step in range(1, horizon):
        total = total + spread[:, step * seqs : (step + 1) * seqs]
    prio[...] = total / (TWIN * horizon)

    quarter = size.net_rows // 4
    for h in range(2):
        place = core if h == 0 else 1 - core
        for k in range(4):
            out = ((keep0, keep1, keep2, keep3), (send0, send1, send2, send3))[h][k]
            start = (place * 2 + lax.div(square(k), 2)) * quarter
            out[...] = grads[k % 2, pl.ds(pl.multiple_of(start, 8), quarter)]


def policy_kernel(
    size, pol_w2, pol_w3, joint, pol_h1, pol_h2, chosen_grad, pol, w_act, act_grad
):
    lat, act, one = size.lat, size.act, size.one
    mlp, cols = size.mlp, size.cols
    joined = lat + act
    states = split(joint[:, :cols])
    w_act[...] = jnp.zeros_like(w_act)
    w_act[:act] = pol_w3[...]
    act_grad[...] = jnp.zeros_like(act_grad)
    chosen = joint[lat:joined, cols : 2 * cols]
    act_grad[:act] = chosen_grad[lat:joined] * (1.0 - chosen * chosen)
    out_parts = split(act_grad[...])
    weight = split(w_act[...])
    h2 = pol_h2[...]
    h2_grad = mm(stack_weight(weight), stack_input(out_parts), TN) * elu_slope(h2)
    h2_parts = split(h2_grad)
    h1 = pol_h1[...]
    pol[:mlp] = dot3(split(h1), h2_parts, NT)
    h1_grad = dot3(split(pol_w2[...]), h2_parts, NN) * elu_slope(h1)
    pol[mlp:] = dot3(states, split(h1_grad), NT)
    pol[mlp + lat : mlp + joined] = dot3(out_parts, split(h2), NT)[:act]
    pol[mlp + one + 1 : mlp + one + 2] = rows_of([fold(h2_grad)])[:1]
    sums = rows_of([fold(act_grad[...])])
    pol[mlp + one + 2 : mlp + one + 3] = jnp.zeros((1, mlp), f32)
    pol[mlp + one + 2 : mlp + one + 3, : size.act_deep] = sums[:1]


def shared_kernel(
    size,
    scale,
    total,
    obs_first,
    enc_w1,
    enc_w2,
    dyn_w1,
    dyn_w2,
    dyn_w3,
    joint,
    reward_state,
    consist,
    dyn_h1,
    dyn_h2,
    enc_h,
    value_state,
    prio,
    pol,
    keep0,
    keep1,
    keep2,
    keep3,
    send0,
    send1,
    send2,
    send3,
    obs_grad,
    obs_aug,
    w_out,
    e_out,
    lat_grad,
    second_high,
    second_low,
    first_high,
    first_low,
    dyn,
):
    lat, act, one, deep = size.lat, size.act, size.one, size.deep
    mlp, seqs, cols, horizon = size.mlp, size.seqs, size.cols, size.horizon
    joined = lat + act
    lat_deep, hidden = size.lat_deep, size.hidden
    dp, pb, core, side = places()
    states = split(joint[:, :cols])

    w_out[...] = jnp.zeros_like(w_out)
    w_out[:lat] = dyn_w3[...]
    third = stack_weight(split(w_out[...]))
    second = split(dyn_w2[...])
    first = split(dyn_w1[...])
    lat_rows = lax.broadcasted_iota(jnp.int32, (lat_deep, seqs), 0)
    carry = None
    for step in reversed(range(horizon)):
        here = slice(step * seqs, (step + 1) * seqs)
        grad = consist[:, here]
        if carry is not None:
            after = slice((step + 1) * seqs, (step + 2) * seqs)
            grad = grad + carry + reward_state[:lat_deep, after] + value_state[:lat_deep, after]
            grad = jnp.where(lat_rows < lat, grad, 0.0)
        lat_grad[:, here] = grad
        high, low = split(grad)
        h2_grad = mm(third, jnp.concatenate([high, low, high], axis=0), TN)
        h2_grad = h2_grad * elu_slope(dyn_h2[:, here])
        parts = split(h2_grad)
        second_high[:, here], second_low[:, here] = parts
        h1_grad = dot3_narrow(second, parts, NN) * elu_slope(dyn_h1[:, here])
        parts = split(h1_grad)
        first_high[:, here], first_low[:, here] = parts
        back = dot3_narrow(first, parts, NN)
        carry = jnp.concatenate([back, jnp.zeros((lat_deep - joined, seqs), f32)], axis=0)
    grad = carry + reward_state[:lat_deep, :seqs] + value_state[:lat_deep, :seqs]
    grad = jnp.where(lat_rows < lat, grad, 0.0)
    second_parts = (second_high[...], second_low[...])
    first_parts = (first_high[...], first_low[...])
    dyn[:mlp] = dot3(split(dyn_h1[...]), second_parts, NT)
    dyn[mlp : size.net_rows] = dot3(states, first_parts, NT)
    out_grad = lat_grad[...]
    b2_sum = fold(second_high[...].astype(f32) + second_low[...].astype(f32))
    dyn[size.at_w3 : size.at_enc] = dot3(split(out_grad), split(dyn_h2[...]), NT)[
        : size.at_enc - size.at_w3
    ]
    dyn[mlp + one + 1 : mlp + one + 2] = rows_of([b2_sum])[:1]
    dyn[mlp + one + 2 : mlp + one + 3] = jnp.zeros((1, mlp), f32)
    dyn[mlp + one + 2 : mlp + one + 3, :lat_deep] = rows_of([fold(out_grad)])[:1]

    dyn[size.at_enc :] = jnp.zeros((dyn.shape[0] - size.at_enc, mlp), f32)
    obs_aug[...] = jnp.zeros_like(obs_aug)
    obs_aug[: size.obs] = obs_first[...]
    obs_aug[size.obs : size.obs + 1] = jnp.ones((1, seqs), f32)
    e_out[...] = jnp.zeros_like(e_out)
    e_out[:lat] = enc_w2[...]
    parts = split(grad)
    h = enc_h[...]
    h_grad = dot3(split(e_out[...]), parts, TN) * elu_slope(h)
    h_parts = split(h_grad)
    dyn[size.at_enc : size.at_enc + lat_deep, :hidden] = dot3(parts, split(h), NT)
    dyn[size.at_enc : size.at_enc + size.obs_deep, hidden : 2 * hidden] = dot3(
        split(obs_aug[...]), h_parts, NT
    )
    at = size.at_enc + size.obs_deep
    dyn[at : at + 1, hidden : hidden + lat_deep] = rows_of([grad])[:1]
    obs_grad[...] = total * dot3(split(enc_w1[...]), h_parts, NN)

    index = (dp * 2 + pb) * seqs
    rows = size.prio_rows
    at = lax.broadcasted_iota(jnp.int32, (rows, mlp), 0) * mlp
    at = at + lax.broadcasted_iota(jnp.int32, (rows, mlp), 1)
    mine = (at >= index) & (at < index + seqs)
    value = jnp.concatenate([prio[...]] * (mlp // seqs), axis=1)
    dyn[size.at_prio : size.at_prio + rows] = jnp.where(mine, value, 0.0)

    small, large = size.net_rows // 8, dyn.shape[0] // 8
    for h in range(2):
        place = core if h == 0 else 1 - core
        for k in range(4):
            out = ((keep0, keep1, keep2, keep3), (send0, send1, send2, send3))[h][k]
            start = (place * 4 + square(k)) * small
            out[:small] = pol[pl.ds(pl.multiple_of(start, 8), small)]
            start = (place * 4 + square(k)) * large
            out[small:] = dyn[pl.ds(pl.multiple_of(start, 8), large)]


def halve_kernel(*refs):
    for k in range(4):
        refs[8 + k][...] = refs[k][...] + refs[4 + k][...]


def sum_kernel(*refs):
    total = refs[0][...]
    for ref in refs[1:-1]:
        total = total + ref[...]
    refs[-1][...] = total


def lane_half(other):
    mine = lax.rem(lax.div(lax.axis_index("dp"), 4), 2)
    at = 1 - mine if other else mine
    return pl.ds(pl.multiple_of(at * 256, 256), 256)


def cut_kernel(*refs):
    *summed, own, from_x, from_y, from_xy, mine, other, whole = refs
    at = 0
    for ref in summed:
        whole[at : at + ref.shape[0]] = ref[...]
        at = at + ref.shape[0]
    whole[at:] = (own[...] + from_x[...]) + (from_y[...] + from_xy[...])
    mine[...] = whole[:, lane_half(False)]
    other[...] = whole[:, lane_half(True)]


def rejoin_kernel(mine, other, *outs):
    for out in outs:
        out[:, lane_half(False)] = mine[: out.shape[0]]
        out[:, lane_half(True)] = other[: out.shape[0]]


def collect(out, pieces, first, rows, core, side, pb):
    for h in range(2):
        for k in range(4):
            place = lax.rem(core + h, 2) * 4 + lax.rem(side + k // 2, 2) * 2 + lax.rem(pb + k, 2)
            out[pl.ds(pl.multiple_of(place * rows, 8), rows)] = pieces[h][k][first : first + rows]


def finish_value_kernel(
    size,
    own,
    from_x,
    from_y,
    from_xy,
    c_own,
    c_x,
    c_y,
    c_xy,
    rew_w1,
    rew_b1,
    rew_w2,
    rew_b2,
    rew_w3,
    rew_b3,
    q_w1,
    q_b1,
    q_gain,
    q_shift,
    q_w2,
    q_b2,
    q_w3,
    q_b3,
    rew,
    twin,
):
    dp, pb, core, side = places()
    mlp, one = size.mlp, size.one
    eighth, quarter = size.net_rows // 8, size.net_rows // 4
    pieces = ((own, from_y, from_x, from_xy), (c_own, c_y, c_x, c_xy))
    collect(rew, pieces, 0, eighth, core, side, pb)
    for h in range(2):
        for k in range(2):
            place = lax.rem(core + h, 2) * 2 + lax.rem(side + k, 2)
            twin[pl.ds(pl.multiple_of(place * quarter, 8), quarter)] = pieces[h][2 * k][eighth:]
    rew_w2[...] = rew[:mlp]
    rew_w1[...] = rew[mlp : mlp + one]
    for ref, at in ((rew_b1, 0), (rew_b2, 1), (rew_w3, 2), (rew_b3, 3)):
        n = ref.shape[0]
        ref[...] = rew[mlp + one + at : mlp + one + at + 1, :n].reshape(n)
    q_w2[0] = twin[:mlp]
    q_w1[0] = twin[mlp : mlp + one]
    for at, ref in enumerate((q_b1, q_b2, q_gain, q_shift, q_w3)):
        ref[...] = twin[mlp + one + at : mlp + one + at + 1]
    q_b3[...] = twin[mlp + one + 5 : mlp + one + 6, :1].reshape(1)


def finish_shared_kernel(
    size,
    own,
    from_x,
    from_y,
    from_xy,
    c_own,
    c_x,
    c_y,
    c_xy,
    enc_w1,
    enc_b1,
    enc_w2,
    enc_b2,
    dyn_w1,
    dyn_b1,
    dyn_w2,
    dyn_b2,
    dyn_w3,
    dyn_b3,
    pol_w1,
    pol_b1,
    pol_w2,
    pol_b2,
    pol_w3,
    pol_b3,
    prio,
    pol,
    dyn,
):
    dp, pb, core, side = places()
    mlp, one, lat, act, hidden = size.mlp, size.one, size.lat, size.act, size.hidden
    pieces = ((own, from_y, from_x, from_xy), (c_own, c_y, c_x, c_xy))
    small, large = size.net_rows // 8, dyn.shape[0] // 8
    collect(pol, pieces, 0, small, core, side, pb)
    collect(dyn, pieces, small, large, core, side, pb)

    def line(out, source, at, first=0):
        n = out.shape[0]
        out[...] = source[at : at + 1, first : first + n].reshape(n)

    pol_w2[...] = pol[:mlp]
    pol_w1[...] = pol[mlp : mlp + lat]
    pol_w3[...] = pol[mlp + lat : mlp + lat + act]
    line(pol_b1, pol, mlp + one)
    line(pol_b2, pol, mlp + one + 1)
    line(pol_b3, pol, mlp + one + 2)
    dyn_w2[...] = dyn[:mlp]
    dyn_w1[...] = dyn[mlp : mlp + one]
    dyn_w3[...] = dyn[size.at_w3 : size.at_w3 + lat]
    line(dyn_b1, dyn, mlp + one)
    line(dyn_b2, dyn, mlp + one + 1)
    line(dyn_b3, dyn, mlp + one + 2)
    enc_w2[...] = dyn[size.at_enc : size.at_enc + lat, :hidden]
    enc_w1[...] = dyn[size.at_enc : size.at_enc + size.obs, hidden : 2 * hidden]
    line(enc_b1, dyn, size.at_enc + size.obs, hidden)
    line(enc_b2, dyn, size.at_enc + size.obs_deep, hidden)
    for at in range(prio.shape[0] // mlp):
        line(prio.at[at * mlp : (at + 1) * mlp], dyn, size.at_prio + at)


VMEM = pl.BlockSpec(memory_space=pltpu.VMEM)
SMEM = pl.BlockSpec(memory_space=pltpu.SMEM)


ANY = pl.BlockSpec(memory_space=pl.ANY)


def call(
    kernel, name, outs, args, scratch=(), scalars=(), left=(), after=(), mega=16
):
    def made(shape):
        return jax.ShapeDtypeStruct(shape, f32)

    def ordered(*refs):
        return kernel(*refs[: len(args)], *refs[len(args) + len(after) :])

    single = not isinstance(outs, list)
    shapes = [made(shape) for shape in ([outs] if single else outs)]
    specs = [SMEM if at in scalars else ANY if at in left else VMEM for at in range(len(args))]
    return pl.pallas_call(
        ordered,
        out_shape=shapes[0] if single else shapes,
        in_specs=specs + [ANY] * len(after),
        out_specs=VMEM if single else [VMEM] * len(shapes),
        scratch_shapes=list(scratch),
        compiler_params=pltpu.CompilerParams(vmem_limit_bytes=mega * 2**20),
        cost_estimate=pl.CostEstimate(flops=1, bytes_accessed=1, transcendentals=0),
        name=name,
    )(*args, *after)


def flipped(axis, bit):
    count = lax.axis_size(axis)
    return [(at, at ^ (1 << bit)) for at in range(count)]


def on_device(*args):
    a = dict(zip(NAMES, args))
    size = Sizes(a["obs_next"], a["actions"], a["enc_w1"], a["dyn_w1"])
    n_dp, n_pb = lax.axis_size("dp"), lax.axis_size("pb")
    total = size.seqs * n_dp * n_pb
    scale = 1.0 / total
    mlp, cols, seqs, deep = size.mlp, size.cols, size.seqs, size.deep
    dyn_rows = size.dyn_rows(total)
    net_rows = size.net_rows
    joined = size.lat + size.act

    def swap_core(block):
        return lax.ppermute(block, "dp", flipped("dp", 0))

    def swap_x(block):
        return lax.ppermute(block, "dp", flipped("dp", 1))

    def swap_y(block):
        return lax.ppermute(block, "pb", flipped("pb", 0))

    def swap_xy(block):
        route = []
        for dp in range(n_dp):
            for pb in range(n_pb):
                route.append((dp * n_pb + pb, (dp ^ 2) * n_pb + (pb ^ 1)))
        return lax.ppermute(block, ("dp", "pb"), route)

    def shape(rows, width, kind=f32):
        return pltpu.VMEM((rows, width), kind)

    def to_square(block):
        return [swap_x(block[0]), swap_y(block[1]), swap_xy(block[2])]

    def swap_z(block):
        return lax.ppermute(block, "dp", flipped("dp", 2))

    def swapped(parts):
        return parts[:4] + [swap_core(part) for part in parts[4:]]

    def halve(name, parts, after=()):
        own, to_y, to_x, to_xy = call(
            halve_kernel, name, [parts[0].shape] * 4, parts, after=after
        )
        return [own] + to_square((to_x, to_y, to_xy))

    def cut(name, parts, after=()):
        rows = sum(part.shape[0] for part in parts[:-3])
        mine, other = call(
            cut_kernel,
            name,
            [(rows, mlp // 2)] * 2,
            parts,
            scratch=[shape(rows, mlp)],
            after=after,
        )
        return [mine, swap_z(other)]

    def further_z(name, parts):
        for bit in range(3, n_dp.bit_length() - 1):
            whole = call(sum_kernel, name, parts[0].shape, parts)
            parts = [whole, lax.ppermute(whole, "dp", flipped("dp", bit))]
        return parts

    def back_z(name, parts, after=()):
        whole = call(sum_kernel, name, parts[0].shape, parts, after=after)
        return [whole, swap_z(whole)]

    def rejoin(name, parts, head, after=()):
        rows = parts[0].shape[0]
        outs = [(rows, mlp)] + ([(head, mlp)] if head < rows else [])
        outs = call(rejoin_kernel, name, outs, parts, after=after)
        return [outs[0]] + to_square([outs[0], outs[-1], outs[-1]])

    def both_cores(parts):
        return parts + [swap_core(part) for part in parts]

    q = [a[n] for n in NAMES[26:]]
    packed = call(
        pack_kernel,
        "pack",
        (net_rows // 2, mlp),
        q,
        scalars=(7,),
        mega=63,
    )
    packed_y = swap_y(packed)

    eighth = net_rows // 8
    begun, *reward, reward_state, consist, dyn_h1, dyn_h2, enc_h = call(
        functools.partial(rollout_kernel, size, scale),
        "rollout",
        [(deep, 3 * cols)]
        + [(eighth, mlp)] * 8
        + [(deep, cols), (size.lat_deep, cols), (mlp, cols), (mlp, cols), (size.hidden, seqs)],
        [a[n].T if n in TURNED else a[n] for n in NAMES[:20]],
        scratch=[
            shape(size.obs_deep, cols + seqs),
            shape(deep, mlp),
            shape(size.lat_deep, mlp),
            shape(size.obs_deep, size.hidden),
            shape(size.lat_deep, size.hidden),
            shape(net_rows, mlp),
            shape(mlp, mlp),
            shape(mlp, mlp),
            pltpu.SemaphoreType.DMA((2,)),
        ],
        scalars=(19,),
        left=(10, 16),
        mega=50,
    )
    packed_y, begun = lax.optimization_barrier((packed_y, begun))
    packed_c = swap_core(packed_y)
    reward = swapped(reward)
    joint, pol_h1, pol_h2 = call(
        functools.partial(act_kernel, size),
        "act",
        [(deep, 3 * cols), (mlp, cols), (mlp, cols)],
        [begun] + [a[n].T if n in TURNED else a[n] for n in NAMES[20:26]],
        scratch=[shape(deep, mlp), shape(size.act_deep, mlp)],
        mega=32,
    )
    reward = halve("reward_halve", reward, after=[pol_h1])

    rows = 2 * eighth
    *parts, value_state, chosen_grad, prio = call(
        functools.partial(value_kernel, size, scale),
        "value",
        [(rows, mlp)] * 8 + [(deep, cols), (deep, cols), (1, seqs)],
        [joint, a["rewards"]] + q + [packed_y, packed_c],
        scratch=[
            shape(net_rows, mlp),
            shape(deep, mlp),
            pltpu.VMEM((TWIN, 3 * deep, mlp), bf16),
            pltpu.VMEM((TWIN, 2 * deep, mlp), bf16),
            pltpu.VMEM((TWIN, 3 * mlp, mlp), bf16),
            pltpu.VMEM((TWIN, mlp, 3 * mlp), bf16),
            pltpu.VMEM((TWIN, mlp, 4 * LANES), f32),
            pltpu.VMEM((TWIN, 1, LANES), f32),
            shape(3 * deep, 3 * cols, bf16),
            pltpu.VMEM((TWIN, 1, cols), f32),
            shape(1, cols),
            pltpu.VMEM((TWIN, net_rows, mlp), f32),
            shape(mlp, 2 * cols),
            shape(mlp, 2 * cols),
            shape(mlp, 2 * cols),
            shape(3 * mlp, 2 * cols, bf16),
            shape(3 * mlp, 2 * cols, bf16),
            shape(mlp, 4 * LANES),
        ],
        scalars=(9,),
        after=[reward[0]],
        mega=48,
    )

    reward = call(sum_kernel, "reward_sum", reward[0].shape, reward, after=[prio])
    parts[4:], reward = lax.optimization_barrier((parts[4:], reward))
    parts = swapped(parts)
    pol = call(
        functools.partial(policy_kernel, size),
        "policy",
        (net_rows, mlp),
        [a["pol_w2"], a["pol_w3"].T, joint, pol_h1, pol_h2, chosen_grad],
        after=[reward],
        scratch=[shape(size.act_deep, mlp), shape(size.act_deep, cols)],
        mega=32,
    )
    value_rows, shared_rows = rows, eighth + dyn_rows // 8
    value = halve("value_halve", parts, after=[pol])

    *parts, obs_grad = call(
        functools.partial(shared_kernel, size, scale, total),
        "shared",
        [(shared_rows, mlp)] * 8 + [(size.obs, seqs)],
        [
            a["obs_first"],
            a["enc_w1"],
            a["enc_w2"].T,
            a["dyn_w1"],
            a["dyn_w2"],
            a["dyn_w3"].T,
            joint,
            reward_state,
            consist,
            dyn_h1,
            dyn_h2,
            enc_h,
            value_state,
            prio,
            pol,
        ],
        scratch=[
            shape(size.obs_deep, seqs),
            shape(size.lat_deep, mlp),
            shape(size.lat_deep, size.hidden),
            shape(size.lat_deep, cols),
            shape(mlp, cols, bf16),
            shape(mlp, cols, bf16),
            shape(mlp, cols, bf16),
            shape(mlp, cols, bf16),
            shape(dyn_rows, mlp),
        ],
        after=[value[0]],
        mega=32,
    )
    parts = swapped(parts)
    value = cut("value_cut", [reward] + value, after=[obs_grad])
    shared = halve("shared_halve", parts, after=[value[0]])
    value = further_z("value_further", value)
    shared = cut("shared_cut", shared)
    value = back_z("value_back", value, after=[shared[0]])
    shared = further_z("shared_further", shared)
    value = rejoin("value_rejoin", value, eighth, after=[shared[0]])
    shared = back_z("shared_back", shared)
    shared = rejoin("shared_rejoin", shared, shared_rows, after=[value[0]])
    value = both_cores(value)
    value_grads = call(
        functools.partial(finish_value_kernel, size),
        "finish_value",
        [a[n].shape for n in NAMES[14:20]] + [a[n].shape for n in NAMES[26:]],
        value,
        scratch=[shape(net_rows, mlp), shape(net_rows, mlp)],
        after=[shared[0]],
    )
    shared, value_grads = lax.optimization_barrier((shared, value_grads))
    shared = both_cores(shared)
    names = NAMES[4:14] + NAMES[20:26]
    shared_grads = call(
        functools.partial(finish_shared_kernel, size),
        "finish_shared",
        [a[n].shape[::-1] if n in TURNED else a[n].shape for n in names] + [(total,)],
        shared,
        scratch=[shape(net_rows, mlp), shape(dyn_rows, mlp)],
    )
    shared_grads = list(shared_grads)
    for at, n in enumerate(names):
        if n in TURNED:
            shared_grads[at] = shared_grads[at].T
    return (
        tuple(shared_grads[:10])
        + tuple(value_grads[:6])
        + tuple(shared_grads[10:16])
        + tuple(value_grads[6:])
        + (obs_grad, shared_grads[-1])
    )


def solution(mesh):
    whole = P()
    seqs = ("dp", "pb")
    twin = (P("pb", None, None),) + (P("pb", None),) * 3 + (P("pb", None, None),)
    twin = twin + (P("pb", None), P("pb", None), P("pb"))
    placed = (P(None, seqs), P(None, None, seqs), P(None, None, seqs), P(None, seqs))
    return jax.shard_map(
        on_device,
        mesh=mesh,
        in_specs=placed + (whole,) * 22 + twin,
        out_specs=(whole,) * 22 + twin + (P(None, seqs), whole),
        check_vma=False,
    )
```

```python
import functools

import jax
import jax.numpy as jnp
from jax import lax
from jax.experimental import pallas as pl
from jax.experimental.pallas import tpu as pltpu
from jax.sharding import PartitionSpec as P

f32 = jnp.float32
bf16 = jnp.bfloat16

TWIN = 2
LANES = 128
decay_rate = 0.5
discount = 0.99
consist_coef = 2.0
reward_coef = 0.5
value_coef = 0.1
policy_coef = 0.1
norm_epsilon = 1e-05

TURNED = ("enc_w2", "dyn_w3", "pol_w3")
NN = ((1,), (0,))
NT = ((1,), (1,))
TN = ((0,), (0,))

NAMES = (
    "obs_first",
    "obs_next",
    "actions",
    "rewards",
    "enc_w1",
    "enc_b1",
    "enc_w2",
    "enc_b2",
    "dyn_w1",
    "dyn_b1",
    "dyn_w2",
    "dyn_b2",
    "dyn_w3",
    "dyn_b3",
    "rew_w1",
    "rew_b1",
    "rew_w2",
    "rew_b2",
    "rew_w3",
    "rew_b3",
    "pol_w1",
    "pol_b1",
    "pol_w2",
    "pol_b2",
    "pol_w3",
    "pol_b3",
    "q_w1",
    "q_b1",
    "q_gain",
    "q_shift",
    "q_w2",
    "q_b2",
    "q_w3",
    "q_b3",
)


def up(number, multiple):
    return -(-number // multiple) * multiple


def mm(left, right, dims):
    return lax.dot_general(left, right, (dims, ((), ())), preferred_element_type=f32)


def split(value):
    high = value.astype(bf16)
    return high, (value - high.astype(f32)).astype(bf16)


def dot3(left, right, dims):
    return (
        mm(left[0], right[0], dims) + mm(left[0], right[1], dims) + mm(left[1], right[0], dims)
    )


def dot3_narrow(left, right, dims):
    width = right[0].shape[1]
    both = mm(left[0], jnp.concatenate(right, axis=1), dims)
    return both[:, :width] + both[:, width:] + mm(left[1], right[0], dims)


def dot3_short(left, right, dims):
    rows = left[0].shape[0]
    both = mm(jnp.concatenate(left, axis=0), right[0], dims)
    return both[:rows] + both[rows:] + mm(left[0], right[1], dims)


def stack_weight(parts):
    return jnp.concatenate([parts[0], parts[0], parts[1]], axis=0)


def stack_input(parts):
    return jnp.concatenate([parts[0], parts[1], parts[0]], axis=0)


def elu(value):
    return jnp.where(value > 0, value, jnp.exp(jnp.minimum(value, 0.0)) - 1.0)


def elu_slope(result):
    return jnp.where(result > 0, 1.0, result + 1.0)


def fold(value):
    total = value[:, :LANES]
    for at in range(LANES, value.shape[1], LANES):
        total = total + value[:, at : at + LANES]
    return total


def spread_lanes(column, width):
    return jnp.concatenate([column] * (width // LANES), axis=1)


def columns_of(rows):
    count = len(rows)
    deep = up(3 * count, 16)
    value = jnp.concatenate(rows, axis=0)
    first = value.astype(bf16)
    rest = value - first.astype(f32)
    second = rest.astype(bf16)
    third = (rest - second.astype(f32)).astype(bf16)
    parts = [first.astype(f32), second.astype(f32), third.astype(f32)]
    if deep > 3 * count:
        parts.append(jnp.zeros((deep - 3 * count, value.shape[1]), f32))
    stacked = jnp.concatenate(parts, axis=0).astype(bf16)
    at = lax.broadcasted_iota(jnp.int32, (deep, count * LANES), 0)
    lane = lax.broadcasted_iota(jnp.int32, (deep, count * LANES), 1)
    block = lane // LANES
    pick = ((at == block) | (at == block + count) | (at == block + 2 * count)) & (at < 3 * count)
    return mm(stacked, pick.astype(f32).astype(bf16), TN)


def rows_of(blocks):
    count = len(blocks)
    high, low = split(jnp.concatenate(blocks, axis=1))
    at = lax.broadcasted_iota(jnp.int32, (16, count * LANES), 0)
    lane = lax.broadcasted_iota(jnp.int32, (16, count * LANES), 1)
    pick = (lane // LANES == at).astype(f32).astype(bf16)
    return mm(pick, high, NT) + mm(pick, low, NT)


def decay_row(horizon, width, factor):
    return jnp.concatenate(
        [jnp.full((1, width), factor * decay_rate**step, f32) for step in range(horizon)], axis=1
    )


def first_lane(total, width):
    lane = lax.broadcasted_iota(jnp.int32, (1, width), 1)
    return jnp.where(lane == 0, total, 0.0)


def row(ref):
    return ref[...].reshape(1, ref.shape[-1])


class Sizes:
    def __init__(self, obs_next, actions, enc_w1, dyn_w1):
        self.horizon, self.obs, self.seqs = obs_next.shape
        self.act = actions.shape[1]
        self.hidden = enc_w1.shape[1]
        joined, self.mlp = dyn_w1.shape
        self.lat = joined - self.act
        self.one = joined
        self.deep = up(joined + 1, 16)
        self.obs_deep = up(self.obs + 1, 16)
        self.lat_deep = up(self.lat, 16)
        self.act_deep = up(self.act, 16)
        self.cols = self.horizon * self.seqs
        self.net_rows = self.mlp + self.deep
        self.at_w3 = self.net_rows
        self.at_enc = self.at_w3 + up(self.lat, 8)
        self.at_prio = self.at_enc + up(max(self.lat, self.obs_deep + 1), 16)

    def dyn_rows(self, total):
        self.prio_rows = up(-(-total // self.mlp), 8)
        return up(self.at_prio + self.prio_rows, 64)


def places():
    dp = lax.axis_index("dp")
    pb = lax.axis_index("pb")
    core = lax.rem(dp, 2)
    side = lax.rem(lax.div(dp, 2), 2)
    return dp, pb, core, side


def square(relative):
    dp, pb, core, side = places()
    return lax.rem(side + relative // 2, 2) * 2 + lax.rem(pb + relative % 2, 2)


def pack_kernel(w1, b1, gain, shift, w2, b2, w3, b3, out):
    mlp = w2.shape[1]
    joined = w1.shape[1]
    half = out.shape[0]
    core = places()[2]

    @pl.when(core == 0)
    def _():
        out[...] = w2[0, :half]

    @pl.when(core == 1)
    def _():
        at = mlp - half
        out[:at] = w2[0, half:]
        out[at : at + joined] = w1[0]
        at = at + joined
        out[at:] = jnp.zeros((half - at, mlp), f32)
        for ref in (b1, gain, shift, b2, w3):
            out[at : at + 1] = ref[...]
            at = at + 1
        out[at : at + 1] = jnp.full((1, mlp), b3[0], f32)


def rollout_kernel(
    size,
    scale,
    obs_first,
    obs_next,
    actions,
    rewards,
    enc_w1,
    enc_b1,
    enc_w2,
    enc_b2,
    dyn_w1,
    dyn_b1,
    dyn_w2,
    dyn_b2,
    dyn_w3,
    dyn_b3,
    rew_w1,
    rew_b1,
    rew_w2,
    rew_b2,
    rew_w3,
    rew_b3,
    joint,
    keep0,
    keep1,
    keep2,
    keep3,
    send0,
    send1,
    send2,
    send3,
    state_grad,
    consist,
    dyn_h1,
    dyn_h2,
    enc_h,
    obs_aug,
    w_aug,
    w_out,
    e_aug,
    e_out,
    reward_grads,
    dyn_square,
    rew_square,
    sems,
):
    lat, act, one, deep = size.lat, size.act, size.one, size.deep
    mlp, seqs, cols, horizon = size.mlp, size.seqs, size.cols, size.horizon
    joined = lat + act
    dp, pb, core, side = places()
    fetch = [
        pltpu.make_async_copy(dyn_w2, dyn_square, sems.at[0]),
        pltpu.make_async_copy(rew_w2, rew_square, sems.at[1]),
    ]
    for copy in fetch:
        copy.start()

    def first_weight(ref, bias, kept):
        w_aug[...] = jnp.zeros_like(w_aug)
        w_aug[:kept] = ref[...]
        w_aug[one : one + 1] = row(bias)
        return split(w_aug[...])

    obs_aug[...] = jnp.zeros_like(obs_aug)
    for step in range(horizon):
        obs_aug[: size.obs, step * seqs : (step + 1) * seqs] = obs_next[step]
    obs_aug[: size.obs, cols:] = obs_first[...]
    obs_aug[size.obs : size.obs + 1] = jnp.ones((1, cols + seqs), f32)
    e_aug[...] = jnp.zeros_like(e_aug)
    e_aug[: size.obs] = enc_w1[...]
    e_aug[size.obs : size.obs + 1] = row(enc_b1)
    e_out[...] = jnp.zeros_like(e_out)
    e_out[:lat] = enc_w2[...]
    w_out[...] = jnp.zeros_like(w_out)
    w_out[:lat] = dyn_w3[...]
    small = jnp.concatenate(
        [
            jnp.concatenate([row(enc_b2), jnp.zeros((1, LANES - lat), f32)], axis=1),
            jnp.concatenate([row(dyn_b3), jnp.zeros((1, LANES - lat), f32)], axis=1),
        ],
        axis=0,
    )
    small = columns_of([small[0:1], small[1:2]])
    enc_b2_col = small[: size.lat_deep, :LANES]
    dyn_b3_col = small[: size.lat_deep, LANES:]
    wide = columns_of([row(dyn_b2), row(rew_b2), row(rew_w3)])
    dyn_b2_col = wide[:, :LANES]

    enc_first = mm(stack_weight(split(e_aug[...])), stack_input(split(obs_aug[...])), TN)
    enc_hidden = elu(enc_first)
    enc_h[...] = enc_hidden[:, cols:]
    latent = dot3(split(e_out[...]), split(enc_hidden), NN) + spread_lanes(
        enc_b2_col, cols + seqs
    )
    joint[:, :] = jnp.zeros_like(joint)
    joint[: size.lat_deep, 2 * cols :] = latent[:, :cols]
    for step in range(horizon):
        joint[lat : lat + act, step * seqs : (step + 1) * seqs] = actions[step]
    joint[one : one + 1] = jnp.ones((1, 3 * cols), f32)

    first = stack_weight(first_weight(dyn_w1, dyn_b1, joined))
    fetch[0].wait()
    second = split(dyn_square[...].T)
    third = split(w_out[...])
    latent = latent[:, cols:]
    for step in range(horizon):
        here = slice(step * seqs, (step + 1) * seqs)
        joint[:lat, here] = latent[:lat]
        hidden = elu(mm(first, stack_input(split(joint[:, here])), TN))
        dyn_h1[:, here] = hidden
        hidden = elu(dot3_narrow(second, split(hidden), NN) + dyn_b2_col)
        dyn_h2[:, here] = hidden
        latent = dot3_narrow(third, split(hidden), NN) + dyn_b3_col
        after = 2 * cols + step * seqs
        goal = joint[: size.lat_deep, after : after + seqs]
        factor = scale * decay_rate**step * consist_coef * 2.0 / lat
        consist[:, here] = factor * (latent - goal)

    states = split(joint[:, :cols])
    first = first_weight(rew_w1, rew_b1, joined)
    fetch[1].wait()
    second = split(rew_square[...])
    b2_col = spread_lanes(wide[:, LANES : 2 * LANES], cols)
    w3_col = spread_lanes(wide[:, 2 * LANES : 3 * LANES], cols)
    h1 = elu(mm(stack_weight(first), stack_input(states), TN))
    h1_parts = split(h1)
    h2 = elu(dot3(second, h1_parts, TN) + b2_col)
    predicted = jnp.sum(w3_col * h2, axis=0, keepdims=True) + rew_b3[0]
    wanted = jnp.concatenate([rewards[step : step + 1] for step in range(horizon)], axis=1)
    out_grad = decay_row(horizon, seqs, scale * reward_coef * 2.0) * (predicted - wanted)
    h2_grad = w3_col * out_grad * elu_slope(h2)
    h2_parts = split(h2_grad)
    reward_grads[:mlp] = dot3(h1_parts, h2_parts, NT)
    h1_grad = dot3(second, h2_parts, NN) * elu_slope(h1)
    h1_grad = split(h1_grad)
    reward_grads[mlp:] = dot3(states, h1_grad, NT)
    state_grad[...] = dot3_short(first, h1_grad, NN)
    sums = rows_of([fold(h2_grad), fold(h2 * out_grad)])
    reward_grads[mlp + one + 1 : mlp + one + 3] = sums[:2]
    reward_grads[mlp + one + 3 : mlp + one + 4] = first_lane(jnp.sum(out_grad), mlp)

    eighth = size.net_rows // 8
    for h in range(2):
        place = core if h == 0 else 1 - core
        for k in range(4):
            out = ((keep0, keep1, keep2, keep3), (send0, send1, send2, send3))[h][k]
            start = (place * 4 + square(k)) * eighth
            out[...] = reward_grads[pl.ds(pl.multiple_of(start, 8), eighth)]


def act_kernel(
    size,
    begun,
    pol_w1,
    pol_b1,
    pol_w2,
    pol_b2,
    pol_w3,
    pol_b3,
    joint,
    pol_h1,
    pol_h2,
    w_aug,
    w_act,
):
    lat, act, one = size.lat, size.act, size.one
    cols = size.cols
    joined = lat + act
    joint[...] = begun[...]
    w_act[...] = jnp.zeros_like(w_act)
    w_act[:act] = pol_w3[...]
    small = jnp.concatenate([row(pol_b3), jnp.zeros((1, LANES - act), f32)], axis=1)
    pol_b3_col = columns_of([small])[: size.act_deep]
    b2_col = spread_lanes(columns_of([row(pol_b2)]), cols)
    w_aug[...] = jnp.zeros_like(w_aug)
    w_aug[:lat] = pol_w1[...]
    w_aug[one : one + 1] = row(pol_b1)
    first = stack_weight(split(w_aug[...]))
    second = split(pol_w2[...])
    third = split(w_act[...])
    for block in (0, 2):
        here = slice(block * cols, (block + 1) * cols)
        h1 = elu(mm(first, stack_input(split(joint[:, here])), TN))
        h2 = elu(dot3(second, split(h1), TN) + b2_col)
        action = jnp.tanh(dot3(third, split(h2), NN) + spread_lanes(pol_b3_col, cols))[:act]
        if block == 0:
            pol_h1[...] = h1
            pol_h2[...] = h2
            joint[:lat, cols : 2 * cols] = joint[:lat, :cols]
            joint[lat:joined, cols : 2 * cols] = action
        else:
            joint[lat:joined, here] = action


def value_kernel(
    size,
    scale,
    joint,
    rewards,
    q_w1,
    q_b1,
    q_gain,
    q_shift,
    q_w2,
    q_b2,
    q_w3,
    q_b3,
    packed_y,
    packed_c,
    keep0,
    keep1,
    keep2,
    keep3,
    send0,
    send1,
    send2,
    send3,
    state_grad,
    chosen_grad,
    prio,
    packed,
    aug,
    w1_rows,
    w1_parts,
    w2_rows,
    w2_lanes,
    vectors,
    last,
    inputs,
    next_value,
    spread,
    grads,
    work,
    normed,
    second,
    hidden,
    backs,
    sums,
):
    lat, act, one, deep = size.lat, size.act, size.one, size.deep
    mlp, seqs, cols, horizon = size.mlp, size.seqs, size.cols, size.horizon
    joined = lat + act
    dp, pb, core, side = places()
    half = packed_y.shape[0]
    packed[pl.ds(pl.multiple_of(core * half, 8), half)] = packed_y[...]
    packed[pl.ds(pl.multiple_of((1 - core) * half, 8), half)] = packed_c[...]

    at = mlp + joined
    for slot in range(TWIN):
        if slot == 0:
            w1, b1, w2 = q_w1[0], q_b1[...], q_w2[0]
            rows = [q_gain[...], q_shift[...], q_b2[...], q_w3[...]]
            b3 = jnp.full((1, LANES), q_b3[0], f32)
        else:
            w1, b1, w2 = packed[mlp:at], packed[at : at + 1], packed[:mlp]
            rows = [packed[at + i : at + i + 1] for i in (1, 2, 3, 4)]
            b3 = packed[at + 5 : at + 6, :LANES]
        aug[...] = jnp.zeros_like(aug)
        aug[:joined] = w1
        aug[one : one + 1] = b1
        high, low = split(aug[...])
        for place, part in enumerate((high, high, low)):
            w1_rows[slot, place * deep : (place + 1) * deep] = part
            if place > 0:
                w1_parts[slot, (place - 1) * deep : place * deep] = part
        high, low = split(w2)
        for place, part in enumerate((high, high, low)):
            w2_rows[slot, place * mlp : (place + 1) * mlp] = part
            w2_lanes[slot, :, place * mlp : (place + 1) * mlp] = part
        vectors[slot] = columns_of(rows)
        last[slot] = b3
    inputs[...] = stack_input(split(joint[...]))

    height = 32

    def blocks(width):
        for left in range(0, width, cols):
            for top in range(0, mlp, height):
                yield slice(top, top + height), slice(left, left + cols)

    def column(slot, which, rows):
        return spread_lanes(vectors[slot, rows, which * LANES : (which + 1) * LANES], cols)

    def keep_parts(ref, rows, here, value):
        high, low = split(value)
        for place, part in enumerate((high, low, high)):
            ref[rows.start + place * mlp : rows.stop + place * mlp, here] = part

    def added(totals, here, value):
        eight = value.reshape(height // 8, 8, cols).sum(axis=0)
        at = here.start // cols
        totals[at] = eight if totals[at] is None else totals[at] + eight

    def total_of(totals):
        return jnp.concatenate([jnp.sum(t, axis=0, keepdims=True) for t in totals], axis=1)

    def forward(slot, start, width, kept):
        work[:, :width] = mm(w1_rows[slot], inputs[:, start : start + width], TN)
        totals = [None] * (width // cols)
        for rows, here in blocks(width):
            added(totals, here, work[rows, here])
        mean = total_of(totals) / mlp
        totals = [None] * (width // cols)
        for rows, here in blocks(width):
            center = work[rows, here] - mean[:, here]
            added(totals, here, center * center)
        inverse = lax.rsqrt(total_of(totals) / mlp + norm_epsilon)
        for rows, here in blocks(width):
            value = (work[rows, here] - mean[:, here]) * inverse[:, here]
            if kept:
                normed[rows, here] = value
            value = jnp.tanh(column(slot, 0, rows) * value + column(slot, 1, rows))
            keep_parts(hidden, rows, here, value)
        work[:, :width] = mm(w2_rows[slot], hidden[:, :width], TN)
        totals = [None] * (width // cols)
        for rows, here in blocks(width):
            value = elu(work[rows, here] + column(slot, 2, rows))
            if kept:
                second[rows, here] = value
            if here.start == 0:
                added(totals, here, column(slot, 3, rows) * value)
        return total_of(totals[:1]) + spread_lanes(last[slot], cols), inverse

    @pl.loop(0, TWIN)
    def _(slot):
        next_value[slot] = forward(slot, 2 * cols, cols, False)[0]

    wanted = jnp.concatenate([rewards[step : step + 1] for step in range(horizon)], axis=1)
    next_value[0] = wanted + discount * jnp.minimum(next_value[0], next_value[1])
    spread[...] = jnp.zeros_like(spread)
    state_grad[...] = jnp.zeros_like(state_grad)
    chosen_grad[...] = jnp.zeros_like(chosen_grad)

    @pl.loop(0, TWIN)
    def _(slot):
        value, inverse = forward(slot, 0, 2 * cols, True)
        error = value - next_value[0]
        spread[...] += jnp.sqrt(error * error + 1.0)
        out_grad = jnp.concatenate(
            [
                decay_row(horizon, seqs, scale * value_coef * 2.0) * error,
                decay_row(horizon, seqs, -policy_coef * 0.5 * scale),
            ],
            axis=1,
        )
        for rows, here in blocks(2 * cols):
            result = second[rows, here]
            back = column(slot, 3, rows) * out_grad[:, here] * elu_slope(result)
            keep_parts(backs, rows, here, back)
            if here.start == 0:
                sums[rows, :LANES] = fold(back)
                sums[rows, 3 * LANES :] = fold(result * out_grad[:, here])
        work[...] = mm(w2_lanes[slot], backs[...], NN)
        grads[slot, :mlp] = dot3(
            (hidden[:mlp, :cols], hidden[mlp : 2 * mlp, :cols]),
            (backs[:mlp, :cols], backs[mlp : 2 * mlp, :cols]),
            NT,
        )
        plain, along = [None] * 2, [None] * 2
        for rows, here in blocks(2 * cols):
            high = hidden[rows, here].astype(f32)
            low = hidden[mlp + rows.start : mlp + rows.stop, here].astype(f32)
            result = high + low
            pre = work[rows, here] * (1.0 - result * result)
            unit = normed[rows, here]
            if here.start == 0:
                sums[rows, LANES : 2 * LANES] = fold(pre * unit)
                sums[rows, 2 * LANES : 3 * LANES] = fold(pre)
            back = column(slot, 0, rows) * pre
            work[rows, here] = back
            added(plain, here, back)
            added(along, here, back * unit)
        plain, along = total_of(plain) / mlp, total_of(along) / mlp
        for rows, here in blocks(2 * cols):
            back = work[rows, here] - plain[:, here] - normed[rows, here] * along[:, here]
            keep_parts(backs, rows, here, back * inverse[:, here])
        states = (inputs[:deep, :cols], inputs[deep : 2 * deep, :cols])
        first_parts = (backs[:mlp, :cols], backs[mlp : 2 * mlp, :cols])
        grads[slot, mlp:] = dot3(states, first_parts, NT)
        both = mm(w1_parts[slot], backs[:mlp], NN)
        into = both[:deep] + both[deep:] + mm(w1_parts[slot, :deep], backs[mlp : 2 * mlp], NN)
        state_grad[...] += into[:, :cols]
        chosen_grad[...] += into[:, cols:]
        lines = rows_of([sums[:, at * LANES : (at + 1) * LANES] for at in range(4)])
        grads[slot, mlp + one + 1 : mlp + one + 5] = lines[:4]
        grads[slot, mlp + one + 5 : mlp + one + 6] = first_lane(jnp.sum(out_grad[:, :cols]), mlp)

    total = spread[:, :seqs]
    for step in range(1, horizon):
        total = total + spread[:, step * seqs : (step + 1) * seqs]
    prio[...] = total / (TWIN * horizon)

    quarter = size.net_rows // 4
    for h in range(2):
        place = core if h == 0 else 1 - core
        for k in range(4):
            out = ((keep0, keep1, keep2, keep3), (send0, send1, send2, send3))[h][k]
            start = (place * 2 + lax.div(square(k), 2)) * quarter
            out[...] = grads[k % 2, pl.ds(pl.multiple_of(start, 8), quarter)]


def policy_kernel(
    size, pol_w2, pol_w3, joint, pol_h1, pol_h2, chosen_grad, pol, w_act, act_grad
):
    lat, act, one = size.lat, size.act, size.one
    mlp, cols = size.mlp, size.cols
    joined = lat + act
    states = split(joint[:, :cols])
    w_act[...] = jnp.zeros_like(w_act)
    w_act[:act] = pol_w3[...]
    act_grad[...] = jnp.zeros_like(act_grad)
    chosen = joint[lat:joined, cols : 2 * cols]
    act_grad[:act] = chosen_grad[lat:joined] * (1.0 - chosen * chosen)
    out_parts = split(act_grad[...])
    weight = split(w_act[...])
    h2 = pol_h2[...]
    h2_grad = mm(stack_weight(weight), stack_input(out_parts), TN) * elu_slope(h2)
    h2_parts = split(h2_grad)
    h1 = pol_h1[...]
    pol[:mlp] = dot3(split(h1), h2_parts, NT)
    h1_grad = dot3(split(pol_w2[...]), h2_parts, NN) * elu_slope(h1)
    pol[mlp:] = dot3(states, split(h1_grad), NT)
    pol[mlp + lat : mlp + joined] = dot3(out_parts, split(h2), NT)[:act]
    pol[mlp + one + 1 : mlp + one + 2] = rows_of([fold(h2_grad)])[:1]
    sums = rows_of([fold(act_grad[...])])
    pol[mlp + one + 2 : mlp + one + 3] = jnp.zeros((1, mlp), f32)
    pol[mlp + one + 2 : mlp + one + 3, : size.act_deep] = sums[:1]


def shared_kernel(
    size,
    scale,
    total,
    obs_first,
    enc_w1,
    enc_w2,
    dyn_w1,
    dyn_w2,
    dyn_w3,
    joint,
    reward_state,
    consist,
    dyn_h1,
    dyn_h2,
    enc_h,
    value_state,
    prio,
    pol,
    keep0,
    keep1,
    keep2,
    keep3,
    send0,
    send1,
    send2,
    send3,
    obs_grad,
    obs_aug,
    w_out,
    e_out,
    lat_grad,
    second_high,
    second_low,
    first_high,
    first_low,
    dyn,
):
    lat, act, one, deep = size.lat, size.act, size.one, size.deep
    mlp, seqs, cols, horizon = size.mlp, size.seqs, size.cols, size.horizon
    joined = lat + act
    lat_deep, hidden = size.lat_deep, size.hidden
    dp, pb, core, side = places()
    states = split(joint[:, :cols])

    w_out[...] = jnp.zeros_like(w_out)
    w_out[:lat] = dyn_w3[...]
    third = stack_weight(split(w_out[...]))
    second = split(dyn_w2[...])
    first = split(dyn_w1[...])
    lat_rows = lax.broadcasted_iota(jnp.int32, (lat_deep, seqs), 0)
    carry = None
    for step in reversed(range(horizon)):
        here = slice(step * seqs, (step + 1) * seqs)
        grad = consist[:, here]
        if carry is not None:
            after = slice((step + 1) * seqs, (step + 2) * seqs)
            grad = grad + carry + reward_state[:lat_deep, after] + value_state[:lat_deep, after]
            grad = jnp.where(lat_rows < lat, grad, 0.0)
        lat_grad[:, here] = grad
        high, low = split(grad)
        h2_grad = mm(third, jnp.concatenate([high, low, high], axis=0), TN)
        h2_grad = h2_grad * elu_slope(dyn_h2[:, here])
        parts = split(h2_grad)
        second_high[:, here], second_low[:, here] = parts
        h1_grad = dot3_narrow(second, parts, NN) * elu_slope(dyn_h1[:, here])
        parts = split(h1_grad)
        first_high[:, here], first_low[:, here] = parts
        back = dot3_narrow(first, parts, NN)
        carry = jnp.concatenate([back, jnp.zeros((lat_deep - joined, seqs), f32)], axis=0)
    grad = carry + reward_state[:lat_deep, :seqs] + value_state[:lat_deep, :seqs]
    grad = jnp.where(lat_rows < lat, grad, 0.0)
    second_parts = (second_high[...], second_low[...])
    first_parts = (first_high[...], first_low[...])
    dyn[:mlp] = dot3(split(dyn_h1[...]), second_parts, NT)
    dyn[mlp : size.net_rows] = dot3(states, first_parts, NT)
    out_grad = lat_grad[...]
    b2_sum = fold(second_high[...].astype(f32) + second_low[...].astype(f32))
    dyn[size.at_w3 : size.at_enc] = dot3(split(out_grad), split(dyn_h2[...]), NT)[
        : size.at_enc - size.at_w3
    ]
    dyn[mlp + one + 1 : mlp + one + 2] = rows_of([b2_sum])[:1]
    dyn[mlp + one + 2 : mlp + one + 3] = jnp.zeros((1, mlp), f32)
    dyn[mlp + one + 2 : mlp + one + 3, :lat_deep] = rows_of([fold(out_grad)])[:1]

    dyn[size.at_enc :] = jnp.zeros((dyn.shape[0] - size.at_enc, mlp), f32)
    obs_aug[...] = jnp.zeros_like(obs_aug)
    obs_aug[: size.obs] = obs_first[...]
    obs_aug[size.obs : size.obs + 1] = jnp.ones((1, seqs), f32)
    e_out[...] = jnp.zeros_like(e_out)
    e_out[:lat] = enc_w2[...]
    parts = split(grad)
    h = enc_h[...]
    h_grad = dot3(split(e_out[...]), parts, TN) * elu_slope(h)
    h_parts = split(h_grad)
    dyn[size.at_enc : size.at_enc + lat_deep, :hidden] = dot3(parts, split(h), NT)
    dyn[size.at_enc : size.at_enc + size.obs_deep, hidden : 2 * hidden] = dot3(
        split(obs_aug[...]), h_parts, NT
    )
    at = size.at_enc + size.obs_deep
    dyn[at : at + 1, hidden : hidden + lat_deep] = rows_of([grad])[:1]
    obs_grad[...] = total * dot3(split(enc_w1[...]), h_parts, NN)

    index = (dp * 2 + pb) * seqs
    rows = size.prio_rows
    at = lax.broadcasted_iota(jnp.int32, (rows, mlp), 0) * mlp
    at = at + lax.broadcasted_iota(jnp.int32, (rows, mlp), 1)
    mine = (at >= index) & (at < index + seqs)
    value = jnp.concatenate([prio[...]] * (mlp // seqs), axis=1)
    dyn[size.at_prio : size.at_prio + rows] = jnp.where(mine, value, 0.0)

    small, large = size.net_rows // 8, dyn.shape[0] // 8
    for h in range(2):
        place = core if h == 0 else 1 - core
        for k in range(4):
            out = ((keep0, keep1, keep2, keep3), (send0, send1, send2, send3))[h][k]
            start = (place * 4 + square(k)) * small
            out[:small] = pol[pl.ds(pl.multiple_of(start, 8), small)]
            start = (place * 4 + square(k)) * large
            out[small:] = dyn[pl.ds(pl.multiple_of(start, 8), large)]


def halve_kernel(*refs):
    for k in range(4):
        refs[8 + k][...] = refs[k][...] + refs[4 + k][...]


def sum_kernel(*refs):
    total = refs[0][...]
    for ref in refs[1:-1]:
        total = total + ref[...]
    refs[-1][...] = total


def lane_half(other):
    mine = lax.rem(lax.div(lax.axis_index("dp"), 4), 2)
    at = 1 - mine if other else mine
    return pl.ds(pl.multiple_of(at * 256, 256), 256)


def cut_kernel(*refs):
    *summed, own, from_x, from_y, from_xy, mine, other, whole = refs
    at = 0
    for ref in summed:
        whole[at : at + ref.shape[0]] = ref[...]
        at = at + ref.shape[0]
    whole[at:] = (own[...] + from_x[...]) + (from_y[...] + from_xy[...])
    mine[...] = whole[:, lane_half(False)]
    other[...] = whole[:, lane_half(True)]


def rejoin_kernel(mine, other, *outs):
    for out in outs:
        out[:, lane_half(False)] = mine[: out.shape[0]]
        out[:, lane_half(True)] = other[: out.shape[0]]


def collect(out, pieces, first, rows, core, side, pb):
    for h in range(2):
        for k in range(4):
            place = lax.rem(core + h, 2) * 4 + lax.rem(side + k // 2, 2) * 2 + lax.rem(pb + k, 2)
            out[pl.ds(pl.multiple_of(place * rows, 8), rows)] = pieces[h][k][first : first + rows]


def finish_value_kernel(
    size,
    own,
    from_x,
    from_y,
    from_xy,
    c_own,
    c_x,
    c_y,
    c_xy,
    rew_w1,
    rew_b1,
    rew_w2,
    rew_b2,
    rew_w3,
    rew_b3,
    q_w1,
    q_b1,
    q_gain,
    q_shift,
    q_w2,
    q_b2,
    q_w3,
    q_b3,
    rew,
    twin,
):
    dp, pb, core, side = places()
    mlp, one = size.mlp, size.one
    eighth, quarter = size.net_rows // 8, size.net_rows // 4
    pieces = ((own, from_y, from_x, from_xy), (c_own, c_y, c_x, c_xy))
    collect(rew, pieces, 0, eighth, core, side, pb)
    for h in range(2):
        for k in range(2):
            place = lax.rem(core + h, 2) * 2 + lax.rem(side + k, 2)
            twin[pl.ds(pl.multiple_of(place * quarter, 8), quarter)] = pieces[h][2 * k][eighth:]
    rew_w2[...] = rew[:mlp]
    rew_w1[...] = rew[mlp : mlp + one]
    for ref, at in ((rew_b1, 0), (rew_b2, 1), (rew_w3, 2), (rew_b3, 3)):
        n = ref.shape[0]
        ref[...] = rew[mlp + one + at : mlp + one + at + 1, :n].reshape(n)
    q_w2[0] = twin[:mlp]
    q_w1[0] = twin[mlp : mlp + one]
    for at, ref in enumerate((q_b1, q_b2, q_gain, q_shift, q_w3)):
        ref[...] = twin[mlp + one + at : mlp + one + at + 1]
    q_b3[...] = twin[mlp + one + 5 : mlp + one + 6, :1].reshape(1)


def finish_shared_kernel(
    size,
    own,
    from_x,
    from_y,
    from_xy,
    c_own,
    c_x,
    c_y,
    c_xy,
    enc_w1,
    enc_b1,
    enc_w2,
    enc_b2,
    dyn_w1,
    dyn_b1,
    dyn_w2,
    dyn_b2,
    dyn_w3,
    dyn_b3,
    pol_w1,
    pol_b1,
    pol_w2,
    pol_b2,
    pol_w3,
    pol_b3,
    prio,
    pol,
    dyn,
):
    dp, pb, core, side = places()
    mlp, one, lat, act, hidden = size.mlp, size.one, size.lat, size.act, size.hidden
    pieces = ((own, from_y, from_x, from_xy), (c_own, c_y, c_x, c_xy))
    small, large = size.net_rows // 8, dyn.shape[0] // 8
    collect(pol, pieces, 0, small, core, side, pb)
    collect(dyn, pieces, small, large, core, side, pb)

    def line(out, source, at, first=0):
        n = out.shape[0]
        out[...] = source[at : at + 1, first : first + n].reshape(n)

    pol_w2[...] = pol[:mlp]
    pol_w1[...] = pol[mlp : mlp + lat]
    pol_w3[...] = pol[mlp + lat : mlp + lat + act]
    line(pol_b1, pol, mlp + one)
    line(pol_b2, pol, mlp + one + 1)
    line(pol_b3, pol, mlp + one + 2)
    dyn_w2[...] = dyn[:mlp]
    dyn_w1[...] = dyn[mlp : mlp + one]
    dyn_w3[...] = dyn[size.at_w3 : size.at_w3 + lat]
    line(dyn_b1, dyn, mlp + one)
    line(dyn_b2, dyn, mlp + one + 1)
    line(dyn_b3, dyn, mlp + one + 2)
    enc_w2[...] = dyn[size.at_enc : size.at_enc + lat, :hidden]
    enc_w1[...] = dyn[size.at_enc : size.at_enc + size.obs, hidden : 2 * hidden]
    line(enc_b1, dyn, size.at_enc + size.obs, hidden)
    line(enc_b2, dyn, size.at_enc + size.obs_deep, hidden)
    for at in range(prio.shape[0] // mlp):
        line(prio.at[at * mlp : (at + 1) * mlp], dyn, size.at_prio + at)


VMEM = pl.BlockSpec(memory_space=pltpu.VMEM)
SMEM = pl.BlockSpec(memory_space=pltpu.SMEM)


ANY = pl.BlockSpec(memory_space=pl.ANY)


def call(
    kernel, name, outs, args, scratch=(), scalars=(), left=(), after=(), mega=16
):
    def made(shape):
        return jax.ShapeDtypeStruct(shape, f32)

    def ordered(*refs):
        return kernel(*refs[: len(args)], *refs[len(args) + len(after) :])

    single = not isinstance(outs, list)
    shapes = [made(shape) for shape in ([outs] if single else outs)]
    specs = [SMEM if at in scalars else ANY if at in left else VMEM for at in range(len(args))]
    return pl.pallas_call(
        ordered,
        out_shape=shapes[0] if single else shapes,
        in_specs=specs + [ANY] * len(after),
        out_specs=VMEM if single else [VMEM] * len(shapes),
        scratch_shapes=list(scratch),
        compiler_params=pltpu.CompilerParams(vmem_limit_bytes=mega * 2**20),
        cost_estimate=pl.CostEstimate(flops=1, bytes_accessed=1, transcendentals=0),
        name=name,
    )(*args, *after)


def flipped(axis, bit):
    count = lax.axis_size(axis)
    return [(at, at ^ (1 << bit)) for at in range(count)]


def on_device(*args):
    a = dict(zip(NAMES, args))
    size = Sizes(a["obs_next"], a["actions"], a["enc_w1"], a["dyn_w1"])
    n_dp, n_pb = lax.axis_size("dp"), lax.axis_size("pb")
    total = size.seqs * n_dp * n_pb
    scale = 1.0 / total
    mlp, cols, seqs, deep = size.mlp, size.cols, size.seqs, size.deep
    dyn_rows = size.dyn_rows(total)
    net_rows = size.net_rows
    joined = size.lat + size.act

    def swap_core(block):
        return lax.ppermute(block, "dp", flipped("dp", 0))

    def swap_x(block):
        return lax.ppermute(block, "dp", flipped("dp", 1))

    def swap_y(block):
        return lax.ppermute(block, "pb", flipped("pb", 0))

    def swap_xy(block):
        route = []
        for dp in range(n_dp):
            for pb in range(n_pb):
                route.append((dp * n_pb + pb, (dp ^ 2) * n_pb + (pb ^ 1)))
        return lax.ppermute(block, ("dp", "pb"), route)

    def shape(rows, width, kind=f32):
        return pltpu.VMEM((rows, width), kind)

    def to_square(block):
        return [swap_x(block[0]), swap_y(block[1]), swap_xy(block[2])]

    def swap_z(block):
        return lax.ppermute(block, "dp", flipped("dp", 2))

    def swapped(parts):
        return parts[:4] + [swap_core(part) for part in parts[4:]]

    def halve(name, parts, after=()):
        own, to_y, to_x, to_xy = call(
            halve_kernel, name, [parts[0].shape] * 4, parts, after=after
        )
        return [own] + to_square((to_x, to_y, to_xy))

    def cut(name, parts, after=()):
        rows = sum(part.shape[0] for part in parts[:-3])
        mine, other = call(
            cut_kernel,
            name,
            [(rows, mlp // 2)] * 2,
            parts,
            scratch=[shape(rows, mlp)],
            after=after,
        )
        return [mine, swap_z(other)]

    def further_z(name, parts):
        for bit in range(3, n_dp.bit_length() - 1):
            whole = call(sum_kernel, name, parts[0].shape, parts)
            parts = [whole, lax.ppermute(whole, "dp", flipped("dp", bit))]
        return parts

    def back_z(name, parts, after=()):
        whole = call(sum_kernel, name, parts[0].shape, parts, after=after)
        return [whole, swap_z(whole)]

    def rejoin(name, parts, head, after=()):
        rows = parts[0].shape[0]
        outs = [(rows, mlp)] + ([(head, mlp)] if head < rows else [])
        outs = call(rejoin_kernel, name, outs, parts, after=after)
        return [outs[0]] + to_square([outs[0], outs[-1], outs[-1]])

    def both_cores(parts):
        return parts + [swap_core(part) for part in parts]

    q = [a[n] for n in NAMES[26:]]
    packed = call(
        pack_kernel,
        "pack",
        (net_rows // 2, mlp),
        q,
        scalars=(7,),
        mega=63,
    )
    packed_y = swap_y(packed)

    eighth = net_rows // 8
    begun, *reward, reward_state, consist, dyn_h1, dyn_h2, enc_h = call(
        functools.partial(rollout_kernel, size, scale),
        "rollout",
        [(deep, 3 * cols)]
        + [(eighth, mlp)] * 8
        + [(deep, cols), (size.lat_deep, cols), (mlp, cols), (mlp, cols), (size.hidden, seqs)],
        [a[n].T if n in TURNED else a[n] for n in NAMES[:20]],
        scratch=[
            shape(size.obs_deep, cols + seqs),
            shape(deep, mlp),
            shape(size.lat_deep, mlp),
            shape(size.obs_deep, size.hidden),
            shape(size.lat_deep, size.hidden),
            shape(net_rows, mlp),
            shape(mlp, mlp),
            shape(mlp, mlp),
            pltpu.SemaphoreType.DMA((2,)),
        ],
        scalars=(19,),
        left=(10, 16),
        mega=50,
    )
    packed_y, begun = lax.optimization_barrier((packed_y, begun))
    packed_c = swap_core(packed_y)
    reward = swapped(reward)
    joint, pol_h1, pol_h2 = call(
        functools.partial(act_kernel, size),
        "act",
        [(deep, 3 * cols), (mlp, cols), (mlp, cols)],
        [begun] + [a[n].T if n in TURNED else a[n] for n in NAMES[20:26]],
        scratch=[shape(deep, mlp), shape(size.act_deep, mlp)],
        mega=32,
    )
    reward = halve("reward_halve", reward, after=[pol_h1])

    rows = 2 * eighth
    *parts, value_state, chosen_grad, prio = call(
        functools.partial(value_kernel, size, scale),
        "value",
        [(rows, mlp)] * 8 + [(deep, cols), (deep, cols), (1, seqs)],
        [joint, a["rewards"]] + q + [packed_y, packed_c],
        scratch=[
            shape(net_rows, mlp),
            shape(deep, mlp),
            pltpu.VMEM((TWIN, 3 * deep, mlp), bf16),
            pltpu.VMEM((TWIN, 2 * deep, mlp), bf16),
            pltpu.VMEM((TWIN, 3 * mlp, mlp), bf16),
            pltpu.VMEM((TWIN, mlp, 3 * mlp), bf16),
            pltpu.VMEM((TWIN, mlp, 4 * LANES), f32),
            pltpu.VMEM((TWIN, 1, LANES), f32),
            shape(3 * deep, 3 * cols, bf16),
            pltpu.VMEM((TWIN, 1, cols), f32),
            shape(1, cols),
            pltpu.VMEM((TWIN, net_rows, mlp), f32),
            shape(mlp, 2 * cols),
            shape(mlp, 2 * cols),
            shape(mlp, 2 * cols),
            shape(3 * mlp, 2 * cols, bf16),
            shape(3 * mlp, 2 * cols, bf16),
            shape(mlp, 4 * LANES),
        ],
        scalars=(9,),
        after=[reward[0]],
        mega=48,
    )

    reward = call(sum_kernel, "reward_sum", reward[0].shape, reward, after=[prio])
    parts[4:], reward = lax.optimization_barrier((parts[4:], reward))
    parts = swapped(parts)
    value_rows, shared_rows = rows, eighth + dyn_rows // 8
    value = halve("value_halve", parts, after=[reward])
    pol = call(
        functools.partial(policy_kernel, size),
        "policy",
        (net_rows, mlp),
        [a["pol_w2"], a["pol_w3"].T, joint, pol_h1, pol_h2, chosen_grad],
        after=[value[0]],
        scratch=[shape(size.act_deep, mlp), shape(size.act_deep, cols)],
        mega=32,
    )

    *parts, obs_grad = call(
        functools.partial(shared_kernel, size, scale, total),
        "shared",
        [(shared_rows, mlp)] * 8 + [(size.obs, seqs)],
        [
            a["obs_first"],
            a["enc_w1"],
            a["enc_w2"].T,
            a["dyn_w1"],
            a["dyn_w2"],
            a["dyn_w3"].T,
            joint,
            reward_state,
            consist,
            dyn_h1,
            dyn_h2,
            enc_h,
            value_state,
            prio,
            pol,
        ],
        scratch=[
            shape(size.obs_deep, seqs),
            shape(size.lat_deep, mlp),
            shape(size.lat_deep, size.hidden),
            shape(size.lat_deep, cols),
            shape(mlp, cols, bf16),
            shape(mlp, cols, bf16),
            shape(mlp, cols, bf16),
            shape(mlp, cols, bf16),
            shape(dyn_rows, mlp),
        ],
        after=[value[0]],
        mega=32,
    )
    parts = swapped(parts)
    value = cut("value_cut", [reward] + value, after=[obs_grad])
    shared = halve("shared_halve", parts, after=[value[0]])
    value = further_z("value_further", value)
    shared = cut("shared_cut", shared)
    value = back_z("value_back", value, after=[shared[0]])
    shared = further_z("shared_further", shared)
    value = rejoin("value_rejoin", value, eighth, after=[shared[0]])
    shared = back_z("shared_back", shared)
    shared = rejoin("shared_rejoin", shared, shared_rows, after=[value[0]])
    value = both_cores(value)
    value_grads = call(
        functools.partial(finish_value_kernel, size),
        "finish_value",
        [a[n].shape for n in NAMES[14:20]] + [a[n].shape for n in NAMES[26:]],
        value,
        scratch=[shape(net_rows, mlp), shape(net_rows, mlp)],
        after=[shared[0]],
    )
    shared, value_grads = lax.optimization_barrier((shared, value_grads))
    shared = both_cores(shared)
    names = NAMES[4:14] + NAMES[20:26]
    shared_grads = call(
        functools.partial(finish_shared_kernel, size),
        "finish_shared",
        [a[n].shape[::-1] if n in TURNED else a[n].shape for n in names] + [(total,)],
        shared,
        scratch=[shape(net_rows, mlp), shape(dyn_rows, mlp)],
    )
    shared_grads = list(shared_grads)
    for at, n in enumerate(names):
        if n in TURNED:
            shared_grads[at] = shared_grads[at].T
    return (
        tuple(shared_grads[:10])
        + tuple(value_grads[:6])
        + tuple(shared_grads[10:16])
        + tuple(value_grads[6:])
        + (obs_grad, shared_grads[-1])
    )


def solution(mesh):
    whole = P()
    seqs = ("dp", "pb")
    twin = (P("pb", None, None),) + (P("pb", None),) * 3 + (P("pb", None, None),)
    twin = twin + (P("pb", None), P("pb", None), P("pb"))
    placed = (P(None, seqs), P(None, None, seqs), P(None, None, seqs), P(None, seqs))
    return jax.shard_map(
        on_device,
        mesh=mesh,
        in_specs=placed + (whole,) * 22 + twin,
        out_specs=(whole,) * 22 + twin + (P(None, seqs), whole),
        check_vma=False,
    )
```

```python
import functools

import jax
import jax.numpy as jnp
from jax import lax
from jax.experimental import pallas as pl
from jax.experimental.pallas import tpu as pltpu
from jax.sharding import PartitionSpec as P

f32 = jnp.float32
bf16 = jnp.bfloat16

TWIN = 2
LANES = 128
decay_rate = 0.5
discount = 0.99
consist_coef = 2.0
reward_coef = 0.5
value_coef = 0.1
policy_coef = 0.1
norm_epsilon = 1e-05

TURNED = ("enc_w2", "dyn_w3", "pol_w3")
NN = ((1,), (0,))
NT = ((1,), (1,))
TN = ((0,), (0,))

NAMES = (
    "obs_first",
    "obs_next",
    "actions",
    "rewards",
    "enc_w1",
    "enc_b1",
    "enc_w2",
    "enc_b2",
    "dyn_w1",
    "dyn_b1",
    "dyn_w2",
    "dyn_b2",
    "dyn_w3",
    "dyn_b3",
    "rew_w1",
    "rew_b1",
    "rew_w2",
    "rew_b2",
    "rew_w3",
    "rew_b3",
    "pol_w1",
    "pol_b1",
    "pol_w2",
    "pol_b2",
    "pol_w3",
    "pol_b3",
    "q_w1",
    "q_b1",
    "q_gain",
    "q_shift",
    "q_w2",
    "q_b2",
    "q_w3",
    "q_b3",
)


def up(number, multiple):
    return -(-number // multiple) * multiple


def mm(left, right, dims):
    return lax.dot_general(left, right, (dims, ((), ())), preferred_element_type=f32)


def split(value):
    high = value.astype(bf16)
    return high, (value - high.astype(f32)).astype(bf16)


def dot3(left, right, dims):
    return (
        mm(left[0], right[0], dims) + mm(left[0], right[1], dims) + mm(left[1], right[0], dims)
    )


def dot3_narrow(left, right, dims):
    width = right[0].shape[1]
    both = mm(left[0], jnp.concatenate(right, axis=1), dims)
    return both[:, :width] + both[:, width:] + mm(left[1], right[0], dims)


def dot3_short(left, right, dims):
    rows = left[0].shape[0]
    both = mm(jnp.concatenate(left, axis=0), right[0], dims)
    return both[:rows] + both[rows:] + mm(left[0], right[1], dims)


def stack_weight(parts):
    return jnp.concatenate([parts[0], parts[0], parts[1]], axis=0)


def stack_input(parts):
    return jnp.concatenate([parts[0], parts[1], parts[0]], axis=0)


def elu(value):
    return jnp.where(value > 0, value, jnp.exp(jnp.minimum(value, 0.0)) - 1.0)


def elu_slope(result):
    return jnp.where(result > 0, 1.0, result + 1.0)


def fold(value):
    total = value[:, :LANES]
    for at in range(LANES, value.shape[1], LANES):
        total = total + value[:, at : at + LANES]
    return total


def spread_lanes(column, width):
    return jnp.concatenate([column] * (width // LANES), axis=1)


def columns_of(rows):
    count = len(rows)
    deep = up(3 * count, 16)
    value = jnp.concatenate(rows, axis=0)
    first = value.astype(bf16)
    rest = value - first.astype(f32)
    second = rest.astype(bf16)
    third = (rest - second.astype(f32)).astype(bf16)
    parts = [first.astype(f32), second.astype(f32), third.astype(f32)]
    if deep > 3 * count:
        parts.append(jnp.zeros((deep - 3 * count, value.shape[1]), f32))
    stacked = jnp.concatenate(parts, axis=0).astype(bf16)
    at = lax.broadcasted_iota(jnp.int32, (deep, count * LANES), 0)
    lane = lax.broadcasted_iota(jnp.int32, (deep, count * LANES), 1)
    block = lane // LANES
    pick = ((at == block) | (at == block + count) | (at == block + 2 * count)) & (at < 3 * count)
    return mm(stacked, pick.astype(f32).astype(bf16), TN)


def rows_of(blocks):
    count = len(blocks)
    high, low = split(jnp.concatenate(blocks, axis=1))
    at = lax.broadcasted_iota(jnp.int32, (16, count * LANES), 0)
    lane = lax.broadcasted_iota(jnp.int32, (16, count * LANES), 1)
    pick = (lane // LANES == at).astype(f32).astype(bf16)
    return mm(pick, high, NT) + mm(pick, low, NT)


def decay_row(horizon, width, factor):
    return jnp.concatenate(
        [jnp.full((1, width), factor * decay_rate**step, f32) for step in range(horizon)], axis=1
    )


def first_lane(total, width):
    lane = lax.broadcasted_iota(jnp.int32, (1, width), 1)
    return jnp.where(lane == 0, total, 0.0)


def row(ref):
    return ref[...].reshape(1, ref.shape[-1])


class Sizes:
    def __init__(self, obs_next, actions, enc_w1, dyn_w1):
        self.horizon, self.obs, self.seqs = obs_next.shape
        self.act = actions.shape[1]
        self.hidden = enc_w1.shape[1]
        joined, self.mlp = dyn_w1.shape
        self.lat = joined - self.act
        self.one = joined
        self.deep = up(joined + 1, 16)
        self.obs_deep = up(self.obs + 1, 16)
        self.lat_deep = up(self.lat, 16)
        self.act_deep = up(self.act, 16)
        self.cols = self.horizon * self.seqs
        self.net_rows = self.mlp + self.deep
        self.at_w3 = self.net_rows
        self.at_enc = self.at_w3 + up(self.lat, 8)
        self.at_prio = self.at_enc + up(max(self.lat, self.obs_deep + 1), 16)

    def dyn_rows(self, total):
        self.prio_rows = up(-(-total // self.mlp), 8)
        return up(self.at_prio + self.prio_rows, 64)


def places():
    dp = lax.axis_index("dp")
    pb = lax.axis_index("pb")
    core = lax.rem(dp, 2)
    side = lax.rem(lax.div(dp, 2), 2)
    return dp, pb, core, side


def square(relative):
    dp, pb, core, side = places()
    return lax.rem(side + relative // 2, 2) * 2 + lax.rem(pb + relative % 2, 2)


def pack_kernel(w1, b1, gain, shift, w2, b2, w3, b3, out):
    mlp = w2.shape[1]
    joined = w1.shape[1]
    half = out.shape[0]
    core = places()[2]

    @pl.when(core == 0)
    def _():
        out[...] = w2[0, :half]

    @pl.when(core == 1)
    def _():
        at = mlp - half
        out[:at] = w2[0, half:]
        out[at : at + joined] = w1[0]
        at = at + joined
        out[at:] = jnp.zeros((half - at, mlp), f32)
        for ref in (b1, gain, shift, b2, w3):
            out[at : at + 1] = ref[...]
            at = at + 1
        out[at : at + 1] = jnp.full((1, mlp), b3[0], f32)


def rollout_kernel(
    size,
    scale,
    obs_first,
    obs_next,
    actions,
    rewards,
    enc_w1,
    enc_b1,
    enc_w2,
    enc_b2,
    dyn_w1,
    dyn_b1,
    dyn_w2,
    dyn_b2,
    dyn_w3,
    dyn_b3,
    rew_w1,
    rew_b1,
    rew_w2,
    rew_b2,
    rew_w3,
    rew_b3,
    joint,
    keep0,
    keep1,
    keep2,
    keep3,
    send0,
    send1,
    send2,
    send3,
    state_grad,
    consist,
    dyn_h1,
    dyn_h2,
    enc_h,
    obs_aug,
    w_aug,
    w_out,
    e_aug,
    e_out,
    reward_grads,
    dyn_square,
    rew_square,
    sems,
):
    lat, act, one, deep = size.lat, size.act, size.one, size.deep
    mlp, seqs, cols, horizon = size.mlp, size.seqs, size.cols, size.horizon
    joined = lat + act
    dp, pb, core, side = places()
    fetch = [
        pltpu.make_async_copy(dyn_w2, dyn_square, sems.at[0]),
        pltpu.make_async_copy(rew_w2, rew_square, sems.at[1]),
    ]
    for copy in fetch:
        copy.start()

    def first_weight(ref, bias, kept):
        w_aug[...] = jnp.zeros_like(w_aug)
        w_aug[:kept] = ref[...]
        w_aug[one : one + 1] = row(bias)
        return split(w_aug[...])

    obs_aug[...] = jnp.zeros_like(obs_aug)
    for step in range(horizon):
        obs_aug[: size.obs, step * seqs : (step + 1) * seqs] = obs_next[step]
    obs_aug[: size.obs, cols:] = obs_first[...]
    obs_aug[size.obs : size.obs + 1] = jnp.ones((1, cols + seqs), f32)
    e_aug[...] = jnp.zeros_like(e_aug)
    e_aug[: size.obs] = enc_w1[...]
    e_aug[size.obs : size.obs + 1] = row(enc_b1)
    e_out[...] = jnp.zeros_like(e_out)
    e_out[:lat] = enc_w2[...]
    w_out[...] = jnp.zeros_like(w_out)
    w_out[:lat] = dyn_w3[...]
    small = jnp.concatenate(
        [
            jnp.concatenate([row(enc_b2), jnp.zeros((1, LANES - lat), f32)], axis=1),
            jnp.concatenate([row(dyn_b3), jnp.zeros((1, LANES - lat), f32)], axis=1),
        ],
        axis=0,
    )
    small = columns_of([small[0:1], small[1:2]])
    enc_b2_col = small[: size.lat_deep, :LANES]
    dyn_b3_col = small[: size.lat_deep, LANES:]
    wide = columns_of([row(dyn_b2), row(rew_b2), row(rew_w3)])
    dyn_b2_col = wide[:, :LANES]

    enc_first = mm(stack_weight(split(e_aug[...])), stack_input(split(obs_aug[...])), TN)
    enc_hidden = elu(enc_first)
    enc_h[...] = enc_hidden[:, cols:]
    latent = dot3(split(e_out[...]), split(enc_hidden), NN) + spread_lanes(
        enc_b2_col, cols + seqs
    )
    joint[:, :] = jnp.zeros_like(joint)
    joint[: size.lat_deep, 2 * cols :] = latent[:, :cols]
    for step in range(horizon):
        joint[lat : lat + act, step * seqs : (step + 1) * seqs] = actions[step]
    joint[one : one + 1] = jnp.ones((1, 3 * cols), f32)

    first = stack_weight(first_weight(dyn_w1, dyn_b1, joined))
    fetch[0].wait()
    second = split(dyn_square[...].T)
    third = split(w_out[...])
    latent = latent[:, cols:]
    for step in range(horizon):
        here = slice(step * seqs, (step + 1) * seqs)
        joint[:lat, here] = latent[:lat]
        hidden = elu(mm(first, stack_input(split(joint[:, here])), TN))
        dyn_h1[:, here] = hidden
        hidden = elu(dot3_narrow(second, split(hidden), NN) + dyn_b2_col)
        dyn_h2[:, here] = hidden
        latent = dot3_narrow(third, split(hidden), NN) + dyn_b3_col
        after = 2 * cols + step * seqs
        goal = joint[: size.lat_deep, after : after + seqs]
        factor = scale * decay_rate**step * consist_coef * 2.0 / lat
        consist[:, here] = factor * (latent - goal)

    states = split(joint[:, :cols])
    first = first_weight(rew_w1, rew_b1, joined)
    fetch[1].wait()
    second = split(rew_square[...])
    b2_col = spread_lanes(wide[:, LANES : 2 * LANES], cols)
    w3_col = spread_lanes(wide[:, 2 * LANES : 3 * LANES], cols)
    h1 = elu(mm(stack_weight(first), stack_input(states), TN))
    h1_parts = split(h1)
    h2 = elu(dot3(second, h1_parts, TN) + b2_col)
    predicted = jnp.sum(w3_col * h2, axis=0, keepdims=True) + rew_b3[0]
    wanted = jnp.concatenate([rewards[step : step + 1] for step in range(horizon)], axis=1)
    out_grad = decay_row(horizon, seqs, scale * reward_coef * 2.0) * (predicted - wanted)
    h2_grad = w3_col * out_grad * elu_slope(h2)
    h2_parts = split(h2_grad)
    reward_grads[:mlp] = dot3(h1_parts, h2_parts, NT)
    h1_grad = dot3(second, h2_parts, NN) * elu_slope(h1)
    h1_grad = split(h1_grad)
    reward_grads[mlp:] = dot3(states, h1_grad, NT)
    state_grad[...] = dot3_short(first, h1_grad, NN)
    sums = rows_of([fold(h2_grad), fold(h2 * out_grad)])
    reward_grads[mlp + one + 1 : mlp + one + 3] = sums[:2]
    reward_grads[mlp + one + 3 : mlp + one + 4] = first_lane(jnp.sum(out_grad), mlp)

    eighth = size.net_rows // 8
    for h in range(2):
        place = core if h == 0 else 1 - core
        for k in range(4):
            out = ((keep0, keep1, keep2, keep3), (send0, send1, send2, send3))[h][k]
            start = (place * 4 + square(k)) * eighth
            out[...] = reward_grads[pl.ds(pl.multiple_of(start, 8), eighth)]


def act_kernel(
    size,
    begun,
    pol_w1,
    pol_b1,
    pol_w2,
    pol_b2,
    pol_w3,
    pol_b3,
    joint,
    pol_h1,
    pol_h2,
    w_aug,
    w_act,
):
    lat, act, one = size.lat, size.act, size.one
    cols = size.cols
    joined = lat + act
    joint[...] = begun[...]
    w_act[...] = jnp.zeros_like(w_act)
    w_act[:act] = pol_w3[...]
    small = jnp.concatenate([row(pol_b3), jnp.zeros((1, LANES - act), f32)], axis=1)
    pol_b3_col = columns_of([small])[: size.act_deep]
    b2_col = spread_lanes(columns_of([row(pol_b2)]), cols)
    w_aug[...] = jnp.zeros_like(w_aug)
    w_aug[:lat] = pol_w1[...]
    w_aug[one : one + 1] = row(pol_b1)
    first = stack_weight(split(w_aug[...]))
    second = split(pol_w2[...])
    third = split(w_act[...])
    for block in (0, 2):
        here = slice(block * cols, (block + 1) * cols)
        h1 = elu(mm(first, stack_input(split(joint[:, here])), TN))
        h2 = elu(dot3(second, split(h1), TN) + b2_col)
        action = jnp.tanh(dot3(third, split(h2), NN) + spread_lanes(pol_b3_col, cols))[:act]
        if block == 0:
            pol_h1[...] = h1
            pol_h2[...] = h2
            joint[:lat, cols : 2 * cols] = joint[:lat, :cols]
            joint[lat:joined, cols : 2 * cols] = action
        else:
            joint[lat:joined, here] = action


def value_kernel(
    size,
    scale,
    joint,
    rewards,
    q_w1,
    q_b1,
    q_gain,
    q_shift,
    q_w2,
    q_b2,
    q_w3,
    q_b3,
    packed_y,
    packed_c,
    keep0,
    keep1,
    keep2,
    keep3,
    send0,
    send1,
    send2,
    send3,
    state_grad,
    chosen_grad,
    prio,
    packed,
    aug,
    w1_rows,
    w1_parts,
    w2_rows,
    w2_lanes,
    vectors,
    last,
    inputs,
    next_value,
    spread,
    grads,
    work,
    normed,
    second,
    hidden,
    backs,
    sums,
):
    lat, act, one, deep = size.lat, size.act, size.one, size.deep
    mlp, seqs, cols, horizon = size.mlp, size.seqs, size.cols, size.horizon
    joined = lat + act
    dp, pb, core, side = places()
    half = packed_y.shape[0]
    packed[pl.ds(pl.multiple_of(core * half, 8), half)] = packed_y[...]
    packed[pl.ds(pl.multiple_of((1 - core) * half, 8), half)] = packed_c[...]

    at = mlp + joined
    for slot in range(TWIN):
        if slot == 0:
            w1, b1, w2 = q_w1[0], q_b1[...], q_w2[0]
            rows = [q_gain[...], q_shift[...], q_b2[...], q_w3[...]]
            b3 = jnp.full((1, LANES), q_b3[0], f32)
        else:
            w1, b1, w2 = packed[mlp:at], packed[at : at + 1], packed[:mlp]
            rows = [packed[at + i : at + i + 1] for i in (1, 2, 3, 4)]
            b3 = packed[at + 5 : at + 6, :LANES]
        aug[...] = jnp.zeros_like(aug)
        aug[:joined] = w1
        aug[one : one + 1] = b1
        high, low = split(aug[...])
        for place, part in enumerate((high, high, low)):
            w1_rows[slot, place * deep : (place + 1) * deep] = part
            if place > 0:
                w1_parts[slot, (place - 1) * deep : place * deep] = part
        high, low = split(w2)
        for place, part in enumerate((high, high, low)):
            w2_rows[slot, place * mlp : (place + 1) * mlp] = part
            w2_lanes[slot, :, place * mlp : (place + 1) * mlp] = part
        vectors[slot] = columns_of(rows)
        last[slot] = b3
    inputs[...] = stack_input(split(joint[...]))

    height = 32

    def blocks(width):
        for left in range(0, width, cols):
            for top in range(0, mlp, height):
                yield slice(top, top + height), slice(left, left + cols)

    def column(slot, which, rows):
        return spread_lanes(vectors[slot, rows, which * LANES : (which + 1) * LANES], cols)

    def keep_parts(ref, rows, here, value):
        high, low = split(value)
        for place, part in enumerate((high, low, high)):
            ref[rows.start + place * mlp : rows.stop + place * mlp, here] = part

    def added(totals, here, value):
        eight = value.reshape(height // 8, 8, cols).sum(axis=0)
        at = here.start // cols
        totals[at] = eight if totals[at] is None else totals[at] + eight

    def total_of(totals):
        return jnp.concatenate([jnp.sum(t, axis=0, keepdims=True) for t in totals], axis=1)

    def forward(slot, start, width, kept):
        work[:, :width] = mm(w1_rows[slot], inputs[:, start : start + width], TN)
        totals = [None] * (width // cols)
        for rows, here in blocks(width):
            added(totals, here, work[rows, here])
        mean = total_of(totals) / mlp
        totals = [None] * (width // cols)
        for rows, here in blocks(width):
            center = work[rows, here] - mean[:, here]
            added(totals, here, center * center)
        inverse = lax.rsqrt(total_of(totals) / mlp + norm_epsilon)
        for rows, here in blocks(width):
            value = (work[rows, here] - mean[:, here]) * inverse[:, here]
            if kept:
                normed[rows, here] = value
            value = jnp.tanh(column(slot, 0, rows) * value + column(slot, 1, rows))
            keep_parts(hidden, rows, here, value)
        work[:, :width] = mm(w2_rows[slot], hidden[:, :width], TN)
        totals = [None] * (width // cols)
        for rows, here in blocks(width):
            value = elu(work[rows, here] + column(slot, 2, rows))
            if kept:
                second[rows, here] = value
            if here.start == 0:
                added(totals, here, column(slot, 3, rows) * value)
        return total_of(totals[:1]) + spread_lanes(last[slot], cols), inverse

    for slot in range(TWIN):
        next_value[slot] = forward(slot, 2 * cols, cols, False)[0]

    wanted = jnp.concatenate([rewards[step : step + 1] for step in range(horizon)], axis=1)
    next_value[0] = wanted + discount * jnp.minimum(next_value[0], next_value[1])
    spread[...] = jnp.zeros_like(spread)
    state_grad[...] = jnp.zeros_like(state_grad)
    chosen_grad[...] = jnp.zeros_like(chosen_grad)

    for slot in range(TWIN):
        value, inverse = forward(slot, 0, 2 * cols, True)
        error = value - next_value[0]
        spread[...] += jnp.sqrt(error * error + 1.0)
        out_grad = jnp.concatenate(
            [
                decay_row(horizon, seqs, scale * value_coef * 2.0) * error,
                decay_row(horizon, seqs, -policy_coef * 0.5 * scale),
            ],
            axis=1,
        )
        for rows, here in blocks(2 * cols):
            result = second[rows, here]
            back = column(slot, 3, rows) * out_grad[:, here] * elu_slope(result)
            keep_parts(backs, rows, here, back)
            if here.start == 0:
                sums[rows, :LANES] = fold(back)
                sums[rows, 3 * LANES :] = fold(result * out_grad[:, here])
        work[...] = mm(w2_lanes[slot], backs[...], NN)
        grads[slot, :mlp] = dot3(
            (hidden[:mlp, :cols], hidden[mlp : 2 * mlp, :cols]),
            (backs[:mlp, :cols], backs[mlp : 2 * mlp, :cols]),
            NT,
        )
        plain, along = [None] * 2, [None] * 2
        for rows, here in blocks(2 * cols):
            high = hidden[rows, here].astype(f32)
            low = hidden[mlp + rows.start : mlp + rows.stop, here].astype(f32)
            result = high + low
            pre = work[rows, here] * (1.0 - result * result)
            unit = normed[rows, here]
            if here.start == 0:
                sums[rows, LANES : 2 * LANES] = fold(pre * unit)
                sums[rows, 2 * LANES : 3 * LANES] = fold(pre)
            back = column(slot, 0, rows) * pre
            work[rows, here] = back
            added(plain, here, back)
            added(along, here, back * unit)
        plain, along = total_of(plain) / mlp, total_of(along) / mlp
        for rows, here in blocks(2 * cols):
            back = work[rows, here] - plain[:, here] - normed[rows, here] * along[:, here]
            keep_parts(backs, rows, here, back * inverse[:, here])
        states = (inputs[:deep, :cols], inputs[deep : 2 * deep, :cols])
        first_parts = (backs[:mlp, :cols], backs[mlp : 2 * mlp, :cols])
        grads[slot, mlp:] = dot3(states, first_parts, NT)
        both = mm(w1_parts[slot], backs[:mlp], NN)
        into = both[:deep] + both[deep:] + mm(w1_parts[slot, :deep], backs[mlp : 2 * mlp], NN)
        state_grad[...] += into[:, :cols]
        chosen_grad[...] += into[:, cols:]
        lines = rows_of([sums[:, at * LANES : (at + 1) * LANES] for at in range(4)])
        grads[slot, mlp + one + 1 : mlp + one + 5] = lines[:4]
        grads[slot, mlp + one + 5 : mlp + one + 6] = first_lane(jnp.sum(out_grad[:, :cols]), mlp)

    total = spread[:, :seqs]
    for step in range(1, horizon):
        total = total + spread[:, step * seqs : (step + 1) * seqs]
    prio[...] = total / (TWIN * horizon)

    quarter = size.net_rows // 4
    for h in range(2):
        place = core if h == 0 else 1 - core
        for k in range(4):
            out = ((keep0, keep1, keep2, keep3), (send0, send1, send2, send3))[h][k]
            start = (place * 2 + lax.div(square(k), 2)) * quarter
            out[...] = grads[k % 2, pl.ds(pl.multiple_of(start, 8), quarter)]


def policy_kernel(
    size, pol_w2, pol_w3, joint, pol_h1, pol_h2, chosen_grad, pol, w_act, act_grad
):
    lat, act, one = size.lat, size.act, size.one
    mlp, cols = size.mlp, size.cols
    joined = lat + act
    states = split(joint[:, :cols])
    w_act[...] = jnp.zeros_like(w_act)
    w_act[:act] = pol_w3[...]
    act_grad[...] = jnp.zeros_like(act_grad)
    chosen = joint[lat:joined, cols : 2 * cols]
    act_grad[:act] = chosen_grad[lat:joined] * (1.0 - chosen * chosen)
    out_parts = split(act_grad[...])
    weight = split(w_act[...])
    h2 = pol_h2[...]
    h2_grad = mm(stack_weight(weight), stack_input(out_parts), TN) * elu_slope(h2)
    h2_parts = split(h2_grad)
    h1 = pol_h1[...]
    pol[:mlp] = dot3(split(h1), h2_parts, NT)
    h1_grad = dot3(split(pol_w2[...]), h2_parts, NN) * elu_slope(h1)
    pol[mlp:] = dot3(states, split(h1_grad), NT)
    pol[mlp + lat : mlp + joined] = dot3(out_parts, split(h2), NT)[:act]
    pol[mlp + one + 1 : mlp + one + 2] = rows_of([fold(h2_grad)])[:1]
    sums = rows_of([fold(act_grad[...])])
    pol[mlp + one + 2 : mlp + one + 3] = jnp.zeros((1, mlp), f32)
    pol[mlp + one + 2 : mlp + one + 3, : size.act_deep] = sums[:1]


def shared_kernel(
    size,
    scale,
    total,
    obs_first,
    enc_w1,
    enc_w2,
    dyn_w1,
    dyn_w2,
    dyn_w3,
    joint,
    reward_state,
    consist,
    dyn_h1,
    dyn_h2,
    enc_h,
    value_state,
    prio,
    pol,
    keep0,
    keep1,
    keep2,
    keep3,
    send0,
    send1,
    send2,
    send3,
    obs_grad,
    obs_aug,
    w_out,
    e_out,
    lat_grad,
    second_high,
    second_low,
    first_high,
    first_low,
    dyn,
):
    lat, act, one, deep = size.lat, size.act, size.one, size.deep
    mlp, seqs, cols, horizon = size.mlp, size.seqs, size.cols, size.horizon
    joined = lat + act
    lat_deep, hidden = size.lat_deep, size.hidden
    dp, pb, core, side = places()
    states = split(joint[:, :cols])

    w_out[...] = jnp.zeros_like(w_out)
    w_out[:lat] = dyn_w3[...]
    third = stack_weight(split(w_out[...]))
    second = split(dyn_w2[...])
    first = split(dyn_w1[...])
    lat_rows = lax.broadcasted_iota(jnp.int32, (lat_deep, seqs), 0)
    carry = None
    for step in reversed(range(horizon)):
        here = slice(step * seqs, (step + 1) * seqs)
        grad = consist[:, here]
        if carry is not None:
            after = slice((step + 1) * seqs, (step + 2) * seqs)
            grad = grad + carry + reward_state[:lat_deep, after] + value_state[:lat_deep, after]
            grad = jnp.where(lat_rows < lat, grad, 0.0)
        lat_grad[:, here] = grad
        high, low = split(grad)
        h2_grad = mm(third, jnp.concatenate([high, low, high], axis=0), TN)
        h2_grad = h2_grad * elu_slope(dyn_h2[:, here])
        parts = split(h2_grad)
        second_high[:, here], second_low[:, here] = parts
        h1_grad = dot3_narrow(second, parts, NN) * elu_slope(dyn_h1[:, here])
        parts = split(h1_grad)
        first_high[:, here], first_low[:, here] = parts
        back = dot3_narrow(first, parts, NN)
        carry = jnp.concatenate([back, jnp.zeros((lat_deep - joined, seqs), f32)], axis=0)
    grad = carry + reward_state[:lat_deep, :seqs] + value_state[:lat_deep, :seqs]
    grad = jnp.where(lat_rows < lat, grad, 0.0)
    second_parts = (second_high[...], second_low[...])
    first_parts = (first_high[...], first_low[...])
    dyn[:mlp] = dot3(split(dyn_h1[...]), second_parts, NT)
    dyn[mlp : size.net_rows] = dot3(states, first_parts, NT)
    out_grad = lat_grad[...]
    b2_sum = fold(second_high[...].astype(f32) + second_low[...].astype(f32))
    dyn[size.at_w3 : size.at_enc] = dot3(split(out_grad), split(dyn_h2[...]), NT)[
        : size.at_enc - size.at_w3
    ]
    dyn[mlp + one + 1 : mlp + one + 2] = rows_of([b2_sum])[:1]
    dyn[mlp + one + 2 : mlp + one + 3] = jnp.zeros((1, mlp), f32)
    dyn[mlp + one + 2 : mlp + one + 3, :lat_deep] = rows_of([fold(out_grad)])[:1]

    dyn[size.at_enc :] = jnp.zeros((dyn.shape[0] - size.at_enc, mlp), f32)
    obs_aug[...] = jnp.zeros_like(obs_aug)
    obs_aug[: size.obs] = obs_first[...]
    obs_aug[size.obs : size.obs + 1] = jnp.ones((1, seqs), f32)
    e_out[...] = jnp.zeros_like(e_out)
    e_out[:lat] = enc_w2[...]
    parts = split(grad)
    h = enc_h[...]
    h_grad = dot3(split(e_out[...]), parts, TN) * elu_slope(h)
    h_parts = split(h_grad)
    dyn[size.at_enc : size.at_enc + lat_deep, :hidden] = dot3(parts, split(h), NT)
    dyn[size.at_enc : size.at_enc + size.obs_deep, hidden : 2 * hidden] = dot3(
        split(obs_aug[...]), h_parts, NT
    )
    at = size.at_enc + size.obs_deep
    dyn[at : at + 1, hidden : hidden + lat_deep] = rows_of([grad])[:1]
    obs_grad[...] = total * dot3(split(enc_w1[...]), h_parts, NN)

    index = (dp * 2 + pb) * seqs
    rows = size.prio_rows
    at = lax.broadcasted_iota(jnp.int32, (rows, mlp), 0) * mlp
    at = at + lax.broadcasted_iota(jnp.int32, (rows, mlp), 1)
    mine = (at >= index) & (at < index + seqs)
    value = jnp.concatenate([prio[...]] * (mlp // seqs), axis=1)
    dyn[size.at_prio : size.at_prio + rows] = jnp.where(mine, value, 0.0)

    small, large = size.net_rows // 8, dyn.shape[0] // 8
    for h in range(2):
        place = core if h == 0 else 1 - core
        for k in range(4):
            out = ((keep0, keep1, keep2, keep3), (send0, send1, send2, send3))[h][k]
            start = (place * 4 + square(k)) * small
            out[:small] = pol[pl.ds(pl.multiple_of(start, 8), small)]
            start = (place * 4 + square(k)) * large
            out[small:] = dyn[pl.ds(pl.multiple_of(start, 8), large)]


def halve_kernel(*refs):
    for k in range(4):
        refs[8 + k][...] = refs[k][...] + refs[4 + k][...]


def sum_kernel(*refs):
    total = refs[0][...]
    for ref in refs[1:-1]:
        total = total + ref[...]
    refs[-1][...] = total


def lane_half(other):
    mine = lax.rem(lax.div(lax.axis_index("dp"), 4), 2)
    at = 1 - mine if other else mine
    return pl.ds(pl.multiple_of(at * 256, 256), 256)


def cut_kernel(*refs):
    *summed, own, from_x, from_y, from_xy, mine, other, whole = refs
    at = 0
    for ref in summed:
        whole[at : at + ref.shape[0]] = ref[...]
        at = at + ref.shape[0]
    whole[at:] = (own[...] + from_x[...]) + (from_y[...] + from_xy[...])
    mine[...] = whole[:, lane_half(False)]
    other[...] = whole[:, lane_half(True)]


def rejoin_kernel(mine, other, *outs):
    for out in outs:
        out[:, lane_half(False)] = mine[: out.shape[0]]
        out[:, lane_half(True)] = other[: out.shape[0]]


def collect(out, pieces, first, rows, core, side, pb):
    for h in range(2):
        for k in range(4):
            place = lax.rem(core + h, 2) * 4 + lax.rem(side + k // 2, 2) * 2 + lax.rem(pb + k, 2)
            out[pl.ds(pl.multiple_of(place * rows, 8), rows)] = pieces[h][k][first : first + rows]


def finish_value_kernel(
    size,
    own,
    from_x,
    from_y,
    from_xy,
    c_own,
    c_x,
    c_y,
    c_xy,
    rew_w1,
    rew_b1,
    rew_w2,
    rew_b2,
    rew_w3,
    rew_b3,
    q_w1,
    q_b1,
    q_gain,
    q_shift,
    q_w2,
    q_b2,
    q_w3,
    q_b3,
    rew,
    twin,
):
    dp, pb, core, side = places()
    mlp, one = size.mlp, size.one
    eighth, quarter = size.net_rows // 8, size.net_rows // 4
    pieces = ((own, from_y, from_x, from_xy), (c_own, c_y, c_x, c_xy))
    collect(rew, pieces, 0, eighth, core, side, pb)
    for h in range(2):
        for k in range(2):
            place = lax.rem(core + h, 2) * 2 + lax.rem(side + k, 2)
            twin[pl.ds(pl.multiple_of(place * quarter, 8), quarter)] = pieces[h][2 * k][eighth:]
    rew_w2[...] = rew[:mlp]
    rew_w1[...] = rew[mlp : mlp + one]
    for ref, at in ((rew_b1, 0), (rew_b2, 1), (rew_w3, 2), (rew_b3, 3)):
        n = ref.shape[0]
        ref[...] = rew[mlp + one + at : mlp + one + at + 1, :n].reshape(n)
    q_w2[0] = twin[:mlp]
    q_w1[0] = twin[mlp : mlp + one]
    for at, ref in enumerate((q_b1, q_b2, q_gain, q_shift, q_w3)):
        ref[...] = twin[mlp + one + at : mlp + one + at + 1]
    q_b3[...] = twin[mlp + one + 5 : mlp + one + 6, :1].reshape(1)


def finish_shared_kernel(
    size,
    own,
    from_x,
    from_y,
    from_xy,
    c_own,
    c_x,
    c_y,
    c_xy,
    enc_w1,
    enc_b1,
    enc_w2,
    enc_b2,
    dyn_w1,
    dyn_b1,
    dyn_w2,
    dyn_b2,
    dyn_w3,
    dyn_b3,
    pol_w1,
    pol_b1,
    pol_w2,
    pol_b2,
    pol_w3,
    pol_b3,
    prio,
    pol,
    dyn,
):
    dp, pb, core, side = places()
    mlp, one, lat, act, hidden = size.mlp, size.one, size.lat, size.act, size.hidden
    pieces = ((own, from_y, from_x, from_xy), (c_own, c_y, c_x, c_xy))
    small, large = size.net_rows // 8, dyn.shape[0] // 8
    collect(pol, pieces, 0, small, core, side, pb)
    collect(dyn, pieces, small, large, core, side, pb)

    def line(out, source, at, first=0):
        n = out.shape[0]
        out[...] = source[at : at + 1, first : first + n].reshape(n)

    pol_w2[...] = pol[:mlp]
    pol_w1[...] = pol[mlp : mlp + lat]
    pol_w3[...] = pol[mlp + lat : mlp + lat + act]
    line(pol_b1, pol, mlp + one)
    line(pol_b2, pol, mlp + one + 1)
    line(pol_b3, pol, mlp + one + 2)
    dyn_w2[...] = dyn[:mlp]
    dyn_w1[...] = dyn[mlp : mlp + one]
    dyn_w3[...] = dyn[size.at_w3 : size.at_w3 + lat]
    line(dyn_b1, dyn, mlp + one)
    line(dyn_b2, dyn, mlp + one + 1)
    line(dyn_b3, dyn, mlp + one + 2)
    enc_w2[...] = dyn[size.at_enc : size.at_enc + lat, :hidden]
    enc_w1[...] = dyn[size.at_enc : size.at_enc + size.obs, hidden : 2 * hidden]
    line(enc_b1, dyn, size.at_enc + size.obs, hidden)
    line(enc_b2, dyn, size.at_enc + size.obs_deep, hidden)
    for at in range(prio.shape[0] // mlp):
        line(prio.at[at * mlp : (at + 1) * mlp], dyn, size.at_prio + at)


VMEM = pl.BlockSpec(memory_space=pltpu.VMEM)
SMEM = pl.BlockSpec(memory_space=pltpu.SMEM)


ANY = pl.BlockSpec(memory_space=pl.ANY)


def call(
    kernel, name, outs, args, scratch=(), scalars=(), left=(), after=(), mega=16
):
    def made(shape):
        return jax.ShapeDtypeStruct(shape, f32)

    def ordered(*refs):
        return kernel(*refs[: len(args)], *refs[len(args) + len(after) :])

    single = not isinstance(outs, list)
    shapes = [made(shape) for shape in ([outs] if single else outs)]
    specs = [SMEM if at in scalars else ANY if at in left else VMEM for at in range(len(args))]
    return pl.pallas_call(
        ordered,
        out_shape=shapes[0] if single else shapes,
        in_specs=specs + [ANY] * len(after),
        out_specs=VMEM if single else [VMEM] * len(shapes),
        scratch_shapes=list(scratch),
        compiler_params=pltpu.CompilerParams(vmem_limit_bytes=mega * 2**20),
        cost_estimate=pl.CostEstimate(flops=1, bytes_accessed=1, transcendentals=0),
        name=name,
    )(*args, *after)


def flipped(axis, bit):
    count = lax.axis_size(axis)
    return [(at, at ^ (1 << bit)) for at in range(count)]


def on_device(*args):
    a = dict(zip(NAMES, args))
    size = Sizes(a["obs_next"], a["actions"], a["enc_w1"], a["dyn_w1"])
    n_dp, n_pb = lax.axis_size("dp"), lax.axis_size("pb")
    total = size.seqs * n_dp * n_pb
    scale = 1.0 / total
    mlp, cols, seqs, deep = size.mlp, size.cols, size.seqs, size.deep
    dyn_rows = size.dyn_rows(total)
    net_rows = size.net_rows
    joined = size.lat + size.act

    def swap_core(block):
        return lax.ppermute(block, "dp", flipped("dp", 0))

    def swap_x(block):
        return lax.ppermute(block, "dp", flipped("dp", 1))

    def swap_y(block):
        return lax.ppermute(block, "pb", flipped("pb", 0))

    def swap_xy(block):
        route = []
        for dp in range(n_dp):
            for pb in range(n_pb):
                route.append((dp * n_pb + pb, (dp ^ 2) * n_pb + (pb ^ 1)))
        return lax.ppermute(block, ("dp", "pb"), route)

    def shape(rows, width, kind=f32):
        return pltpu.VMEM((rows, width), kind)

    def to_square(block):
        return [swap_x(block[0]), swap_y(block[1]), swap_xy(block[2])]

    def swap_z(block):
        return lax.ppermute(block, "dp", flipped("dp", 2))

    def swapped(parts):
        return parts[:4] + [swap_core(part) for part in parts[4:]]

    def halve(name, parts, after=()):
        own, to_y, to_x, to_xy = call(
            halve_kernel, name, [parts[0].shape] * 4, parts, after=after
        )
        return [own] + to_square((to_x, to_y, to_xy))

    def cut(name, parts, after=()):
        rows = sum(part.shape[0] for part in parts[:-3])
        mine, other = call(
            cut_kernel,
            name,
            [(rows, mlp // 2)] * 2,
            parts,
            scratch=[shape(rows, mlp)],
            after=after,
        )
        return [mine, swap_z(other)]

    def further_z(name, parts):
        for bit in range(3, n_dp.bit_length() - 1):
            whole = call(sum_kernel, name, parts[0].shape, parts)
            parts = [whole, lax.ppermute(whole, "dp", flipped("dp", bit))]
        return parts

    def back_z(name, parts, after=()):
        whole = call(sum_kernel, name, parts[0].shape, parts, after=after)
        return [whole, swap_z(whole)]

    def rejoin(name, parts, head, after=()):
        rows = parts[0].shape[0]
        outs = [(rows, mlp)] + ([(head, mlp)] if head < rows else [])
        outs = call(rejoin_kernel, name, outs, parts, after=after)
        return [outs[0]] + to_square([outs[0], outs[-1], outs[-1]])

    def both_cores(parts):
        return parts + [swap_core(part) for part in parts]

    q = [a[n] for n in NAMES[26:]]
    packed = call(
        pack_kernel,
        "pack",
        (net_rows // 2, mlp),
        q,
        scalars=(7,),
        mega=63,
    )
    packed_y = swap_y(packed)

    eighth = net_rows // 8
    begun, *reward, reward_state, consist, dyn_h1, dyn_h2, enc_h = call(
        functools.partial(rollout_kernel, size, scale),
        "rollout",
        [(deep, 3 * cols)]
        + [(eighth, mlp)] * 8
        + [(deep, cols), (size.lat_deep, cols), (mlp, cols), (mlp, cols), (size.hidden, seqs)],
        [a[n].T if n in TURNED else a[n] for n in NAMES[:20]],
        scratch=[
            shape(size.obs_deep, cols + seqs),
            shape(deep, mlp),
            shape(size.lat_deep, mlp),
            shape(size.obs_deep, size.hidden),
            shape(size.lat_deep, size.hidden),
            shape(net_rows, mlp),
            shape(mlp, mlp),
            shape(mlp, mlp),
            pltpu.SemaphoreType.DMA((2,)),
        ],
        scalars=(19,),
        left=(10, 16),
        mega=50,
    )
    packed_y, begun = lax.optimization_barrier((packed_y, begun))
    packed_c = swap_core(packed_y)
    reward = swapped(reward)
    joint, pol_h1, pol_h2 = call(
        functools.partial(act_kernel, size),
        "act",
        [(deep, 3 * cols), (mlp, cols), (mlp, cols)],
        [begun] + [a[n].T if n in TURNED else a[n] for n in NAMES[20:26]],
        scratch=[shape(deep, mlp), shape(size.act_deep, mlp)],
        mega=32,
    )
    reward = halve("reward_halve", reward, after=[pol_h1])

    rows = 2 * eighth
    *parts, value_state, chosen_grad, prio = call(
        functools.partial(value_kernel, size, scale),
        "value",
        [(rows, mlp)] * 8 + [(deep, cols), (deep, cols), (1, seqs)],
        [joint, a["rewards"]] + q + [packed_y, packed_c],
        scratch=[
            shape(net_rows, mlp),
            shape(deep, mlp),
            pltpu.VMEM((TWIN, 3 * deep, mlp), bf16),
            pltpu.VMEM((TWIN, 2 * deep, mlp), bf16),
            pltpu.VMEM((TWIN, 3 * mlp, mlp), bf16),
            pltpu.VMEM((TWIN, mlp, 3 * mlp), bf16),
            pltpu.VMEM((TWIN, mlp, 4 * LANES), f32),
            pltpu.VMEM((TWIN, 1, LANES), f32),
            shape(3 * deep, 3 * cols, bf16),
            pltpu.VMEM((TWIN, 1, cols), f32),
            shape(1, cols),
            pltpu.VMEM((TWIN, net_rows, mlp), f32),
            shape(mlp, 2 * cols),
            shape(mlp, 2 * cols),
            shape(mlp, 2 * cols),
            shape(3 * mlp, 2 * cols, bf16),
            shape(3 * mlp, 2 * cols, bf16),
            shape(mlp, 4 * LANES),
        ],
        scalars=(9,),
        after=[reward[0]],
        mega=40,
    )

    reward = call(sum_kernel, "reward_sum", reward[0].shape, reward, after=[prio])
    parts[4:], reward = lax.optimization_barrier((parts[4:], reward))
    parts = swapped(parts)
    value_rows, shared_rows = rows, eighth + dyn_rows // 8
    value = halve("value_halve", parts, after=[reward])
    pol = call(
        functools.partial(policy_kernel, size),
        "policy",
        (net_rows, mlp),
        [a["pol_w2"], a["pol_w3"].T, joint, pol_h1, pol_h2, chosen_grad],
        after=[value[0]],
        scratch=[shape(size.act_deep, mlp), shape(size.act_deep, cols)],
        mega=32,
    )

    *parts, obs_grad = call(
        functools.partial(shared_kernel, size, scale, total),
        "shared",
        [(shared_rows, mlp)] * 8 + [(size.obs, seqs)],
        [
            a["obs_first"],
            a["enc_w1"],
            a["enc_w2"].T,
            a["dyn_w1"],
            a["dyn_w2"],
            a["dyn_w3"].T,
            joint,
            reward_state,
            consist,
            dyn_h1,
            dyn_h2,
            enc_h,
            value_state,
            prio,
            pol,
        ],
        scratch=[
            shape(size.obs_deep, seqs),
            shape(size.lat_deep, mlp),
            shape(size.lat_deep, size.hidden),
            shape(size.lat_deep, cols),
            shape(mlp, cols, bf16),
            shape(mlp, cols, bf16),
            shape(mlp, cols, bf16),
            shape(mlp, cols, bf16),
            shape(dyn_rows, mlp),
        ],
        after=[value[0]],
        mega=32,
    )
    parts = swapped(parts)
    value = cut("value_cut", [reward] + value, after=[obs_grad])
    shared = halve("shared_halve", parts, after=[value[0]])
    value = further_z("value_further", value)
    value = back_z("value_back", value)
    shared = cut("shared_cut", shared, after=[value[0]])
    shared = further_z("shared_further", shared)
    value = rejoin("value_rejoin", value, eighth, after=[shared[0]])
    shared = back_z("shared_back", shared)
    shared = rejoin("shared_rejoin", shared, shared_rows, after=[value[0]])
    value = both_cores(value)
    value_grads = call(
        functools.partial(finish_value_kernel, size),
        "finish_value",
        [a[n].shape for n in NAMES[14:20]] + [a[n].shape for n in NAMES[26:]],
        value,
        scratch=[shape(net_rows, mlp), shape(net_rows, mlp)],
        after=[shared[0]],
    )
    shared, value_grads = lax.optimization_barrier((shared, value_grads))
    shared = both_cores(shared)
    names = NAMES[4:14] + NAMES[20:26]
    shared_grads = call(
        functools.partial(finish_shared_kernel, size),
        "finish_shared",
        [a[n].shape[::-1] if n in TURNED else a[n].shape for n in names] + [(total,)],
        shared,
        scratch=[shape(net_rows, mlp), shape(dyn_rows, mlp)],
    )
    shared_grads = list(shared_grads)
    for at, n in enumerate(names):
        if n in TURNED:
            shared_grads[at] = shared_grads[at].T
    return (
        tuple(shared_grads[:10])
        + tuple(value_grads[:6])
        + tuple(shared_grads[10:16])
        + tuple(value_grads[6:])
        + (obs_grad, shared_grads[-1])
    )


def solution(mesh):
    whole = P()
    seqs = ("dp", "pb")
    twin = (P("pb", None, None),) + (P("pb", None),) * 3 + (P("pb", None, None),)
    twin = twin + (P("pb", None), P("pb", None), P("pb"))
    placed = (P(None, seqs), P(None, None, seqs), P(None, None, seqs), P(None, seqs))
    return jax.shard_map(
        on_device,
        mesh=mesh,
        in_specs=placed + (whole,) * 22 + twin,
        out_specs=(whole,) * 22 + twin + (P(None, seqs), whole),
        check_vma=False,
    )
```

```python
import functools

import jax
import jax.numpy as jnp
from jax import lax
from jax.experimental import pallas as pl
from jax.experimental.pallas import tpu as pltpu
from jax.sharding import PartitionSpec as P

f32 = jnp.float32
bf16 = jnp.bfloat16

TWIN = 2
LANES = 128
decay_rate = 0.5
discount = 0.99
consist_coef = 2.0
reward_coef = 0.5
value_coef = 0.1
policy_coef = 0.1
norm_epsilon = 1e-05

TURNED = ("enc_w2", "dyn_w3", "pol_w3")
NN = ((1,), (0,))
NT = ((1,), (1,))
TN = ((0,), (0,))

NAMES = (
    "obs_first",
    "obs_next",
    "actions",
    "rewards",
    "enc_w1",
    "enc_b1",
    "enc_w2",
    "enc_b2",
    "dyn_w1",
    "dyn_b1",
    "dyn_w2",
    "dyn_b2",
    "dyn_w3",
    "dyn_b3",
    "rew_w1",
    "rew_b1",
    "rew_w2",
    "rew_b2",
    "rew_w3",
    "rew_b3",
    "pol_w1",
    "pol_b1",
    "pol_w2",
    "pol_b2",
    "pol_w3",
    "pol_b3",
    "q_w1",
    "q_b1",
    "q_gain",
    "q_shift",
    "q_w2",
    "q_b2",
    "q_w3",
    "q_b3",
)


def up(number, multiple):
    return -(-number // multiple) * multiple


def mm(left, right, dims):
    return lax.dot_general(left, right, (dims, ((), ())), preferred_element_type=f32)


def split(value):
    high = value.astype(bf16)
    return high, (value - high.astype(f32)).astype(bf16)


def dot3(left, right, dims):
    return (
        mm(left[0], right[0], dims) + mm(left[0], right[1], dims) + mm(left[1], right[0], dims)
    )


def dot3_narrow(left, right, dims):
    width = right[0].shape[1]
    both = mm(left[0], jnp.concatenate(right, axis=1), dims)
    return both[:, :width] + both[:, width:] + mm(left[1], right[0], dims)


def dot3_short(left, right, dims):
    rows = left[0].shape[0]
    both = mm(jnp.concatenate(left, axis=0), right[0], dims)
    return both[:rows] + both[rows:] + mm(left[0], right[1], dims)


def stack_weight(parts):
    return jnp.concatenate([parts[0], parts[0], parts[1]], axis=0)


def stack_input(parts):
    return jnp.concatenate([parts[0], parts[1], parts[0]], axis=0)


def elu(value):
    return jnp.where(value > 0, value, jnp.exp(jnp.minimum(value, 0.0)) - 1.0)


def elu_slope(result):
    return jnp.where(result > 0, 1.0, result + 1.0)


def fold(value):
    total = value[:, :LANES]
    for at in range(LANES, value.shape[1], LANES):
        total = total + value[:, at : at + LANES]
    return total


def spread_lanes(column, width):
    return jnp.concatenate([column] * (width // LANES), axis=1)


def columns_of(rows):
    count = len(rows)
    deep = up(3 * count, 16)
    value = jnp.concatenate(rows, axis=0)
    first = value.astype(bf16)
    rest = value - first.astype(f32)
    second = rest.astype(bf16)
    third = (rest - second.astype(f32)).astype(bf16)
    parts = [first.astype(f32), second.astype(f32), third.astype(f32)]
    if deep > 3 * count:
        parts.append(jnp.zeros((deep - 3 * count, value.shape[1]), f32))
    stacked = jnp.concatenate(parts, axis=0).astype(bf16)
    at = lax.broadcasted_iota(jnp.int32, (deep, count * LANES), 0)
    lane = lax.broadcasted_iota(jnp.int32, (deep, count * LANES), 1)
    block = lane // LANES
    pick = ((at == block) | (at == block + count) | (at == block + 2 * count)) & (at < 3 * count)
    return mm(stacked, pick.astype(f32).astype(bf16), TN)


def rows_of(blocks):
    count = len(blocks)
    high, low = split(jnp.concatenate(blocks, axis=1))
    at = lax.broadcasted_iota(jnp.int32, (16, count * LANES), 0)
    lane = lax.broadcasted_iota(jnp.int32, (16, count * LANES), 1)
    pick = (lane // LANES == at).astype(f32).astype(bf16)
    return mm(pick, high, NT) + mm(pick, low, NT)


def decay_row(horizon, width, factor):
    return jnp.concatenate(
        [jnp.full((1, width), factor * decay_rate**step, f32) for step in range(horizon)], axis=1
    )


def first_lane(total, width):
    lane = lax.broadcasted_iota(jnp.int32, (1, width), 1)
    return jnp.where(lane == 0, total, 0.0)


def row(ref):
    return ref[...].reshape(1, ref.shape[-1])


class Sizes:
    def __init__(self, obs_next, actions, enc_w1, dyn_w1):
        self.horizon, self.obs, self.seqs = obs_next.shape
        self.act = actions.shape[1]
        self.hidden = enc_w1.shape[1]
        joined, self.mlp = dyn_w1.shape
        self.lat = joined - self.act
        self.one = joined
        self.deep = up(joined + 1, 16)
        self.obs_deep = up(self.obs + 1, 16)
        self.lat_deep = up(self.lat, 16)
        self.act_deep = up(self.act, 16)
        self.cols = self.horizon * self.seqs
        self.net_rows = self.mlp + self.deep
        self.at_w3 = self.net_rows
        self.at_enc = self.at_w3 + up(self.lat, 8)
        self.at_prio = self.at_enc + up(max(self.lat, self.obs_deep + 1), 16)

    def dyn_rows(self, total):
        self.prio_rows = up(-(-total // self.mlp), 8)
        return up(self.at_prio + self.prio_rows, 64)


def places():
    dp = lax.axis_index("dp")
    pb = lax.axis_index("pb")
    core = lax.rem(dp, 2)
    side = lax.rem(lax.div(dp, 2), 2)
    return dp, pb, core, side


def square(relative):
    dp, pb, core, side = places()
    return lax.rem(side + relative // 2, 2) * 2 + lax.rem(pb + relative % 2, 2)


def pack_kernel(w1, b1, gain, shift, w2, b2, w3, b3, out):
    mlp = w2.shape[1]
    joined = w1.shape[1]
    half = out.shape[0]
    core = places()[2]

    @pl.when(core == 0)
    def _():
        out[...] = w2[0, :half]

    @pl.when(core == 1)
    def _():
        at = mlp - half
        out[:at] = w2[0, half:]
        out[at : at + joined] = w1[0]
        at = at + joined
        out[at:] = jnp.zeros((half - at, mlp), f32)
        for ref in (b1, gain, shift, b2, w3):
            out[at : at + 1] = ref[...]
            at = at + 1
        out[at : at + 1] = jnp.full((1, mlp), b3[0], f32)


def rollout_kernel(
    size,
    scale,
    obs_first,
    obs_next,
    actions,
    rewards,
    enc_w1,
    enc_b1,
    enc_w2,
    enc_b2,
    dyn_w1,
    dyn_b1,
    dyn_w2,
    dyn_b2,
    dyn_w3,
    dyn_b3,
    rew_w1,
    rew_b1,
    rew_w2,
    rew_b2,
    rew_w3,
    rew_b3,
    joint,
    keep0,
    keep1,
    keep2,
    keep3,
    send0,
    send1,
    send2,
    send3,
    state_grad,
    consist,
    dyn_h1,
    dyn_h2,
    enc_h,
    obs_aug,
    w_aug,
    w_out,
    e_aug,
    e_out,
    reward_grads,
    dyn_square,
    rew_square,
    sems,
):
    lat, act, one, deep = size.lat, size.act, size.one, size.deep
    mlp, seqs, cols, horizon = size.mlp, size.seqs, size.cols, size.horizon
    joined = lat + act
    dp, pb, core, side = places()
    fetch = [
        pltpu.make_async_copy(dyn_w2, dyn_square, sems.at[0]),
        pltpu.make_async_copy(rew_w2, rew_square, sems.at[1]),
    ]
    for copy in fetch:
        copy.start()

    def first_weight(ref, bias, kept):
        w_aug[...] = jnp.zeros_like(w_aug)
        w_aug[:kept] = ref[...]
        w_aug[one : one + 1] = row(bias)
        return split(w_aug[...])

    obs_aug[...] = jnp.zeros_like(obs_aug)
    for step in range(horizon):
        obs_aug[: size.obs, step * seqs : (step + 1) * seqs] = obs_next[step]
    obs_aug[: size.obs, cols:] = obs_first[...]
    obs_aug[size.obs : size.obs + 1] = jnp.ones((1, cols + seqs), f32)
    e_aug[...] = jnp.zeros_like(e_aug)
    e_aug[: size.obs] = enc_w1[...]
    e_aug[size.obs : size.obs + 1] = row(enc_b1)
    e_out[...] = jnp.zeros_like(e_out)
    e_out[:lat] = enc_w2[...]
    w_out[...] = jnp.zeros_like(w_out)
    w_out[:lat] = dyn_w3[...]
    small = jnp.concatenate(
        [
            jnp.concatenate([row(enc_b2), jnp.zeros((1, LANES - lat), f32)], axis=1),
            jnp.concatenate([row(dyn_b3), jnp.zeros((1, LANES - lat), f32)], axis=1),
        ],
        axis=0,
    )
    small = columns_of([small[0:1], small[1:2]])
    enc_b2_col = small[: size.lat_deep, :LANES]
    dyn_b3_col = small[: size.lat_deep, LANES:]
    wide = columns_of([row(dyn_b2), row(rew_b2), row(rew_w3)])
    dyn_b2_col = wide[:, :LANES]

    enc_first = mm(stack_weight(split(e_aug[...])), stack_input(split(obs_aug[...])), TN)
    enc_hidden = elu(enc_first)
    enc_h[...] = enc_hidden[:, cols:]
    latent = dot3_short(split(e_out[...]), split(enc_hidden), NN) + spread_lanes(
        enc_b2_col, cols + seqs
    )
    joint[:, :] = jnp.zeros_like(joint)
    joint[: size.lat_deep, :cols] = latent[:, :cols]
    for step in range(horizon):
        at = cols + step * seqs
        joint[lat : lat + act, at : at + seqs] = actions[step]
    joint[one : one + 1] = jnp.ones((1, 3 * cols), f32)

    first = stack_weight(first_weight(dyn_w1, dyn_b1, joined))
    fetch[0].wait()
    second = split(dyn_square[...].T)
    third = split(w_out[...])
    latent = latent[:, cols:]
    for step in range(horizon):
        here = slice(step * seqs, (step + 1) * seqs)
        there = slice(cols + step * seqs, cols + (step + 1) * seqs)
        joint[:lat, there] = latent[:lat]
        hidden = elu(mm(first, stack_input(split(joint[:, there])), TN))
        dyn_h1[:, here] = hidden
        hidden = elu(dot3_narrow(second, split(hidden), NN) + dyn_b2_col)
        dyn_h2[:, here] = hidden
        latent = dot3_narrow(third, split(hidden), NN) + dyn_b3_col
        goal = joint[: size.lat_deep, here]
        factor = scale * decay_rate**step * consist_coef * 2.0 / lat
        consist[:, here] = factor * (latent - goal)

    states = split(joint[:, cols : 2 * cols])
    first = first_weight(rew_w1, rew_b1, joined)
    fetch[1].wait()
    second = split(rew_square[...])
    b2_col = spread_lanes(wide[:, LANES : 2 * LANES], cols)
    w3_col = spread_lanes(wide[:, 2 * LANES : 3 * LANES], cols)
    h1 = elu(mm(stack_weight(first), stack_input(states), TN))
    h1_parts = split(h1)
    h2 = elu(mm(stack_weight(second), stack_input(h1_parts), TN) + b2_col)
    predicted = jnp.sum(w3_col * h2, axis=0, keepdims=True) + rew_b3[0]
    wanted = jnp.concatenate([rewards[step : step + 1] for step in range(horizon)], axis=1)
    out_grad = decay_row(horizon, seqs, scale * reward_coef * 2.0) * (predicted - wanted)
    h2_grad = w3_col * out_grad * elu_slope(h2)
    h2_parts = split(h2_grad)
    reward_grads[:mlp] = dot3(h1_parts, h2_parts, NT)
    h1_grad = dot3(second, h2_parts, NN) * elu_slope(h1)
    h1_grad = split(h1_grad)
    reward_grads[mlp:] = dot3(states, h1_grad, NT)
    state_grad[...] = dot3_short(first, h1_grad, NN)
    sums = rows_of([fold(h2_grad), fold(h2 * out_grad)])
    reward_grads[mlp + one + 1 : mlp + one + 3] = sums[:2]
    reward_grads[mlp + one + 3 : mlp + one + 4] = first_lane(jnp.sum(out_grad), mlp)

    eighth = size.net_rows // 8
    for h in range(2):
        place = core if h == 0 else 1 - core
        for k in range(4):
            out = ((keep0, keep1, keep2, keep3), (send0, send1, send2, send3))[h][k]
            start = (place * 4 + square(k)) * eighth
            out[...] = reward_grads[pl.ds(pl.multiple_of(start, 8), eighth)]


def act_kernel(
    size,
    begun,
    pol_w1,
    pol_b1,
    pol_w2,
    pol_b2,
    pol_w3,
    pol_b3,
    joint,
    pol_h1,
    pol_h2,
    w_aug,
    w_act,
):
    lat, act, one = size.lat, size.act, size.one
    cols = size.cols
    joined = lat + act
    joint[...] = begun[...]
    w_act[...] = jnp.zeros_like(w_act)
    w_act[:act] = pol_w3[...]
    small = jnp.concatenate([row(pol_b3), jnp.zeros((1, LANES - act), f32)], axis=1)
    pol_b3_col = columns_of([small])[: size.act_deep]
    b2_col = spread_lanes(columns_of([row(pol_b2)]), 2 * cols)
    w_aug[...] = jnp.zeros_like(w_aug)
    w_aug[:lat] = pol_w1[...]
    w_aug[one : one + 1] = row(pol_b1)
    first = stack_weight(split(w_aug[...]))
    second = split(pol_w2[...])
    third = split(w_act[...])
    both = slice(0, 2 * cols)
    h1 = elu(mm(first, stack_input(split(joint[:, both])), TN))
    h2 = elu(mm(stack_weight(second), stack_input(split(h1)), TN) + b2_col)
    action = dot3_short(third, split(h2), NN) + spread_lanes(pol_b3_col, 2 * cols)
    action = jnp.tanh(action)[:act]
    pol_h1[...] = h1[:, cols:]
    pol_h2[...] = h2[:, cols:]
    joint[lat:joined, :cols] = action[:, :cols]
    joint[:lat, 2 * cols :] = joint[:lat, cols : 2 * cols]
    joint[lat:joined, 2 * cols :] = action[:, cols:]


def value_kernel(
    size,
    scale,
    joint,
    rewards,
    q_w1,
    q_b1,
    q_gain,
    q_shift,
    q_w2,
    q_b2,
    q_w3,
    q_b3,
    packed_y,
    packed_c,
    keep0,
    keep1,
    keep2,
    keep3,
    send0,
    send1,
    send2,
    send3,
    state_grad,
    chosen_grad,
    prio,
    packed,
    aug,
    w1_rows,
    w1_parts,
    w2_rows,
    w2_lanes,
    vectors,
    last,
    inputs,
    next_value,
    spread,
    grads,
    work,
    normed,
    second,
    hidden,
    backs,
    sums,
):
    lat, act, one, deep = size.lat, size.act, size.one, size.deep
    mlp, seqs, cols, horizon = size.mlp, size.seqs, size.cols, size.horizon
    joined = lat + act
    dp, pb, core, side = places()
    half = packed_y.shape[0]
    packed[pl.ds(pl.multiple_of(core * half, 8), half)] = packed_y[...]
    packed[pl.ds(pl.multiple_of((1 - core) * half, 8), half)] = packed_c[...]

    at = mlp + joined
    for slot in range(TWIN):
        if slot == 0:
            w1, b1, w2 = q_w1[0], q_b1[...], q_w2[0]
            rows = [q_gain[...], q_shift[...], q_b2[...], q_w3[...]]
            b3 = jnp.full((1, LANES), q_b3[0], f32)
        else:
            w1, b1, w2 = packed[mlp:at], packed[at : at + 1], packed[:mlp]
            rows = [packed[at + i : at + i + 1] for i in (1, 2, 3, 4)]
            b3 = packed[at + 5 : at + 6, :LANES]
        aug[...] = jnp.zeros_like(aug)
        aug[:joined] = w1
        aug[one : one + 1] = b1
        high, low = split(aug[...])
        for place, part in enumerate((high, high, low)):
            w1_rows[slot, place * deep : (place + 1) * deep] = part
            if place > 0:
                w1_parts[slot, (place - 1) * deep : place * deep] = part
        high, low = split(w2)
        for place, part in enumerate((high, high, low)):
            w2_rows[slot, place * mlp : (place + 1) * mlp] = part
            w2_lanes[slot, :, place * mlp : (place + 1) * mlp] = part
        vectors[slot] = columns_of(rows)
        last[slot] = b3
    inputs[...] = stack_input(split(joint[...]))

    height = 32

    def blocks(width):
        for left in range(0, width, cols):
            for top in range(0, mlp, height):
                yield slice(top, top + height), slice(left, left + cols)

    def column(slot, which, rows):
        return spread_lanes(vectors[slot, rows, which * LANES : (which + 1) * LANES], cols)

    def keep_parts(ref, rows, here, value):
        high, low = split(value)
        for place, part in enumerate((high, low, high)):
            ref[rows.start + place * mlp : rows.stop + place * mlp, here] = part

    def added(totals, here, value):
        eight = value.reshape(height // 8, 8, cols).sum(axis=0)
        at = here.start // cols
        totals[at] = eight if totals[at] is None else totals[at] + eight

    def total_of(totals):
        return jnp.concatenate([jnp.sum(t, axis=0, keepdims=True) for t in totals], axis=1)

    def forward(slot, start, width, kept):
        work[:, :width] = mm(w1_rows[slot], inputs[:, start : start + width], TN)
        totals = [None] * (width // cols)
        for rows, here in blocks(width):
            added(totals, here, work[rows, here])
        mean = total_of(totals) / mlp
        totals = [None] * (width // cols)
        for rows, here in blocks(width):
            center = work[rows, here] - mean[:, here]
            added(totals, here, center * center)
        inverse = lax.rsqrt(total_of(totals) / mlp + norm_epsilon)
        for rows, here in blocks(width):
            value = (work[rows, here] - mean[:, here]) * inverse[:, here]
            if kept:
                normed[rows, here] = value
            value = jnp.tanh(column(slot, 0, rows) * value + column(slot, 1, rows))
            keep_parts(hidden, rows, here, value)
        work[:, :width] = mm(w2_rows[slot], hidden[:, :width], TN)
        totals = [None] * (width // cols)
        for rows, here in blocks(width):
            value = elu(work[rows, here] + column(slot, 2, rows))
            if kept:
                second[rows, here] = value
            if here.start == 0:
                added(totals, here, column(slot, 3, rows) * value)
        return total_of(totals[:1]) + spread_lanes(last[slot], cols), inverse

    for slot in range(TWIN):
        next_value[slot] = forward(slot, 0, cols, False)[0]

    wanted = jnp.concatenate([rewards[step : step + 1] for step in range(horizon)], axis=1)
    next_value[0] = wanted + discount * jnp.minimum(next_value[0], next_value[1])
    spread[...] = jnp.zeros_like(spread)
    state_grad[...] = jnp.zeros_like(state_grad)
    chosen_grad[...] = jnp.zeros_like(chosen_grad)

    for slot in range(TWIN):
        value, inverse = forward(slot, cols, 2 * cols, True)
        error = value - next_value[0]
        spread[...] += jnp.sqrt(error * error + 1.0)
        out_grad = jnp.concatenate(
            [
                decay_row(horizon, seqs, scale * value_coef * 2.0) * error,
                decay_row(horizon, seqs, -policy_coef * 0.5 * scale),
            ],
            axis=1,
        )
        for rows, here in blocks(2 * cols):
            result = second[rows, here]
            back = column(slot, 3, rows) * out_grad[:, here] * elu_slope(result)
            keep_parts(backs, rows, here, back)
            if here.start == 0:
                sums[rows, :LANES] = fold(back)
                sums[rows, 3 * LANES :] = fold(result * out_grad[:, here])
        work[...] = mm(w2_lanes[slot], backs[...], NN)
        grads[slot, :mlp] = dot3(
            (hidden[:mlp, :cols], hidden[mlp : 2 * mlp, :cols]),
            (backs[:mlp, :cols], backs[mlp : 2 * mlp, :cols]),
            NT,
        )
        plain, along = [None] * 2, [None] * 2
        for rows, here in blocks(2 * cols):
            high = hidden[rows, here].astype(f32)
            low = hidden[mlp + rows.start : mlp + rows.stop, here].astype(f32)
            result = high + low
            pre = work[rows, here] * (1.0 - result * result)
            unit = normed[rows, here]
            if here.start == 0:
                sums[rows, LANES : 2 * LANES] = fold(pre * unit)
                sums[rows, 2 * LANES : 3 * LANES] = fold(pre)
            back = column(slot, 0, rows) * pre
            work[rows, here] = back
            added(plain, here, back)
            added(along, here, back * unit)
        plain, along = total_of(plain) / mlp, total_of(along) / mlp
        for rows, here in blocks(2 * cols):
            back = work[rows, here] - plain[:, here] - normed[rows, here] * along[:, here]
            keep_parts(backs, rows, here, back * inverse[:, here])
        here = slice(cols, 2 * cols)
        states = (inputs[:deep, here], inputs[deep : 2 * deep, here])
        first_parts = (backs[:mlp, :cols], backs[mlp : 2 * mlp, :cols])
        grads[slot, mlp:] = dot3(states, first_parts, NT)
        both = mm(w1_parts[slot], backs[:mlp], NN)
        into = both[:deep] + both[deep:] + mm(w1_parts[slot, :deep], backs[mlp : 2 * mlp], NN)
        state_grad[...] += into[:, :cols]
        chosen_grad[...] += into[:, cols:]
        lines = rows_of([sums[:, at * LANES : (at + 1) * LANES] for at in range(4)])
        grads[slot, mlp + one + 1 : mlp + one + 5] = lines[:4]
        grads[slot, mlp + one + 5 : mlp + one + 6] = first_lane(jnp.sum(out_grad[:, :cols]), mlp)

    total = spread[:, :seqs]
    for step in range(1, horizon):
        total = total + spread[:, step * seqs : (step + 1) * seqs]
    prio[...] = total / (TWIN * horizon)

    quarter = size.net_rows // 4
    for h in range(2):
        place = core if h == 0 else 1 - core
        for k in range(4):
            out = ((keep0, keep1, keep2, keep3), (send0, send1, send2, send3))[h][k]
            start = (place * 2 + lax.div(square(k), 2)) * quarter
            out[...] = grads[k % 2, pl.ds(pl.multiple_of(start, 8), quarter)]


def policy_kernel(
    size, pol_w2, pol_w3, joint, pol_h1, pol_h2, chosen_grad, pol, w_act, act_grad
):
    lat, act, one = size.lat, size.act, size.one
    mlp, cols = size.mlp, size.cols
    joined = lat + act
    states = split(joint[:, cols : 2 * cols])
    w_act[...] = jnp.zeros_like(w_act)
    w_act[:act] = pol_w3[...]
    act_grad[...] = jnp.zeros_like(act_grad)
    chosen = joint[lat:joined, 2 * cols :]
    act_grad[:act] = chosen_grad[lat:joined] * (1.0 - chosen * chosen)
    out_parts = split(act_grad[...])
    weight = split(w_act[...])
    h2 = pol_h2[...]
    h2_grad = mm(stack_weight(weight), stack_input(out_parts), TN) * elu_slope(h2)
    h2_parts = split(h2_grad)
    h1 = pol_h1[...]
    pol[:mlp] = dot3(split(h1), h2_parts, NT)
    h1_grad = dot3(split(pol_w2[...]), h2_parts, NN) * elu_slope(h1)
    pol[mlp:] = dot3(states, split(h1_grad), NT)
    pol[mlp + lat : mlp + joined] = dot3(out_parts, split(h2), NT)[:act]
    pol[mlp + one + 1 : mlp + one + 2] = rows_of([fold(h2_grad)])[:1]
    sums = rows_of([fold(act_grad[...])])
    pol[mlp + one + 2 : mlp + one + 3] = jnp.zeros((1, mlp), f32)
    pol[mlp + one + 2 : mlp + one + 3, : size.act_deep] = sums[:1]


def shared_kernel(
    size,
    scale,
    total,
    obs_first,
    enc_w1,
    enc_w2,
    dyn_w1,
    dyn_w2,
    dyn_w3,
    joint,
    reward_state,
    consist,
    dyn_h1,
    dyn_h2,
    enc_h,
    value_state,
    prio,
    pol,
    keep0,
    keep1,
    keep2,
    keep3,
    send0,
    send1,
    send2,
    send3,
    obs_grad,
    obs_aug,
    w_out,
    e_out,
    lat_grad,
    second_high,
    second_low,
    first_high,
    first_low,
    dyn,
):
    lat, act, one, deep = size.lat, size.act, size.one, size.deep
    mlp, seqs, cols, horizon = size.mlp, size.seqs, size.cols, size.horizon
    joined = lat + act
    lat_deep, hidden = size.lat_deep, size.hidden
    dp, pb, core, side = places()
    states = split(joint[:, cols : 2 * cols])

    w_out[...] = jnp.zeros_like(w_out)
    w_out[:lat] = dyn_w3[...]
    third = stack_weight(split(w_out[...]))
    second = split(dyn_w2[...])
    first = split(dyn_w1[...])
    lat_rows = lax.broadcasted_iota(jnp.int32, (lat_deep, seqs), 0)
    carry = None
    for step in reversed(range(horizon)):
        here = slice(step * seqs, (step + 1) * seqs)
        grad = consist[:, here]
        if carry is not None:
            after = slice((step + 1) * seqs, (step + 2) * seqs)
            grad = grad + carry + reward_state[:lat_deep, after] + value_state[:lat_deep, after]
            grad = jnp.where(lat_rows < lat, grad, 0.0)
        lat_grad[:, here] = grad
        high, low = split(grad)
        h2_grad = mm(third, jnp.concatenate([high, low, high], axis=0), TN)
        h2_grad = h2_grad * elu_slope(dyn_h2[:, here])
        parts = split(h2_grad)
        second_high[:, here], second_low[:, here] = parts
        h1_grad = dot3_narrow(second, parts, NN) * elu_slope(dyn_h1[:, here])
        parts = split(h1_grad)
        first_high[:, here], first_low[:, here] = parts
        back = dot3_narrow(first, parts, NN)
        carry = jnp.concatenate([back, jnp.zeros((lat_deep - joined, seqs), f32)], axis=0)
    grad = carry + reward_state[:lat_deep, :seqs] + value_state[:lat_deep, :seqs]
    grad = jnp.where(lat_rows < lat, grad, 0.0)
    second_parts = (second_high[...], second_low[...])
    first_parts = (first_high[...], first_low[...])
    dyn[:mlp] = dot3(split(dyn_h1[...]), second_parts, NT)
    dyn[mlp : size.net_rows] = dot3(states, first_parts, NT)
    out_grad = lat_grad[...]
    b2_sum = fold(second_high[...].astype(f32) + second_low[...].astype(f32))
    dyn[size.at_w3 : size.at_enc] = dot3(split(out_grad), split(dyn_h2[...]), NT)[
        : size.at_enc - size.at_w3
    ]
    dyn[mlp + one + 1 : mlp + one + 2] = rows_of([b2_sum])[:1]
    dyn[mlp + one + 2 : mlp + one + 3] = jnp.zeros((1, mlp), f32)
    dyn[mlp + one + 2 : mlp + one + 3, :lat_deep] = rows_of([fold(out_grad)])[:1]

    dyn[size.at_enc :] = jnp.zeros((dyn.shape[0] - size.at_enc, mlp), f32)
    obs_aug[...] = jnp.zeros_like(obs_aug)
    obs_aug[: size.obs] = obs_first[...]
    obs_aug[size.obs : size.obs + 1] = jnp.ones((1, seqs), f32)
    e_out[...] = jnp.zeros_like(e_out)
    e_out[:lat] = enc_w2[...]
    parts = split(grad)
    h = enc_h[...]
    h_grad = dot3(split(e_out[...]), parts, TN) * elu_slope(h)
    h_parts = split(h_grad)
    dyn[size.at_enc : size.at_enc + lat_deep, :hidden] = dot3(parts, split(h), NT)
    dyn[size.at_enc : size.at_enc + size.obs_deep, hidden : 2 * hidden] = dot3(
        split(obs_aug[...]), h_parts, NT
    )
    at = size.at_enc + size.obs_deep
    dyn[at : at + 1, hidden : hidden + lat_deep] = rows_of([grad])[:1]
    obs_grad[...] = total * dot3(split(enc_w1[...]), h_parts, NN)

    index = (dp * 2 + pb) * seqs
    rows = size.prio_rows
    at = lax.broadcasted_iota(jnp.int32, (rows, mlp), 0) * mlp
    at = at + lax.broadcasted_iota(jnp.int32, (rows, mlp), 1)
    mine = (at >= index) & (at < index + seqs)
    value = jnp.concatenate([prio[...]] * (mlp // seqs), axis=1)
    dyn[size.at_prio : size.at_prio + rows] = jnp.where(mine, value, 0.0)

    small, large = size.net_rows // 8, dyn.shape[0] // 8
    for h in range(2):
        place = core if h == 0 else 1 - core
        for k in range(4):
            out = ((keep0, keep1, keep2, keep3), (send0, send1, send2, send3))[h][k]
            start = (place * 4 + square(k)) * small
            out[:small] = pol[pl.ds(pl.multiple_of(start, 8), small)]
            start = (place * 4 + square(k)) * large
            out[small:] = dyn[pl.ds(pl.multiple_of(start, 8), large)]


def halve_kernel(*refs):
    for k in range(4):
        refs[8 + k][...] = refs[k][...] + refs[4 + k][...]


def sum_kernel(*refs):
    total = refs[0][...]
    for ref in refs[1:-1]:
        total = total + ref[...]
    refs[-1][...] = total


def lane_half(other):
    mine = lax.rem(lax.div(lax.axis_index("dp"), 4), 2)
    at = 1 - mine if other else mine
    return pl.ds(pl.multiple_of(at * 256, 256), 256)


def cut_kernel(*refs):
    *summed, own, from_x, from_y, from_xy, mine, other, whole = refs
    at = 0
    for ref in summed:
        whole[at : at + ref.shape[0]] = ref[...]
        at = at + ref.shape[0]
    whole[at:] = (own[...] + from_x[...]) + (from_y[...] + from_xy[...])
    mine[...] = whole[:, lane_half(False)]
    other[...] = whole[:, lane_half(True)]


def rejoin_kernel(mine, other, *outs):
    for out in outs:
        out[:, lane_half(False)] = mine[: out.shape[0]]
        out[:, lane_half(True)] = other[: out.shape[0]]


def collect(out, pieces, first, rows, core, side, pb):
    for h in range(2):
        for k in range(4):
            place = lax.rem(core + h, 2) * 4 + lax.rem(side + k // 2, 2) * 2 + lax.rem(pb + k, 2)
            out[pl.ds(pl.multiple_of(place * rows, 8), rows)] = pieces[h][k][first : first + rows]


def finish_value_kernel(
    size,
    own,
    from_x,
    from_y,
    from_xy,
    c_own,
    c_x,
    c_y,
    c_xy,
    rew_w1,
    rew_b1,
    rew_w2,
    rew_b2,
    rew_w3,
    rew_b3,
    q_w1,
    q_b1,
    q_gain,
    q_shift,
    q_w2,
    q_b2,
    q_w3,
    q_b3,
    rew,
    twin,
):
    dp, pb, core, side = places()
    mlp, one = size.mlp, size.one
    eighth, quarter = size.net_rows // 8, size.net_rows // 4
    pieces = ((own, from_y, from_x, from_xy), (c_own, c_y, c_x, c_xy))
    collect(rew, pieces, 0, eighth, core, side, pb)
    for h in range(2):
        for k in range(2):
            place = lax.rem(core + h, 2) * 2 + lax.rem(side + k, 2)
            twin[pl.ds(pl.multiple_of(place * quarter, 8), quarter)] = pieces[h][2 * k][eighth:]
    rew_w2[...] = rew[:mlp]
    rew_w1[...] = rew[mlp : mlp + one]
    for ref, at in ((rew_b1, 0), (rew_b2, 1), (rew_w3, 2), (rew_b3, 3)):
        n = ref.shape[0]
        ref[...] = rew[mlp + one + at : mlp + one + at + 1, :n].reshape(n)
    q_w2[0] = twin[:mlp]
    q_w1[0] = twin[mlp : mlp + one]
    for at, ref in enumerate((q_b1, q_b2, q_gain, q_shift, q_w3)):
        ref[...] = twin[mlp + one + at : mlp + one + at + 1]
    q_b3[...] = twin[mlp + one + 5 : mlp + one + 6, :1].reshape(1)


def finish_shared_kernel(
    size,
    own,
    from_x,
    from_y,
    from_xy,
    c_own,
    c_x,
    c_y,
    c_xy,
    enc_w1,
    enc_b1,
    enc_w2,
    enc_b2,
    dyn_w1,
    dyn_b1,
    dyn_w2,
    dyn_b2,
    dyn_w3,
    dyn_b3,
    pol_w1,
    pol_b1,
    pol_w2,
    pol_b2,
    pol_w3,
    pol_b3,
    prio,
    pol,
    dyn,
):
    dp, pb, core, side = places()
    mlp, one, lat, act, hidden = size.mlp, size.one, size.lat, size.act, size.hidden
    pieces = ((own, from_y, from_x, from_xy), (c_own, c_y, c_x, c_xy))
    small, large = size.net_rows // 8, dyn.shape[0] // 8
    collect(pol, pieces, 0, small, core, side, pb)
    collect(dyn, pieces, small, large, core, side, pb)

    def line(out, source, at, first=0):
        n = out.shape[0]
        out[...] = source[at : at + 1, first : first + n].reshape(n)

    pol_w2[...] = pol[:mlp]
    pol_w1[...] = pol[mlp : mlp + lat]
    pol_w3[...] = pol[mlp + lat : mlp + lat + act]
    line(pol_b1, pol, mlp + one)
    line(pol_b2, pol, mlp + one + 1)
    line(pol_b3, pol, mlp + one + 2)
    dyn_w2[...] = dyn[:mlp]
    dyn_w1[...] = dyn[mlp : mlp + one]
    dyn_w3[...] = dyn[size.at_w3 : size.at_w3 + lat]
    line(dyn_b1, dyn, mlp + one)
    line(dyn_b2, dyn, mlp + one + 1)
    line(dyn_b3, dyn, mlp + one + 2)
    enc_w2[...] = dyn[size.at_enc : size.at_enc + lat, :hidden]
    enc_w1[...] = dyn[size.at_enc : size.at_enc + size.obs, hidden : 2 * hidden]
    line(enc_b1, dyn, size.at_enc + size.obs, hidden)
    line(enc_b2, dyn, size.at_enc + size.obs_deep, hidden)
    for at in range(prio.shape[0] // mlp):
        line(prio.at[at * mlp : (at + 1) * mlp], dyn, size.at_prio + at)


VMEM = pl.BlockSpec(memory_space=pltpu.VMEM)
SMEM = pl.BlockSpec(memory_space=pltpu.SMEM)


ANY = pl.BlockSpec(memory_space=pl.ANY)


def call(
    kernel, name, outs, args, scratch=(), scalars=(), left=(), after=(), mega=16
):
    def made(shape):
        return jax.ShapeDtypeStruct(shape, f32)

    def ordered(*refs):
        return kernel(*refs[: len(args)], *refs[len(args) + len(after) :])

    single = not isinstance(outs, list)
    shapes = [made(shape) for shape in ([outs] if single else outs)]
    specs = [SMEM if at in scalars else ANY if at in left else VMEM for at in range(len(args))]
    return pl.pallas_call(
        ordered,
        out_shape=shapes[0] if single else shapes,
        in_specs=specs + [ANY] * len(after),
        out_specs=VMEM if single else [VMEM] * len(shapes),
        scratch_shapes=list(scratch),
        compiler_params=pltpu.CompilerParams(vmem_limit_bytes=mega * 2**20),
        cost_estimate=pl.CostEstimate(flops=1, bytes_accessed=1, transcendentals=0),
        name=name,
    )(*args, *after)


def flipped(axis, bit):
    count = lax.axis_size(axis)
    return [(at, at ^ (1 << bit)) for at in range(count)]


def on_device(*args):
    a = dict(zip(NAMES, args))
    size = Sizes(a["obs_next"], a["actions"], a["enc_w1"], a["dyn_w1"])
    n_dp, n_pb = lax.axis_size("dp"), lax.axis_size("pb")
    total = size.seqs * n_dp * n_pb
    scale = 1.0 / total
    mlp, cols, seqs, deep = size.mlp, size.cols, size.seqs, size.deep
    dyn_rows = size.dyn_rows(total)
    net_rows = size.net_rows
    joined = size.lat + size.act

    def swap_core(block):
        return lax.ppermute(block, "dp", flipped("dp", 0))

    def swap_x(block):
        return lax.ppermute(block, "dp", flipped("dp", 1))

    def swap_y(block):
        return lax.ppermute(block, "pb", flipped("pb", 0))

    def swap_xy(block):
        route = []
        for dp in range(n_dp):
            for pb in range(n_pb):
                route.append((dp * n_pb + pb, (dp ^ 2) * n_pb + (pb ^ 1)))
        return lax.ppermute(block, ("dp", "pb"), route)

    def shape(rows, width, kind=f32):
        return pltpu.VMEM((rows, width), kind)

    def to_square(block):
        return [swap_x(block[0]), swap_y(block[1]), swap_xy(block[2])]

    def swap_z(block):
        return lax.ppermute(block, "dp", flipped("dp", 2))

    def swapped(parts):
        return parts[:4] + [swap_core(part) for part in parts[4:]]

    def halve(name, parts, after=()):
        own, to_y, to_x, to_xy = call(
            halve_kernel, name, [parts[0].shape] * 4, parts, after=after
        )
        return [own] + to_square((to_x, to_y, to_xy))

    def cut(name, parts, after=()):
        rows = sum(part.shape[0] for part in parts[:-3])
        mine, other = call(
            cut_kernel,
            name,
            [(rows, mlp // 2)] * 2,
            parts,
            scratch=[shape(rows, mlp)],
            after=after,
        )
        return [mine, swap_z(other)]

    def further_z(name, parts):
        for bit in range(3, n_dp.bit_length() - 1):
            whole = call(sum_kernel, name, parts[0].shape, parts)
            parts = [whole, lax.ppermute(whole, "dp", flipped("dp", bit))]
        return parts

    def back_z(name, parts, after=()):
        whole = call(sum_kernel, name, parts[0].shape, parts, after=after)
        return [whole, swap_z(whole)]

    def rejoin(name, parts, head, after=()):
        rows = parts[0].shape[0]
        outs = [(rows, mlp)] + ([(head, mlp)] if head < rows else [])
        outs = call(rejoin_kernel, name, outs, parts, after=after)
        return [outs[0]] + to_square([outs[0], outs[-1], outs[-1]])

    def both_cores(parts):
        return parts + [swap_core(part) for part in parts]

    q = [a[n] for n in NAMES[26:]]
    packed = call(
        pack_kernel,
        "pack",
        (net_rows // 2, mlp),
        q,
        scalars=(7,),
        mega=63,
    )
    packed_y = swap_y(packed)

    eighth = net_rows // 8
    begun, *reward, reward_state, consist, dyn_h1, dyn_h2, enc_h = call(
        functools.partial(rollout_kernel, size, scale),
        "rollout",
        [(deep, 3 * cols)]
        + [(eighth, mlp)] * 8
        + [(deep, cols), (size.lat_deep, cols), (mlp, cols), (mlp, cols), (size.hidden, seqs)],
        [a[n].T if n in TURNED else a[n] for n in NAMES[:20]],
        scratch=[
            shape(size.obs_deep, cols + seqs),
            shape(deep, mlp),
            shape(size.lat_deep, mlp),
            shape(size.obs_deep, size.hidden),
            shape(size.lat_deep, size.hidden),
            shape(net_rows, mlp),
            shape(mlp, mlp),
            shape(mlp, mlp),
            pltpu.SemaphoreType.DMA((2,)),
        ],
        scalars=(19,),
        left=(10, 16),
        mega=50,
    )
    reward = swapped(reward)
    joint, pol_h1, pol_h2 = call(
        functools.partial(act_kernel, size),
        "act",
        [(deep, 3 * cols), (mlp, cols), (mlp, cols)],
        [begun] + [a[n].T if n in TURNED else a[n] for n in NAMES[20:26]],
        scratch=[shape(deep, mlp), shape(size.act_deep, mlp)],
        mega=32,
    )
    reward = halve("reward_halve", reward, after=[pol_h1])
    packed_y, reward[0] = lax.optimization_barrier((packed_y, reward[0]))
    packed_c = swap_core(packed_y)

    rows = 2 * eighth
    *parts, value_state, chosen_grad, prio = call(
        functools.partial(value_kernel, size, scale),
        "value",
        [(rows, mlp)] * 8 + [(deep, cols), (deep, cols), (1, seqs)],
        [joint, a["rewards"]] + q + [packed_y, packed_c],
        scratch=[
            shape(net_rows, mlp),
            shape(deep, mlp),
            pltpu.VMEM((TWIN, 3 * deep, mlp), bf16),
            pltpu.VMEM((TWIN, 2 * deep, mlp), bf16),
            pltpu.VMEM((TWIN, 3 * mlp, mlp), bf16),
            pltpu.VMEM((TWIN, mlp, 3 * mlp), bf16),
            pltpu.VMEM((TWIN, mlp, 4 * LANES), f32),
            pltpu.VMEM((TWIN, 1, LANES), f32),
            shape(3 * deep, 3 * cols, bf16),
            pltpu.VMEM((TWIN, 1, cols), f32),
            shape(1, cols),
            pltpu.VMEM((TWIN, net_rows, mlp), f32),
            shape(mlp, 2 * cols),
            shape(mlp, 2 * cols),
            shape(mlp, 2 * cols),
            shape(3 * mlp, 2 * cols, bf16),
            shape(3 * mlp, 2 * cols, bf16),
            shape(mlp, 4 * LANES),
        ],
        scalars=(9,),
        after=[reward[0]],
        mega=40,
    )

    reward = call(sum_kernel, "reward_sum", reward[0].shape, reward, after=[prio])
    parts[4:], reward = lax.optimization_barrier((parts[4:], reward))
    parts = swapped(parts)
    value_rows, shared_rows = rows, eighth + dyn_rows // 8
    value = halve("value_halve", parts, after=[reward])
    pol = call(
        functools.partial(policy_kernel, size),
        "policy",
        (net_rows, mlp),
        [a["pol_w2"], a["pol_w3"].T, joint, pol_h1, pol_h2, chosen_grad],
        after=[value[0]],
        scratch=[shape(size.act_deep, mlp), shape(size.act_deep, cols)],
        mega=32,
    )

    *parts, obs_grad = call(
        functools.partial(shared_kernel, size, scale, total),
        "shared",
        [(shared_rows, mlp)] * 8 + [(size.obs, seqs)],
        [
            a["obs_first"],
            a["enc_w1"],
            a["enc_w2"].T,
            a["dyn_w1"],
            a["dyn_w2"],
            a["dyn_w3"].T,
            joint,
            reward_state,
            consist,
            dyn_h1,
            dyn_h2,
            enc_h,
            value_state,
            prio,
            pol,
        ],
        scratch=[
            shape(size.obs_deep, seqs),
            shape(size.lat_deep, mlp),
            shape(size.lat_deep, size.hidden),
            shape(size.lat_deep, cols),
            shape(mlp, cols, bf16),
            shape(mlp, cols, bf16),
            shape(mlp, cols, bf16),
            shape(mlp, cols, bf16),
            shape(dyn_rows, mlp),
        ],
        after=[value[0]],
        mega=32,
    )
    parts = swapped(parts)
    value = cut("value_cut", [reward] + value, after=[obs_grad])
    shared = halve("shared_halve", parts, after=[value[0]])
    value = further_z("value_further", value)
    shared = cut("shared_cut", shared)
    value = back_z("value_back", value, after=[shared[0]])
    shared = further_z("shared_further", shared)
    value = rejoin("value_rejoin", value, eighth, after=[shared[0]])
    shared = back_z("shared_back", shared)
    shared = rejoin("shared_rejoin", shared, shared_rows, after=[value[0]])
    value = both_cores(value)
    value_grads = call(
        functools.partial(finish_value_kernel, size),
        "finish_value",
        [a[n].shape for n in NAMES[14:20]] + [a[n].shape for n in NAMES[26:]],
        value,
        scratch=[shape(net_rows, mlp), shape(net_rows, mlp)],
        after=[shared[0]],
    )
    shared, value_grads = lax.optimization_barrier((shared, value_grads))
    shared = both_cores(shared)
    names = NAMES[4:14] + NAMES[20:26]
    shared_grads = call(
        functools.partial(finish_shared_kernel, size),
        "finish_shared",
        [a[n].shape[::-1] if n in TURNED else a[n].shape for n in names] + [(total,)],
        shared,
        scratch=[shape(net_rows, mlp), shape(dyn_rows, mlp)],
    )
    shared_grads = list(shared_grads)
    for at, n in enumerate(names):
        if n in TURNED:
            shared_grads[at] = shared_grads[at].T
    return (
        tuple(shared_grads[:10])
        + tuple(value_grads[:6])
        + tuple(shared_grads[10:16])
        + tuple(value_grads[6:])
        + (obs_grad, shared_grads[-1])
    )


def solution(mesh):
    whole = P()
    seqs = ("dp", "pb")
    twin = (P("pb", None, None),) + (P("pb", None),) * 3 + (P("pb", None, None),)
    twin = twin + (P("pb", None), P("pb", None), P("pb"))
    placed = (P(None, seqs), P(None, None, seqs), P(None, None, seqs), P(None, seqs))
    return jax.shard_map(
        on_device,
        mesh=mesh,
        in_specs=placed + (whole,) * 22 + twin,
        out_specs=(whole,) * 22 + twin + (P(None, seqs), whole),
        check_vma=False,
    )
```

```python
import functools

import jax
import jax.numpy as jnp
from jax import lax
from jax.experimental import pallas as pl
from jax.experimental.pallas import tpu as pltpu
from jax.sharding import PartitionSpec as P

f32 = jnp.float32
bf16 = jnp.bfloat16

TWIN = 2
LANES = 128
decay_rate = 0.5
discount = 0.99
consist_coef = 2.0
reward_coef = 0.5
value_coef = 0.1
policy_coef = 0.1
norm_epsilon = 1e-05

TURNED = ("enc_w2", "dyn_w3", "pol_w3")
NN = ((1,), (0,))
NT = ((1,), (1,))
TN = ((0,), (0,))

NAMES = (
    "obs_first",
    "obs_next",
    "actions",
    "rewards",
    "enc_w1",
    "enc_b1",
    "enc_w2",
    "enc_b2",
    "dyn_w1",
    "dyn_b1",
    "dyn_w2",
    "dyn_b2",
    "dyn_w3",
    "dyn_b3",
    "rew_w1",
    "rew_b1",
    "rew_w2",
    "rew_b2",
    "rew_w3",
    "rew_b3",
    "pol_w1",
    "pol_b1",
    "pol_w2",
    "pol_b2",
    "pol_w3",
    "pol_b3",
    "q_w1",
    "q_b1",
    "q_gain",
    "q_shift",
    "q_w2",
    "q_b2",
    "q_w3",
    "q_b3",
)


def up(number, multiple):
    return -(-number // multiple) * multiple


def mm(left, right, dims):
    return lax.dot_general(left, right, (dims, ((), ())), preferred_element_type=f32)


def split(value):
    high = value.astype(bf16)
    return high, (value - high.astype(f32)).astype(bf16)


def dot3(left, right, dims):
    return (
        mm(left[0], right[0], dims) + mm(left[0], right[1], dims) + mm(left[1], right[0], dims)
    )


def dot3_narrow(left, right, dims):
    width = right[0].shape[1]
    both = mm(left[0], jnp.concatenate(right, axis=1), dims)
    return both[:, :width] + both[:, width:] + mm(left[1], right[0], dims)


def dot3_short(left, right, dims):
    rows = left[0].shape[0]
    both = mm(jnp.concatenate(left, axis=0), right[0], dims)
    return both[:rows] + both[rows:] + mm(left[0], right[1], dims)


def stack_weight(parts):
    return jnp.concatenate([parts[0], parts[0], parts[1]], axis=0)


def stack_input(parts):
    return jnp.concatenate([parts[0], parts[1], parts[0]], axis=0)


def elu(value):
    return jnp.where(value > 0, value, jnp.exp(jnp.minimum(value, 0.0)) - 1.0)


def elu_slope(result):
    return jnp.where(result > 0, 1.0, result + 1.0)


def fold(value):
    total = value[:, :LANES]
    for at in range(LANES, value.shape[1], LANES):
        total = total + value[:, at : at + LANES]
    return total


def spread_lanes(column, width):
    return jnp.concatenate([column] * (width // LANES), axis=1)


def columns_of(rows):
    count = len(rows)
    deep = up(3 * count, 16)
    value = jnp.concatenate(rows, axis=0)
    first = value.astype(bf16)
    rest = value - first.astype(f32)
    second = rest.astype(bf16)
    third = (rest - second.astype(f32)).astype(bf16)
    parts = [first.astype(f32), second.astype(f32), third.astype(f32)]
    if deep > 3 * count:
        parts.append(jnp.zeros((deep - 3 * count, value.shape[1]), f32))
    stacked = jnp.concatenate(parts, axis=0).astype(bf16)
    at = lax.broadcasted_iota(jnp.int32, (deep, count * LANES), 0)
    lane = lax.broadcasted_iota(jnp.int32, (deep, count * LANES), 1)
    block = lane // LANES
    pick = ((at == block) | (at == block + count) | (at == block + 2 * count)) & (at < 3 * count)
    return mm(stacked, pick.astype(f32).astype(bf16), TN)


def rows_of(blocks):
    count = len(blocks)
    high, low = split(jnp.concatenate(blocks, axis=1))
    at = lax.broadcasted_iota(jnp.int32, (16, count * LANES), 0)
    lane = lax.broadcasted_iota(jnp.int32, (16, count * LANES), 1)
    pick = (lane // LANES == at).astype(f32).astype(bf16)
    return mm(pick, high, NT) + mm(pick, low, NT)


def decay_row(horizon, width, factor):
    return jnp.concatenate(
        [jnp.full((1, width), factor * decay_rate**step, f32) for step in range(horizon)], axis=1
    )


def first_lane(total, width):
    lane = lax.broadcasted_iota(jnp.int32, (1, width), 1)
    return jnp.where(lane == 0, total, 0.0)


def row(ref):
    return ref[...].reshape(1, ref.shape[-1])


class Sizes:
    def __init__(self, obs_next, actions, enc_w1, dyn_w1):
        self.horizon, self.obs, self.seqs = obs_next.shape
        self.act = actions.shape[1]
        self.hidden = enc_w1.shape[1]
        joined, self.mlp = dyn_w1.shape
        self.lat = joined - self.act
        self.one = joined
        self.deep = up(joined + 1, 16)
        self.obs_deep = up(self.obs + 1, 16)
        self.lat_deep = up(self.lat, 16)
        self.act_deep = up(self.act, 16)
        self.cols = self.horizon * self.seqs
        self.net_rows = self.mlp + self.deep
        self.at_w3 = self.net_rows
        self.at_enc = self.at_w3 + up(self.lat, 8)
        self.at_prio = self.at_enc + up(max(self.lat, self.obs_deep + 1), 16)

    def dyn_rows(self, total):
        self.prio_rows = up(-(-total // self.mlp), 8)
        return up(self.at_prio + self.prio_rows, 64)


def places():
    dp = lax.axis_index("dp")
    pb = lax.axis_index("pb")
    core = lax.rem(dp, 2)
    side = lax.rem(lax.div(dp, 2), 2)
    return dp, pb, core, side


def square(relative):
    dp, pb, core, side = places()
    return lax.rem(side + relative // 2, 2) * 2 + lax.rem(pb + relative % 2, 2)


def pack_kernel(w1, b1, gain, shift, w2, b2, w3, b3, out):
    mlp = w2.shape[1]
    joined = w1.shape[1]
    half = out.shape[0]
    core = places()[2]

    @pl.when(core == 0)
    def _():
        out[...] = w2[0, :half]

    @pl.when(core == 1)
    def _():
        at = mlp - half
        out[:at] = w2[0, half:]
        out[at : at + joined] = w1[0]
        at = at + joined
        out[at:] = jnp.zeros((half - at, mlp), f32)
        for ref in (b1, gain, shift, b2, w3):
            out[at : at + 1] = ref[...]
            at = at + 1
        out[at : at + 1] = jnp.full((1, mlp), b3[0], f32)


def rollout_kernel(
    size,
    scale,
    obs_first,
    obs_next,
    actions,
    rewards,
    enc_w1,
    enc_b1,
    enc_w2,
    enc_b2,
    dyn_w1,
    dyn_b1,
    dyn_w2,
    dyn_b2,
    dyn_w3,
    dyn_b3,
    rew_w1,
    rew_b1,
    rew_w2,
    rew_b2,
    rew_w3,
    rew_b3,
    joint,
    keep0,
    keep1,
    keep2,
    keep3,
    send0,
    send1,
    send2,
    send3,
    state_grad,
    consist,
    dyn_h1,
    dyn_h2,
    enc_h,
    obs_aug,
    w_aug,
    w_out,
    e_aug,
    e_out,
    reward_grads,
    dyn_square,
    rew_square,
    sems,
):
    lat, act, one, deep = size.lat, size.act, size.one, size.deep
    mlp, seqs, cols, horizon = size.mlp, size.seqs, size.cols, size.horizon
    joined = lat + act
    dp, pb, core, side = places()
    fetch = [
        pltpu.make_async_copy(dyn_w2, dyn_square, sems.at[0]),
        pltpu.make_async_copy(rew_w2, rew_square, sems.at[1]),
    ]
    for copy in fetch:
        copy.start()

    def first_weight(ref, bias, kept):
        w_aug[...] = jnp.zeros_like(w_aug)
        w_aug[:kept] = ref[...]
        w_aug[one : one + 1] = row(bias)
        return split(w_aug[...])

    obs_aug[...] = jnp.zeros_like(obs_aug)
    for step in range(horizon):
        obs_aug[: size.obs, step * seqs : (step + 1) * seqs] = obs_next[step]
    obs_aug[: size.obs, cols:] = obs_first[...]
    obs_aug[size.obs : size.obs + 1] = jnp.ones((1, cols + seqs), f32)
    e_aug[...] = jnp.zeros_like(e_aug)
    e_aug[: size.obs] = enc_w1[...]
    e_aug[size.obs : size.obs + 1] = row(enc_b1)
    e_out[...] = jnp.zeros_like(e_out)
    e_out[:lat] = enc_w2[...]
    w_out[...] = jnp.zeros_like(w_out)
    w_out[:lat] = dyn_w3[...]
    small = jnp.concatenate(
        [
            jnp.concatenate([row(enc_b2), jnp.zeros((1, LANES - lat), f32)], axis=1),
            jnp.concatenate([row(dyn_b3), jnp.zeros((1, LANES - lat), f32)], axis=1),
        ],
        axis=0,
    )
    small = columns_of([small[0:1], small[1:2]])
    enc_b2_col = small[: size.lat_deep, :LANES]
    dyn_b3_col = small[: size.lat_deep, LANES:]
    wide = columns_of([row(dyn_b2), row(rew_b2), row(rew_w3)])
    dyn_b2_col = wide[:, :LANES]

    enc_first = mm(stack_weight(split(e_aug[...])), stack_input(split(obs_aug[...])), TN)
    enc_hidden = elu(enc_first)
    enc_h[...] = enc_hidden[:, cols:]
    latent = dot3_short(split(e_out[...]), split(enc_hidden), NN) + spread_lanes(
        enc_b2_col, cols + seqs
    )
    joint[:, :] = jnp.zeros_like(joint)
    joint[: size.lat_deep, :cols] = latent[:, :cols]
    for step in range(horizon):
        at = cols + step * seqs
        joint[lat : lat + act, at : at + seqs] = actions[step]
    joint[one : one + 1] = jnp.ones((1, 3 * cols), f32)

    first = stack_weight(first_weight(dyn_w1, dyn_b1, joined))
    fetch[0].wait()
    second = split(dyn_square[...].T)
    third = split(w_out[...])
    latent = latent[:, cols:]
    for step in range(horizon):
        here = slice(step * seqs, (step + 1) * seqs)
        there = slice(cols + step * seqs, cols + (step + 1) * seqs)
        joint[:lat, there] = latent[:lat]
        hidden = elu(mm(first, stack_input(split(joint[:, there])), TN))
        dyn_h1[:, here] = hidden
        hidden = elu(dot3_narrow(second, split(hidden), NN) + dyn_b2_col)
        dyn_h2[:, here] = hidden
        latent = dot3_narrow(third, split(hidden), NN) + dyn_b3_col
        goal = joint[: size.lat_deep, here]
        factor = scale * decay_rate**step * consist_coef * 2.0 / lat
        consist[:, here] = factor * (latent - goal)

    states = split(joint[:, cols : 2 * cols])
    first = first_weight(rew_w1, rew_b1, joined)
    fetch[1].wait()
    second = split(rew_square[...])
    b2_col = spread_lanes(wide[:, LANES : 2 * LANES], cols)
    w3_col = spread_lanes(wide[:, 2 * LANES : 3 * LANES], cols)
    h1 = elu(mm(stack_weight(first), stack_input(states), TN))
    h1_parts = split(h1)
    h2 = elu(mm(stack_weight(second), stack_input(h1_parts), TN) + b2_col)
    predicted = jnp.sum(w3_col * h2, axis=0, keepdims=True) + rew_b3[0]
    wanted = jnp.concatenate([rewards[step : step + 1] for step in range(horizon)], axis=1)
    out_grad = decay_row(horizon, seqs, scale * reward_coef * 2.0) * (predicted - wanted)
    h2_grad = w3_col * out_grad * elu_slope(h2)
    h2_parts = split(h2_grad)
    reward_grads[:mlp] = dot3(h1_parts, h2_parts, NT)
    h1_grad = dot3(second, h2_parts, NN) * elu_slope(h1)
    h1_grad = split(h1_grad)
    reward_grads[mlp:] = dot3(states, h1_grad, NT)
    state_grad[...] = dot3_short(first, h1_grad, NN)
    sums = rows_of([fold(h2_grad), fold(h2 * out_grad)])
    reward_grads[mlp + one + 1 : mlp + one + 3] = sums[:2]
    reward_grads[mlp + one + 3 : mlp + one + 4] = first_lane(jnp.sum(out_grad), mlp)

    eighth = size.net_rows // 8
    for h in range(2):
        place = core if h == 0 else 1 - core
        for k in range(4):
            out = ((keep0, keep1, keep2, keep3), (send0, send1, send2, send3))[h][k]
            start = (place * 4 + square(k)) * eighth
            out[...] = reward_grads[pl.ds(pl.multiple_of(start, 8), eighth)]


def act_kernel(
    size,
    begun,
    pol_w1,
    pol_b1,
    pol_w2,
    pol_b2,
    pol_w3,
    pol_b3,
    joint,
    pol_h1,
    pol_h2,
    w_aug,
    w_act,
):
    lat, act, one = size.lat, size.act, size.one
    cols = size.cols
    joined = lat + act
    joint[...] = begun[...]
    w_act[...] = jnp.zeros_like(w_act)
    w_act[:act] = pol_w3[...]
    small = jnp.concatenate([row(pol_b3), jnp.zeros((1, LANES - act), f32)], axis=1)
    pol_b3_col = columns_of([small])[: size.act_deep]
    b2_col = spread_lanes(columns_of([row(pol_b2)]), 2 * cols)
    w_aug[...] = jnp.zeros_like(w_aug)
    w_aug[:lat] = pol_w1[...]
    w_aug[one : one + 1] = row(pol_b1)
    first = stack_weight(split(w_aug[...]))
    second = split(pol_w2[...])
    third = split(w_act[...])
    both = slice(0, 2 * cols)
    h1 = elu(mm(first, stack_input(split(joint[:, both])), TN))
    h2 = elu(mm(stack_weight(second), stack_input(split(h1)), TN) + b2_col)
    action = dot3_short(third, split(h2), NN) + spread_lanes(pol_b3_col, 2 * cols)
    action = jnp.tanh(action)[:act]
    pol_h1[...] = h1[:, cols:]
    pol_h2[...] = h2[:, cols:]
    joint[lat:joined, :cols] = action[:, :cols]
    joint[:lat, 2 * cols :] = joint[:lat, cols : 2 * cols]
    joint[lat:joined, 2 * cols :] = action[:, cols:]


def value_kernel(
    size,
    scale,
    joint,
    rewards,
    q_w1,
    q_b1,
    q_gain,
    q_shift,
    q_w2,
    q_b2,
    q_w3,
    q_b3,
    packed_y,
    packed_c,
    keep0,
    keep1,
    keep2,
    keep3,
    send0,
    send1,
    send2,
    send3,
    state_grad,
    chosen_grad,
    prio,
    packed,
    aug,
    w1_rows,
    w1_parts,
    w2_rows,
    w2_lanes,
    vectors,
    last,
    inputs,
    next_value,
    spread,
    grads,
    work,
    normed,
    second,
    hidden,
    backs,
    sums,
):
    lat, act, one, deep = size.lat, size.act, size.one, size.deep
    mlp, seqs, cols, horizon = size.mlp, size.seqs, size.cols, size.horizon
    joined = lat + act
    dp, pb, core, side = places()
    half = packed_y.shape[0]
    packed[pl.ds(pl.multiple_of(core * half, 8), half)] = packed_y[...]
    packed[pl.ds(pl.multiple_of((1 - core) * half, 8), half)] = packed_c[...]

    at = mlp + joined
    for slot in range(TWIN):
        if slot == 0:
            w1, b1, w2 = q_w1[0], q_b1[...], q_w2[0]
            rows = [q_gain[...], q_shift[...], q_b2[...], q_w3[...]]
            b3 = jnp.full((1, LANES), q_b3[0], f32)
        else:
            w1, b1, w2 = packed[mlp:at], packed[at : at + 1], packed[:mlp]
            rows = [packed[at + i : at + i + 1] for i in (1, 2, 3, 4)]
            b3 = packed[at + 5 : at + 6, :LANES]
        aug[...] = jnp.zeros_like(aug)
        aug[:joined] = w1
        aug[one : one + 1] = b1
        high, low = split(aug[...])
        for place, part in enumerate((high, high, low)):
            w1_rows[slot, place * deep : (place + 1) * deep] = part
            if place > 0:
                w1_parts[slot, (place - 1) * deep : place * deep] = part
        high, low = split(w2)
        for place, part in enumerate((high, high, low)):
            w2_rows[slot, place * mlp : (place + 1) * mlp] = part
            w2_lanes[slot, :, place * mlp : (place + 1) * mlp] = part
        vectors[slot] = columns_of(rows)
        last[slot] = b3
    inputs[...] = stack_input(split(joint[...]))

    height = 32

    def blocks(width):
        for left in range(0, width, cols):
            for top in range(0, mlp, height):
                yield slice(top, top + height), slice(left, left + cols)

    def column(slot, which, rows):
        return spread_lanes(vectors[slot, rows, which * LANES : (which + 1) * LANES], cols)

    def keep_parts(ref, rows, here, value):
        high, low = split(value)
        for place, part in enumerate((high, low, high)):
            ref[rows.start + place * mlp : rows.stop + place * mlp, here] = part

    def added(totals, here, value):
        eight = value.reshape(height // 8, 8, cols).sum(axis=0)
        at = here.start // cols
        totals[at] = eight if totals[at] is None else totals[at] + eight

    def total_of(totals):
        return jnp.concatenate([jnp.sum(t, axis=0, keepdims=True) for t in totals], axis=1)

    def forward(slot, start, width, kept, shift=0):
        whole = slice(shift, shift + width)

        def moved(here):
            return slice(here.start + shift, here.stop + shift)

        work[:, whole] = mm(w1_rows[slot], inputs[:, start : start + width], TN)
        yield
        totals = [None] * (width // cols)
        for rows, here in blocks(width):
            added(totals, here, work[rows, moved(here)])
        mean = total_of(totals) / mlp
        totals = [None] * (width // cols)
        for rows, here in blocks(width):
            center = work[rows, moved(here)] - mean[:, here]
            added(totals, here, center * center)
        inverse = lax.rsqrt(total_of(totals) / mlp + norm_epsilon)
        for rows, here in blocks(width):
            value = (work[rows, moved(here)] - mean[:, here]) * inverse[:, here]
            if kept:
                normed[rows, here] = value
            value = jnp.tanh(column(slot, 0, rows) * value + column(slot, 1, rows))
            keep_parts(hidden, rows, moved(here), value)
        yield
        work[:, whole] = mm(w2_rows[slot], hidden[:, whole], TN)
        yield
        totals = [None] * (width // cols)
        for rows, here in blocks(width):
            value = elu(work[rows, moved(here)] + column(slot, 2, rows))
            if kept:
                second[rows, here] = value
            if here.start == 0:
                added(totals, here, column(slot, 3, rows) * value)
        return total_of(totals[:1]) + spread_lanes(last[slot], cols), inverse

    def together(runs):
        results = {}
        while len(results) < len(runs):
            for at, run in enumerate(runs):
                if at not in results:
                    try:
                        next(run)
                    except StopIteration as end:
                        results[at] = end.value
        return [results[at] for at in range(len(runs))]

    runs = [forward(slot, 0, cols, False, slot * cols) for slot in range(TWIN)]
    for slot, result in enumerate(together(runs)):
        next_value[slot] = result[0]

    wanted = jnp.concatenate([rewards[step : step + 1] for step in range(horizon)], axis=1)
    next_value[0] = wanted + discount * jnp.minimum(next_value[0], next_value[1])
    spread[...] = jnp.zeros_like(spread)
    state_grad[...] = jnp.zeros_like(state_grad)
    chosen_grad[...] = jnp.zeros_like(chosen_grad)

    for slot in range(TWIN):
        value, inverse = together([forward(slot, cols, 2 * cols, True)])[0]
        error = value - next_value[0]
        spread[...] += jnp.sqrt(error * error + 1.0)
        out_grad = jnp.concatenate(
            [
                decay_row(horizon, seqs, scale * value_coef * 2.0) * error,
                decay_row(horizon, seqs, -policy_coef * 0.5 * scale),
            ],
            axis=1,
        )
        for rows, here in blocks(2 * cols):
            result = second[rows, here]
            back = column(slot, 3, rows) * out_grad[:, here] * elu_slope(result)
            keep_parts(backs, rows, here, back)
            if here.start == 0:
                sums[rows, :LANES] = fold(back)
                sums[rows, 3 * LANES :] = fold(result * out_grad[:, here])
        work[...] = mm(w2_lanes[slot], backs[...], NN)
        grads[slot, :mlp] = dot3(
            (hidden[:mlp, :cols], hidden[mlp : 2 * mlp, :cols]),
            (backs[:mlp, :cols], backs[mlp : 2 * mlp, :cols]),
            NT,
        )
        plain, along = [None] * 2, [None] * 2
        for rows, here in blocks(2 * cols):
            high = hidden[rows, here].astype(f32)
            low = hidden[mlp + rows.start : mlp + rows.stop, here].astype(f32)
            result = high + low
            pre = work[rows, here] * (1.0 - result * result)
            unit = normed[rows, here]
            if here.start == 0:
                sums[rows, LANES : 2 * LANES] = fold(pre * unit)
                sums[rows, 2 * LANES : 3 * LANES] = fold(pre)
            back = column(slot, 0, rows) * pre
            work[rows, here] = back
            added(plain, here, back)
            added(along, here, back * unit)
        plain, along = total_of(plain) / mlp, total_of(along) / mlp
        for rows, here in blocks(2 * cols):
            back = work[rows, here] - plain[:, here] - normed[rows, here] * along[:, here]
            keep_parts(backs, rows, here, back * inverse[:, here])
        here = slice(cols, 2 * cols)
        states = (inputs[:deep, here], inputs[deep : 2 * deep, here])
        first_parts = (backs[:mlp, :cols], backs[mlp : 2 * mlp, :cols])
        grads[slot, mlp:] = dot3(states, first_parts, NT)
        both = mm(w1_parts[slot], backs[:mlp], NN)
        into = both[:deep] + both[deep:] + mm(w1_parts[slot, :deep], backs[mlp : 2 * mlp], NN)
        state_grad[...] += into[:, :cols]
        chosen_grad[...] += into[:, cols:]
        lines = rows_of([sums[:, at * LANES : (at + 1) * LANES] for at in range(4)])
        grads[slot, mlp + one + 1 : mlp + one + 5] = lines[:4]
        grads[slot, mlp + one + 5 : mlp + one + 6] = first_lane(jnp.sum(out_grad[:, :cols]), mlp)

    total = spread[:, :seqs]
    for step in range(1, horizon):
        total = total + spread[:, step * seqs : (step + 1) * seqs]
    prio[...] = total / (TWIN * horizon)

    quarter = size.net_rows // 4
    for h in range(2):
        place = core if h == 0 else 1 - core
        for k in range(4):
            out = ((keep0, keep1, keep2, keep3), (send0, send1, send2, send3))[h][k]
            start = (place * 2 + lax.div(square(k), 2)) * quarter
            out[...] = grads[k % 2, pl.ds(pl.multiple_of(start, 8), quarter)]


def policy_kernel(
    size, pol_w2, pol_w3, joint, pol_h1, pol_h2, chosen_grad, pol, w_act, act_grad
):
    lat, act, one = size.lat, size.act, size.one
    mlp, cols = size.mlp, size.cols
    joined = lat + act
    states = split(joint[:, cols : 2 * cols])
    w_act[...] = jnp.zeros_like(w_act)
    w_act[:act] = pol_w3[...]
    act_grad[...] = jnp.zeros_like(act_grad)
    chosen = joint[lat:joined, 2 * cols :]
    act_grad[:act] = chosen_grad[lat:joined] * (1.0 - chosen * chosen)
    out_parts = split(act_grad[...])
    weight = split(w_act[...])
    h2 = pol_h2[...]
    h2_grad = mm(stack_weight(weight), stack_input(out_parts), TN) * elu_slope(h2)
    h2_parts = split(h2_grad)
    h1 = pol_h1[...]
    pol[:mlp] = dot3(split(h1), h2_parts, NT)
    h1_grad = dot3(split(pol_w2[...]), h2_parts, NN) * elu_slope(h1)
    pol[mlp:] = dot3(states, split(h1_grad), NT)
    pol[mlp + lat : mlp + joined] = dot3(out_parts, split(h2), NT)[:act]
    pol[mlp + one + 1 : mlp + one + 2] = rows_of([fold(h2_grad)])[:1]
    sums = rows_of([fold(act_grad[...])])
    pol[mlp + one + 2 : mlp + one + 3] = jnp.zeros((1, mlp), f32)
    pol[mlp + one + 2 : mlp + one + 3, : size.act_deep] = sums[:1]


def shared_kernel(
    size,
    scale,
    total,
    obs_first,
    enc_w1,
    enc_w2,
    dyn_w1,
    dyn_w2,
    dyn_w3,
    joint,
    reward_state,
    consist,
    dyn_h1,
    dyn_h2,
    enc_h,
    value_state,
    prio,
    pol,
    keep0,
    keep1,
    keep2,
    keep3,
    send0,
    send1,
    send2,
    send3,
    obs_grad,
    obs_aug,
    w_out,
    e_out,
    lat_grad,
    second_high,
    second_low,
    first_high,
    first_low,
    dyn,
):
    lat, act, one, deep = size.lat, size.act, size.one, size.deep
    mlp, seqs, cols, horizon = size.mlp, size.seqs, size.cols, size.horizon
    joined = lat + act
    lat_deep, hidden = size.lat_deep, size.hidden
    dp, pb, core, side = places()
    states = split(joint[:, cols : 2 * cols])

    w_out[...] = jnp.zeros_like(w_out)
    w_out[:lat] = dyn_w3[...]
    third = stack_weight(split(w_out[...]))
    second = split(dyn_w2[...])
    first = split(dyn_w1[...])
    lat_rows = lax.broadcasted_iota(jnp.int32, (lat_deep, seqs), 0)
    carry = None
    for step in reversed(range(horizon)):
        here = slice(step * seqs, (step + 1) * seqs)
        grad = consist[:, here]
        if carry is not None:
            after = slice((step + 1) * seqs, (step + 2) * seqs)
            grad = grad + carry + reward_state[:lat_deep, after] + value_state[:lat_deep, after]
            grad = jnp.where(lat_rows < lat, grad, 0.0)
        lat_grad[:, here] = grad
        high, low = split(grad)
        h2_grad = mm(third, jnp.concatenate([high, low, high], axis=0), TN)
        h2_grad = h2_grad * elu_slope(dyn_h2[:, here])
        parts = split(h2_grad)
        second_high[:, here], second_low[:, here] = parts
        h1_grad = dot3_narrow(second, parts, NN) * elu_slope(dyn_h1[:, here])
        parts = split(h1_grad)
        first_high[:, here], first_low[:, here] = parts
        back = dot3_narrow(first, parts, NN)
        carry = jnp.concatenate([back, jnp.zeros((lat_deep - joined, seqs), f32)], axis=0)
    grad = carry + reward_state[:lat_deep, :seqs] + value_state[:lat_deep, :seqs]
    grad = jnp.where(lat_rows < lat, grad, 0.0)
    second_parts = (second_high[...], second_low[...])
    first_parts = (first_high[...], first_low[...])
    dyn[:mlp] = dot3(split(dyn_h1[...]), second_parts, NT)
    dyn[mlp : size.net_rows] = dot3(states, first_parts, NT)
    out_grad = lat_grad[...]
    b2_sum = fold(second_high[...].astype(f32) + second_low[...].astype(f32))
    dyn[size.at_w3 : size.at_enc] = dot3(split(out_grad), split(dyn_h2[...]), NT)[
        : size.at_enc - size.at_w3
    ]
    dyn[mlp + one + 1 : mlp + one + 2] = rows_of([b2_sum])[:1]
    dyn[mlp + one + 2 : mlp + one + 3] = jnp.zeros((1, mlp), f32)
    dyn[mlp + one + 2 : mlp + one + 3, :lat_deep] = rows_of([fold(out_grad)])[:1]

    dyn[size.at_enc :] = jnp.zeros((dyn.shape[0] - size.at_enc, mlp), f32)
    obs_aug[...] = jnp.zeros_like(obs_aug)
    obs_aug[: size.obs] = obs_first[...]
    obs_aug[size.obs : size.obs + 1] = jnp.ones((1, seqs), f32)
    e_out[...] = jnp.zeros_like(e_out)
    e_out[:lat] = enc_w2[...]
    parts = split(grad)
    h = enc_h[...]
    h_grad = dot3(split(e_out[...]), parts, TN) * elu_slope(h)
    h_parts = split(h_grad)
    dyn[size.at_enc : size.at_enc + lat_deep, :hidden] = dot3(parts, split(h), NT)
    dyn[size.at_enc : size.at_enc + size.obs_deep, hidden : 2 * hidden] = dot3(
        split(obs_aug[...]), h_parts, NT
    )
    at = size.at_enc + size.obs_deep
    dyn[at : at + 1, hidden : hidden + lat_deep] = rows_of([grad])[:1]
    obs_grad[...] = total * dot3(split(enc_w1[...]), h_parts, NN)

    index = (dp * 2 + pb) * seqs
    rows = size.prio_rows
    at = lax.broadcasted_iota(jnp.int32, (rows, mlp), 0) * mlp
    at = at + lax.broadcasted_iota(jnp.int32, (rows, mlp), 1)
    mine = (at >= index) & (at < index + seqs)
    value = jnp.concatenate([prio[...]] * (mlp // seqs), axis=1)
    dyn[size.at_prio : size.at_prio + rows] = jnp.where(mine, value, 0.0)

    small, large = size.net_rows // 8, dyn.shape[0] // 8
    for h in range(2):
        place = core if h == 0 else 1 - core
        for k in range(4):
            out = ((keep0, keep1, keep2, keep3), (send0, send1, send2, send3))[h][k]
            start = (place * 4 + square(k)) * small
            out[:small] = pol[pl.ds(pl.multiple_of(start, 8), small)]
            start = (place * 4 + square(k)) * large
            out[small:] = dyn[pl.ds(pl.multiple_of(start, 8), large)]


def halve_kernel(*refs):
    for k in range(4):
        refs[8 + k][...] = refs[k][...] + refs[4 + k][...]


def sum_kernel(*refs):
    total = refs[0][...]
    for ref in refs[1:-1]:
        total = total + ref[...]
    refs[-1][...] = total


def lane_half(other):
    mine = lax.rem(lax.div(lax.axis_index("dp"), 4), 2)
    at = 1 - mine if other else mine
    return pl.ds(pl.multiple_of(at * 256, 256), 256)


def cut_kernel(*refs):
    *summed, own, from_x, from_y, from_xy, mine, other, whole = refs
    at = 0
    for ref in summed:
        whole[at : at + ref.shape[0]] = ref[...]
        at = at + ref.shape[0]
    whole[at:] = (own[...] + from_x[...]) + (from_y[...] + from_xy[...])
    mine[...] = whole[:, lane_half(False)]
    other[...] = whole[:, lane_half(True)]


def rejoin_kernel(mine, other, *outs):
    for out in outs:
        out[:, lane_half(False)] = mine[: out.shape[0]]
        out[:, lane_half(True)] = other[: out.shape[0]]


def collect(out, pieces, first, rows, core, side, pb):
    for h in range(2):
        for k in range(4):
            place = lax.rem(core + h, 2) * 4 + lax.rem(side + k // 2, 2) * 2 + lax.rem(pb + k, 2)
            out[pl.ds(pl.multiple_of(place * rows, 8), rows)] = pieces[h][k][first : first + rows]


def finish_value_kernel(
    size,
    own,
    from_x,
    from_y,
    from_xy,
    c_own,
    c_x,
    c_y,
    c_xy,
    rew_w1,
    rew_b1,
    rew_w2,
    rew_b2,
    rew_w3,
    rew_b3,
    q_w1,
    q_b1,
    q_gain,
    q_shift,
    q_w2,
    q_b2,
    q_w3,
    q_b3,
    rew,
    twin,
):
    dp, pb, core, side = places()
    mlp, one = size.mlp, size.one
    eighth, quarter = size.net_rows // 8, size.net_rows // 4
    pieces = ((own, from_y, from_x, from_xy), (c_own, c_y, c_x, c_xy))
    collect(rew, pieces, 0, eighth, core, side, pb)
    for h in range(2):
        for k in range(2):
            place = lax.rem(core + h, 2) * 2 + lax.rem(side + k, 2)
            twin[pl.ds(pl.multiple_of(place * quarter, 8), quarter)] = pieces[h][2 * k][eighth:]
    rew_w2[...] = rew[:mlp]
    rew_w1[...] = rew[mlp : mlp + one]
    for ref, at in ((rew_b1, 0), (rew_b2, 1), (rew_w3, 2), (rew_b3, 3)):
        n = ref.shape[0]
        ref[...] = rew[mlp + one + at : mlp + one + at + 1, :n].reshape(n)
    q_w2[0] = twin[:mlp]
    q_w1[0] = twin[mlp : mlp + one]
    for at, ref in enumerate((q_b1, q_b2, q_gain, q_shift, q_w3)):
        ref[...] = twin[mlp + one + at : mlp + one + at + 1]
    q_b3[...] = twin[mlp + one + 5 : mlp + one + 6, :1].reshape(1)


def finish_shared_kernel(
    size,
    own,
    from_x,
    from_y,
    from_xy,
    c_own,
    c_x,
    c_y,
    c_xy,
    enc_w1,
    enc_b1,
    enc_w2,
    enc_b2,
    dyn_w1,
    dyn_b1,
    dyn_w2,
    dyn_b2,
    dyn_w3,
    dyn_b3,
    pol_w1,
    pol_b1,
    pol_w2,
    pol_b2,
    pol_w3,
    pol_b3,
    prio,
    pol,
    dyn,
):
    dp, pb, core, side = places()
    mlp, one, lat, act, hidden = size.mlp, size.one, size.lat, size.act, size.hidden
    pieces = ((own, from_y, from_x, from_xy), (c_own, c_y, c_x, c_xy))
    small, large = size.net_rows // 8, dyn.shape[0] // 8
    collect(pol, pieces, 0, small, core, side, pb)
    collect(dyn, pieces, small, large, core, side, pb)

    def line(out, source, at, first=0):
        n = out.shape[0]
        out[...] = source[at : at + 1, first : first + n].reshape(n)

    pol_w2[...] = pol[:mlp]
    pol_w1[...] = pol[mlp : mlp + lat]
    pol_w3[...] = pol[mlp + lat : mlp + lat + act]
    line(pol_b1, pol, mlp + one)
    line(pol_b2, pol, mlp + one + 1)
    line(pol_b3, pol, mlp + one + 2)
    dyn_w2[...] = dyn[:mlp]
    dyn_w1[...] = dyn[mlp : mlp + one]
    dyn_w3[...] = dyn[size.at_w3 : size.at_w3 + lat]
    line(dyn_b1, dyn, mlp + one)
    line(dyn_b2, dyn, mlp + one + 1)
    line(dyn_b3, dyn, mlp + one + 2)
    enc_w2[...] = dyn[size.at_enc : size.at_enc + lat, :hidden]
    enc_w1[...] = dyn[size.at_enc : size.at_enc + size.obs, hidden : 2 * hidden]
    line(enc_b1, dyn, size.at_enc + size.obs, hidden)
    line(enc_b2, dyn, size.at_enc + size.obs_deep, hidden)
    for at in range(prio.shape[0] // mlp):
        line(prio.at[at * mlp : (at + 1) * mlp], dyn, size.at_prio + at)


VMEM = pl.BlockSpec(memory_space=pltpu.VMEM)
SMEM = pl.BlockSpec(memory_space=pltpu.SMEM)


ANY = pl.BlockSpec(memory_space=pl.ANY)


def call(
    kernel, name, outs, args, scratch=(), scalars=(), left=(), after=(), mega=16
):
    def made(shape):
        return jax.ShapeDtypeStruct(shape, f32)

    def ordered(*refs):
        return kernel(*refs[: len(args)], *refs[len(args) + len(after) :])

    single = not isinstance(outs, list)
    shapes = [made(shape) for shape in ([outs] if single else outs)]
    specs = [SMEM if at in scalars else ANY if at in left else VMEM for at in range(len(args))]
    return pl.pallas_call(
        ordered,
        out_shape=shapes[0] if single else shapes,
        in_specs=specs + [ANY] * len(after),
        out_specs=VMEM if single else [VMEM] * len(shapes),
        scratch_shapes=list(scratch),
        compiler_params=pltpu.CompilerParams(vmem_limit_bytes=mega * 2**20),
        cost_estimate=pl.CostEstimate(flops=1, bytes_accessed=1, transcendentals=0),
        name=name,
    )(*args, *after)


def flipped(axis, bit):
    count = lax.axis_size(axis)
    return [(at, at ^ (1 << bit)) for at in range(count)]


def on_device(*args):
    a = dict(zip(NAMES, args))
    size = Sizes(a["obs_next"], a["actions"], a["enc_w1"], a["dyn_w1"])
    n_dp, n_pb = lax.axis_size("dp"), lax.axis_size("pb")
    total = size.seqs * n_dp * n_pb
    scale = 1.0 / total
    mlp, cols, seqs, deep = size.mlp, size.cols, size.seqs, size.deep
    dyn_rows = size.dyn_rows(total)
    net_rows = size.net_rows
    joined = size.lat + size.act

    def swap_core(block):
        return lax.ppermute(block, "dp", flipped("dp", 0))

    def swap_x(block):
        return lax.ppermute(block, "dp", flipped("dp", 1))

    def swap_y(block):
        return lax.ppermute(block, "pb", flipped("pb", 0))

    def swap_xy(block):
        route = []
        for dp in range(n_dp):
            for pb in range(n_pb):
                route.append((dp * n_pb + pb, (dp ^ 2) * n_pb + (pb ^ 1)))
        return lax.ppermute(block, ("dp", "pb"), route)

    def shape(rows, width, kind=f32):
        return pltpu.VMEM((rows, width), kind)

    def to_square(block):
        return [swap_x(block[0]), swap_y(block[1]), swap_xy(block[2])]

    def swap_z(block):
        return lax.ppermute(block, "dp", flipped("dp", 2))

    def swapped(parts):
        return parts[:4] + [swap_core(part) for part in parts[4:]]

    def halve(name, parts, after=()):
        own, to_y, to_x, to_xy = call(
            halve_kernel, name, [parts[0].shape] * 4, parts, after=after
        )
        return [own] + to_square((to_x, to_y, to_xy))

    def cut(name, parts, after=()):
        rows = sum(part.shape[0] for part in parts[:-3])
        mine, other = call(
            cut_kernel,
            name,
            [(rows, mlp // 2)] * 2,
            parts,
            scratch=[shape(rows, mlp)],
            after=after,
        )
        return [mine, swap_z(other)]

    def further_z(name, parts):
        for bit in range(3, n_dp.bit_length() - 1):
            whole = call(sum_kernel, name, parts[0].shape, parts)
            parts = [whole, lax.ppermute(whole, "dp", flipped("dp", bit))]
        return parts

    def back_z(name, parts, after=()):
        whole = call(sum_kernel, name, parts[0].shape, parts, after=after)
        return [whole, swap_z(whole)]

    def rejoin(name, parts, head, after=()):
        rows = parts[0].shape[0]
        outs = [(rows, mlp)] + ([(head, mlp)] if head < rows else [])
        outs = call(rejoin_kernel, name, outs, parts, after=after)
        return [outs[0]] + to_square([outs[0], outs[-1], outs[-1]])

    def both_cores(parts):
        return parts + [swap_core(part) for part in parts]

    q = [a[n] for n in NAMES[26:]]
    packed = call(
        pack_kernel,
        "pack",
        (net_rows // 2, mlp),
        q,
        scalars=(7,),
        mega=63,
    )
    packed_y = swap_y(packed)

    eighth = net_rows // 8
    begun, *reward, reward_state, consist, dyn_h1, dyn_h2, enc_h = call(
        functools.partial(rollout_kernel, size, scale),
        "rollout",
        [(deep, 3 * cols)]
        + [(eighth, mlp)] * 8
        + [(deep, cols), (size.lat_deep, cols), (mlp, cols), (mlp, cols), (size.hidden, seqs)],
        [a[n].T if n in TURNED else a[n] for n in NAMES[:20]],
        scratch=[
            shape(size.obs_deep, cols + seqs),
            shape(deep, mlp),
            shape(size.lat_deep, mlp),
            shape(size.obs_deep, size.hidden),
            shape(size.lat_deep, size.hidden),
            shape(net_rows, mlp),
            shape(mlp, mlp),
            shape(mlp, mlp),
            pltpu.SemaphoreType.DMA((2,)),
        ],
        scalars=(19,),
        left=(10, 16),
        mega=50,
    )
    reward = swapped(reward)
    joint, pol_h1, pol_h2 = call(
        functools.partial(act_kernel, size),
        "act",
        [(deep, 3 * cols), (mlp, cols), (mlp, cols)],
        [begun] + [a[n].T if n in TURNED else a[n] for n in NAMES[20:26]],
        scratch=[shape(deep, mlp), shape(size.act_deep, mlp)],
        mega=32,
    )
    reward = halve("reward_halve", reward, after=[pol_h1])
    packed_y, reward[0] = lax.optimization_barrier((packed_y, reward[0]))
    packed_c = swap_core(packed_y)

    rows = 2 * eighth
    *parts, value_state, chosen_grad, prio = call(
        functools.partial(value_kernel, size, scale),
        "value",
        [(rows, mlp)] * 8 + [(deep, cols), (deep, cols), (1, seqs)],
        [joint, a["rewards"]] + q + [packed_y, packed_c],
        scratch=[
            shape(net_rows, mlp),
            shape(deep, mlp),
            pltpu.VMEM((TWIN, 3 * deep, mlp), bf16),
            pltpu.VMEM((TWIN, 2 * deep, mlp), bf16),
            pltpu.VMEM((TWIN, 3 * mlp, mlp), bf16),
            pltpu.VMEM((TWIN, mlp, 3 * mlp), bf16),
            pltpu.VMEM((TWIN, mlp, 4 * LANES), f32),
            pltpu.VMEM((TWIN, 1, LANES), f32),
            shape(3 * deep, 3 * cols, bf16),
            pltpu.VMEM((TWIN, 1, cols), f32),
            shape(1, cols),
            pltpu.VMEM((TWIN, net_rows, mlp), f32),
            shape(mlp, 2 * cols),
            shape(mlp, 2 * cols),
            shape(mlp, 2 * cols),
            shape(3 * mlp, 2 * cols, bf16),
            shape(3 * mlp, 2 * cols, bf16),
            shape(mlp, 4 * LANES),
        ],
        scalars=(9,),
        after=[reward[0]],
        mega=40,
    )

    reward = call(sum_kernel, "reward_sum", reward[0].shape, reward, after=[prio])
    parts[4:], reward = lax.optimization_barrier((parts[4:], reward))
    parts = swapped(parts)
    value_rows, shared_rows = rows, eighth + dyn_rows // 8
    value = halve("value_halve", parts, after=[reward])
    pol = call(
        functools.partial(policy_kernel, size),
        "policy",
        (net_rows, mlp),
        [a["pol_w2"], a["pol_w3"].T, joint, pol_h1, pol_h2, chosen_grad],
        after=[value[0]],
        scratch=[shape(size.act_deep, mlp), shape(size.act_deep, cols)],
        mega=32,
    )

    *parts, obs_grad = call(
        functools.partial(shared_kernel, size, scale, total),
        "shared",
        [(shared_rows, mlp)] * 8 + [(size.obs, seqs)],
        [
            a["obs_first"],
            a["enc_w1"],
            a["enc_w2"].T,
            a["dyn_w1"],
            a["dyn_w2"],
            a["dyn_w3"].T,
            joint,
            reward_state,
            consist,
            dyn_h1,
            dyn_h2,
            enc_h,
            value_state,
            prio,
            pol,
        ],
        scratch=[
            shape(size.obs_deep, seqs),
            shape(size.lat_deep, mlp),
            shape(size.lat_deep, size.hidden),
            shape(size.lat_deep, cols),
            shape(mlp, cols, bf16),
            shape(mlp, cols, bf16),
            shape(mlp, cols, bf16),
            shape(mlp, cols, bf16),
            shape(dyn_rows, mlp),
        ],
        after=[value[0]],
        mega=32,
    )
    parts = swapped(parts)
    value = cut("value_cut", [reward] + value, after=[obs_grad])
    shared = halve("shared_halve", parts, after=[value[0]])
    value = further_z("value_further", value)
    shared = cut("shared_cut", shared)
    value = back_z("value_back", value, after=[shared[0]])
    shared = further_z("shared_further", shared)
    value = rejoin("value_rejoin", value, eighth, after=[shared[0]])
    shared = back_z("shared_back", shared)
    shared = rejoin("shared_rejoin", shared, shared_rows, after=[value[0]])
    value = both_cores(value)
    value_grads = call(
        functools.partial(finish_value_kernel, size),
        "finish_value",
        [a[n].shape for n in NAMES[14:20]] + [a[n].shape for n in NAMES[26:]],
        value,
        scratch=[shape(net_rows, mlp), shape(net_rows, mlp)],
        after=[shared[0]],
    )
    shared, value_grads = lax.optimization_barrier((shared, value_grads))
    shared = both_cores(shared)
    names = NAMES[4:14] + NAMES[20:26]
    shared_grads = call(
        functools.partial(finish_shared_kernel, size),
        "finish_shared",
        [a[n].shape[::-1] if n in TURNED else a[n].shape for n in names] + [(total,)],
        shared,
        scratch=[shape(net_rows, mlp), shape(dyn_rows, mlp)],
    )
    shared_grads = list(shared_grads)
    for at, n in enumerate(names):
        if n in TURNED:
            shared_grads[at] = shared_grads[at].T
    return (
        tuple(shared_grads[:10])
        + tuple(value_grads[:6])
        + tuple(shared_grads[10:16])
        + tuple(value_grads[6:])
        + (obs_grad, shared_grads[-1])
    )


def solution(mesh):
    whole = P()
    seqs = ("dp", "pb")
    twin = (P("pb", None, None),) + (P("pb", None),) * 3 + (P("pb", None, None),)
    twin = twin + (P("pb", None), P("pb", None), P("pb"))
    placed = (P(None, seqs), P(None, None, seqs), P(None, None, seqs), P(None, seqs))
    return jax.shard_map(
        on_device,
        mesh=mesh,
        in_specs=placed + (whole,) * 22 + twin,
        out_specs=(whole,) * 22 + twin + (P(None, seqs), whole),
        check_vma=False,
    )
```
